512 devices in a mesh: seq: 64 (over y_hi, z, core), tensor: 8 (over x, y_lo).
Axes of the slice: x: 4, y: 8 (y_hi: 4, y_lo: 2; y = y_hi * 2 + y_lo), z: 8, core: 2. Of those that a mesh axis runs over, the one named last changes fastest.
Arguments:
- embedded: bfloat16 [16384, 4, 2048], P('seq', None, 'tensor'), may hold values from -6 to 6
- delays: int32 [4], replicated, may hold values from 0 to 3, each once
- norm_gain: float32 [2048], replicated, may hold values from 0.1 to 1.9
- w_query: bfloat16 [2048, 2048], P('seq', 'tensor'), may hold values from -0.125 to 0.125
- w_key: bfloat16 [2048, 2048], P('seq', 'tensor'), may hold values from -0.125 to 0.125
- w_value: bfloat16 [2048, 2048], P('seq', 'tensor'), may hold values from -0.125 to 0.125
- w_out: bfloat16 [2048, 2048], P('tensor', 'seq'), may hold values from -0.75 to 0.75
- text_states: bfloat16 [128, 768], P('seq'), may hold values from -6 to 6
- w_text_key: bfloat16 [768, 2048], P('seq', 'tensor'), may hold values from -0.21875 to 0.21875
- w_text_value: bfloat16 [768, 2048], P('seq', 'tensor'), may hold values from -0.21875 to 0.21875
- text_len: int32 [1], replicated, may hold values from 64 to 128
- cotangent: bfloat16 [16384, 2048], P('seq'), may hold values from -16 to 16
Outputs:
- attn_out: bfloat16 [16384, 2048], P('seq', 'tensor')
- d_embedded: bfloat16 [16384, 4, 2048], P('seq', None, 'tensor')
- d_wo: float32 [2048, 2048], P('tensor', 'seq')
- d_wtk: float32 [768, 2048], P('seq', 'tensor')
- d_wtv: float32 [768, 2048], P('seq', 'tensor')
The draws below stay inside these ranges and needn't reach their ends.
Inputs may be any that keep to these rules, and one draw needn't show every extreme that they name: `delays`: each of 0 to 3 appears once. Text tokens with index text_len[0] or more are padding.
All inputs are finite; a program needn't handle non-finite values.
Results may differ from the reference program's by a relative error of at most 0.023.
Values may be sent and summed in bfloat16 or wider, within the bound.
A program may use at most 128 MiB of HBM per device.

```python
import jax
import jax.numpy as jnp
from jax import lax

MODEL_WIDTH = 2048
HEADS = 32
HD = 64
CODEBOOKS = 4
TD = 768
FRAMES_PER_SHARD = 256
WINDOW = 1500
FRAMES = 16384
TEXT = 128
N_SEQ = 64
N_TENSOR = 8


def spiked(result, own_key, source, target, blocks, factor):
    def block_of(position):
        return (jnp.arange(result.shape[position]) // (result.shape[position] // blocks)).reshape((-1,) + (1,) * (result.ndim - 1 - position))

    first = jax.random.permutation(own_key, blocks)[block_of(target)]
    far = (block_of(target) + blocks // 2) % blocks
    return jnp.where((block_of(source) == first) | (block_of(source) == far), factor * result, result)


def shard_levels(rng, shape, split, smallest, largest):
    loudness = 1.0
    for axis_at, blocks in split:
        draws = jax.random.uniform(jax.random.fold_in(jax.random.fold_in(rng, 6), axis_at), (blocks,), jnp.float32, smallest / len(split), largest / len(split))
        loudness = loudness * jnp.repeat(jnp.exp(draws), shape[axis_at] // blocks).reshape((-1,) + (1,) * (len(shape) - 1 - axis_at))
    return loudness


def bell_draw(rng, shape, width, bound, split=(), kind=jnp.bfloat16):
    result = jax.random.normal(rng, shape, jnp.float32) * width
    if len(split) > 0:
        result = shard_levels(rng, shape, split, -0.22, 0.18) * result
    return jnp.clip(result, min=-bound, max=bound).astype(kind)


def heavy_noise(stream_key, extent, width, bound, pieces, heavy, held_as=jnp.bfloat16):
    drawn = width * jax.random.normal(stream_key, extent, jnp.float32)
    if pieces:
        drawn = drawn * shard_levels(stream_key, extent, pieces, -0.22, 0.18)
    return jnp.clip(spiked(drawn, jax.random.fold_in(stream_key, 3), *heavy), -bound, bound).astype(held_as)


def setup_inputs(seed: int = 0) -> dict:
    key_of = jax.random.split(jax.random.key(seed), 13)
    embedded = bell_draw(key_of[0], (FRAMES, CODEBOOKS, MODEL_WIDTH), 1.0, 6.0, ((0, 64), (2, 8)))
    delays = jax.random.permutation(key_of[1], CODEBOOKS).astype(jnp.int32)
    norm_gain = jnp.clip(1.0 + 0.18 * jax.random.normal(key_of[2], (MODEL_WIDTH,), jnp.float32), 0.1, 1.9)
    w_query = bell_draw(key_of[3], (MODEL_WIDTH, MODEL_WIDTH), MODEL_WIDTH ** -0.5, 0.125, ((0, 64), (1, 8)))
    w_key = bell_draw(key_of[4], (MODEL_WIDTH, MODEL_WIDTH), MODEL_WIDTH ** -0.5, 0.125, ((0, 64), (1, 8)))
    w_value = bell_draw(key_of[5], (MODEL_WIDTH, MODEL_WIDTH), MODEL_WIDTH ** -0.5, 0.125, ((0, 64), (1, 8)))
    w_out = bell_draw(key_of[6], (MODEL_WIDTH, MODEL_WIDTH), HD ** -0.5, 0.75, ((0, 8), (1, 64)))
    text_states = bell_draw(key_of[7], (TEXT, TD), 1.0, 6.0, ((0, 64),))
    w_text_key = bell_draw(key_of[8], (TD, MODEL_WIDTH), TD ** -0.5, 0.21875, ((0, 64), (1, 8)))
    w_text_value = bell_draw(key_of[9], (TD, MODEL_WIDTH), TD ** -0.5, 0.21875, ((0, 64), (1, 8)))
    text_len = jax.random.randint(key_of[10], (1,), TEXT // 2, TEXT + 1).astype(jnp.int32)
    cotangent = heavy_noise(key_of[11], (FRAMES, MODEL_WIDTH), 1.0, 16.0, ((0, 64),), (0, 1, 64, 4.0))
    return {"embedded": embedded, "delays": delays, "norm_gain": norm_gain, "w_query": w_query, "w_key": w_key, "w_value": w_value, "w_out": w_out, "text_states": text_states, "w_text_key": w_text_key, "w_text_value": w_text_value, "text_len": text_len, "cotangent": cotangent}


EPS = 1e-05

def rounded(array):
    return lax.optimization_barrier(array.astype(jnp.bfloat16)).astype(jnp.float32)

def norm_forward(frames_in):
    widened = frames_in.astype(jnp.float32)
    row_mean = lax.optimization_barrier(jnp.mean(widened, -1, keepdims=True))
    centred = widened - row_mean
    inv_std = lax.rsqrt(lax.optimization_barrier(jnp.mean(centred * centred, -1, keepdims=True)) + EPS)
    return (centred * inv_std, inv_std)

def split_heads(rows):
    return rows.astype(jnp.float32).reshape(rows.shape[0], HEADS, HD)

def reference(embedded, delays, norm_gain, w_query, w_key, w_value, w_out, text_states, w_text_key, w_text_value, text_len, cotangent):
    padded = jnp.concatenate([jnp.zeros((CODEBOOKS - 1, CODEBOOKS, MODEL_WIDTH), jnp.bfloat16), embedded], 0)
    summed = jnp.zeros((FRAMES, MODEL_WIDTH), jnp.float32)
    for codebook in range(CODEBOOKS):
        offset = (CODEBOOKS - 1 - delays[codebook]).astype(jnp.int32)
        summed = summed + lax.dynamic_slice_in_dim(padded[:, codebook], offset, FRAMES, 0).astype(jnp.float32)
    frames_in = summed.astype(jnp.bfloat16)
    unit_rows, inv_std = norm_forward(frames_in)
    normed = (unit_rows * norm_gain).astype(jnp.bfloat16)
    queries = jnp.dot(normed, w_query, preferred_element_type=jnp.float32).astype(jnp.bfloat16)
    keys_all = jnp.dot(normed, w_key, preferred_element_type=jnp.float32).astype(jnp.bfloat16)
    values_all = jnp.dot(normed, w_value, preferred_element_type=jnp.float32).astype(jnp.bfloat16)
    text_keys = jnp.dot(text_states, w_text_key, preferred_element_type=jnp.float32).astype(jnp.bfloat16)
    text_values = jnp.dot(text_states, w_text_value, preferred_element_type=jnp.float32).astype(jnp.bfloat16)
    out_grad = lax.dot_general(cotangent, w_out, (((1,), (1,)), ((), ())), preferred_element_type=jnp.float32).astype(jnp.bfloat16)
    block_reach = (WINDOW + FRAMES_PER_SHARD - 2) // FRAMES_PER_SHARD
    key_lead = block_reach * FRAMES_PER_SHARD
    key_extent = key_lead + FRAMES_PER_SHARD
    key_padded = jnp.concatenate([jnp.zeros((key_lead, MODEL_WIDTH), jnp.bfloat16), keys_all], 0)
    value_padded = jnp.concatenate([jnp.zeros((key_lead, MODEL_WIDTH), jnp.bfloat16), values_all], 0)
    score_scale = HD ** (-0.5)
    row_ids = jnp.arange(FRAMES_PER_SHARD, dtype=jnp.int32)[:, None]
    col_ids = jnp.arange(key_extent, dtype=jnp.int32)[None, :]
    distance = row_ids + key_lead - col_ids
    near_mask = (distance >= 0) & (distance < WINDOW)
    text_mask = jnp.arange(TEXT, dtype=jnp.int32)[None, :] < text_len[0]
    text_k4 = split_heads(text_keys)
    text_v4 = split_heads(text_values)

    def shard_step(running_totals, shard_index):
        padded_key_gradient, padded_value_gradient, text_keys_gradient, text_values_gradient = running_totals
        leading_row = shard_index * FRAMES_PER_SHARD
        key_mask = near_mask & (leading_row - key_lead + col_ids >= 0)
        q_four = split_heads(lax.dynamic_slice_in_dim(queries, leading_row, FRAMES_PER_SHARD, 0))
        k_four = split_heads(lax.dynamic_slice_in_dim(key_padded, leading_row, key_extent, 0))
        v_four = split_heads(lax.dynamic_slice_in_dim(value_padded, leading_row, key_extent, 0))
        d_four = split_heads(lax.dynamic_slice_in_dim(out_grad, leading_row, FRAMES_PER_SHARD, 0))
        scores = jnp.einsum('qhd,khd->hqk', q_four, k_four) * score_scale
        text_scores = jnp.einsum('qhd,khd->hqk', q_four, text_k4) * score_scale
        weights = jnp.where(key_mask[None], jnp.exp(scores), 0.0)
        text_weights = jnp.where(text_mask[None], jnp.exp(text_scores), 0.0)
        totals = lax.optimization_barrier(jnp.sum(weights, -1)) + lax.optimization_barrier(jnp.sum(text_weights, -1))
        mixture = jnp.einsum('hqk,khd->qhd', rounded(weights), v_four) + jnp.einsum('hqk,khd->qhd', rounded(text_weights), text_v4)
        attended_output = (mixture / totals.T[:, :, None]).astype(jnp.bfloat16)
        a_four = attended_output.astype(jnp.float32)
        inner_dot = lax.optimization_barrier(jnp.sum(d_four * a_four, -1)).T
        shares = weights / totals[:, :, None]
        text_shares = text_weights / totals[:, :, None]
        value_dots = jnp.einsum('qhd,khd->hqk', d_four, v_four)
        text_dots = jnp.einsum('qhd,khd->hqk', d_four, text_v4)
        grad_scores = rounded(shares * (value_dots - inner_dot[:, :, None]))
        text_grad_scores = rounded(text_shares * (text_dots - inner_dot[:, :, None]))
        query_gradient = (jnp.einsum('hqk,khd->qhd', grad_scores, k_four) + jnp.einsum('hqk,khd->qhd', text_grad_scores, text_k4)) * score_scale
        grad_k = jnp.einsum('hqk,qhd->khd', grad_scores, q_four) * score_scale
        value_gradient = jnp.einsum('hqk,qhd->khd', rounded(shares), d_four)
        text_keys_gradient = text_keys_gradient + (jnp.einsum('hqk,qhd->khd', text_grad_scores, q_four) * score_scale).reshape(TEXT, MODEL_WIDTH)
        text_values_gradient = text_values_gradient + jnp.einsum('hqk,qhd->khd', rounded(text_shares), d_four).reshape(TEXT, MODEL_WIDTH)
        padded_key_gradient = lax.dynamic_update_slice_in_dim(padded_key_gradient, lax.dynamic_slice_in_dim(padded_key_gradient, leading_row, key_extent, 0) + grad_k.reshape(key_extent, MODEL_WIDTH), leading_row, 0)
        padded_value_gradient = lax.dynamic_update_slice_in_dim(padded_value_gradient, lax.dynamic_slice_in_dim(padded_value_gradient, leading_row, key_extent, 0) + value_gradient.reshape(key_extent, MODEL_WIDTH), leading_row, 0)
        return ((padded_key_gradient, padded_value_gradient, text_keys_gradient, text_values_gradient), (attended_output.reshape(FRAMES_PER_SHARD, MODEL_WIDTH), query_gradient.astype(jnp.bfloat16).reshape(FRAMES_PER_SHARD, MODEL_WIDTH)))
    start_state = (jnp.zeros((key_lead + FRAMES, MODEL_WIDTH), jnp.float32), jnp.zeros((key_lead + FRAMES, MODEL_WIDTH), jnp.float32), jnp.zeros((TEXT, MODEL_WIDTH), jnp.float32), jnp.zeros((TEXT, MODEL_WIDTH), jnp.float32))
    final_state, (attended_all, grad_queries) = lax.scan(shard_step, start_state, jnp.arange(N_SEQ, dtype=jnp.int32))
    attended_all = attended_all.reshape(FRAMES, MODEL_WIDTH)
    grad_queries = grad_queries.reshape(FRAMES, MODEL_WIDTH)
    grad_keys = final_state[0][key_lead:].astype(jnp.bfloat16)
    grad_values = final_state[1][key_lead:].astype(jnp.bfloat16)
    text_key_grad = final_state[2].astype(jnp.bfloat16)
    text_value_grad = final_state[3].astype(jnp.bfloat16)
    group_width = MODEL_WIDTH // N_TENSOR
    out_sum = jnp.zeros((FRAMES, MODEL_WIDTH), jnp.float32)
    input_sum = jnp.zeros((FRAMES, MODEL_WIDTH), jnp.float32)
    for group_index in range(N_TENSOR):
        group_cols = slice(group_index * group_width, (group_index + 1) * group_width)
        out_sum = out_sum + rounded(jnp.dot(attended_all[:, group_cols], w_out[group_cols], preferred_element_type=jnp.float32))
        term = jnp.dot(grad_queries[:, group_cols], w_query[:, group_cols].T, preferred_element_type=jnp.float32)
        term = term + jnp.dot(grad_keys[:, group_cols], w_key[:, group_cols].T, preferred_element_type=jnp.float32)
        term = term + jnp.dot(grad_values[:, group_cols], w_value[:, group_cols].T, preferred_element_type=jnp.float32)
        input_sum = input_sum + rounded(term)
    attn_out = out_sum.astype(jnp.bfloat16)
    d_wo = jnp.dot(attended_all.T, cotangent, preferred_element_type=jnp.float32)
    scaled = input_sum * norm_gain
    frame_grad = inv_std * (scaled - lax.optimization_barrier(jnp.mean(scaled, -1, keepdims=True)) - unit_rows * lax.optimization_barrier(jnp.mean(scaled * unit_rows, -1, keepdims=True)))
    frame_grad = frame_grad.astype(jnp.bfloat16)
    grad_padded = jnp.concatenate([frame_grad, jnp.zeros((CODEBOOKS - 1, MODEL_WIDTH), jnp.bfloat16)], 0)
    d_embedded = jnp.stack([lax.dynamic_slice_in_dim(grad_padded, delays[codebook].astype(jnp.int32), FRAMES, 0) for codebook in range(CODEBOOKS)], 1)
    d_wtk = jnp.dot(text_states.T, text_key_grad, preferred_element_type=jnp.float32)
    d_wtv = jnp.dot(text_states.T, text_value_grad, preferred_element_type=jnp.float32)
    return (attn_out, d_embedded, d_wo, d_wtk, d_wtv)
```

```python
import functools

import jax
import jax.numpy as jnp
from jax import lax
from jax.experimental import pallas as pl
from jax.experimental.pallas import tpu as pltpu
from jax.sharding import PartitionSpec as P

HD = 64
WINDOW = 1500
EPS = 1e-05
RING = 8
MESH = pl.DeviceIdType.MESH
BF = jnp.bfloat16
F32 = jnp.float32


def dims_of(n_seq):
    z = min(RING, n_seq // 2)
    return n_seq // (2 * z), z


def nt(a, b):
    return lax.dot_general(a, b, (((1,), (1,)), ((), ())), preferred_element_type=F32)


def nn(a, b):
    return lax.dot_general(a, b, (((1,), (0,)), ((), ())), preferred_element_type=F32)


def tn(a, b):
    return lax.dot_general(a, b, (((0,), (0,)), ((), ())), preferred_element_type=F32)


def send(src, dst, ssem, rsem, seq, ten):
    return pltpu.make_async_remote_copy(
        src_ref=src, dst_ref=dst, send_sem=ssem, recv_sem=rsem, device_id=(seq, ten), device_id_type=MESH
    )


def greet(partners):
    sem = pltpu.get_barrier_semaphore()
    for seq, ten in partners:
        pl.semaphore_signal(sem, inc=1, device_id=(seq, ten), device_id_type=MESH)
    pl.semaphore_wait(sem, len(partners))


class Place:
    def __init__(self, n_seq, n_ten):
        self.n_seq, self.n_ten = n_seq, n_ten
        self.H, self.Z = dims_of(n_seq)
        self.s = lax.axis_index("seq")
        self.t = lax.axis_index("tensor")
        self.c = lax.rem(self.s, 2)
        self.p = lax.div(self.s, 2)
        self.h = lax.div(self.p, self.Z)
        self.z = lax.rem(self.p, self.Z)
        self.chips = n_seq // 2

    def seq(self, h, z, c):
        return (h * self.Z + z) * 2 + c

    def sibling(self):
        return self.seq(self.h, self.z, 1 - self.c)

    def chip(self, k):
        return lax.rem(self.p + k + self.chips, self.chips) * 2 + self.c

    def other_h(self, d):
        return lax.rem(self.h + d, self.H)

    def other_z(self, d):
        return lax.rem(self.z + d + self.Z, self.Z)

    def other_t(self, d):
        return lax.rem(self.t + d + self.n_ten, self.n_ten)

    def next(self, d):
        return lax.rem(self.s + d + self.n_seq, self.n_seq)


def gather_kernel(
    n_seq, n_ten, pay, loc, head, rim, cot, g, f, cotx,
    rimbuf, blk, lsem, one_s, one_r, h_s, h_r, z_s, z_r, f_s, f_r, x_s, x_r,
):
    me = Place(n_seq, n_ten)
    H, Z, T = me.H, me.Z, n_ten
    s, t, c, h, z = me.s, me.t, me.c, me.h, me.z
    sib = me.sibling()
    half = Z // 2
    width = loc.shape[1]
    partners = [(sib, t), (me.next(1), t), (me.next(-1), t)]
    partners += [(me.seq(me.other_h(d), z, c), t) for d in range(1, H)]
    right, left = me.seq(h, me.other_z(1), c), me.seq(h, me.other_z(-1), c)
    partners += [(right, t), (left, t)]
    partners += [(s, me.other_t(d)) for d in range(1, T)]
    greet(partners)

    outgoing = []

    def go(copy):
        copy.start()
        outgoing.append(copy)

    def cols(ref, core, ten):
        return ref.at[core, :, pl.ds(pl.multiple_of(ten * width, width), width)]

    go(send(pay.at[1 - c], g.at[h, z, c], one_s.at[0], one_r.at[0], sib, t))
    go(send(rim, rimbuf, one_s.at[1], one_r.at[1], me.next(1), t))
    mine = pltpu.make_async_copy(pay.at[c], g.at[h, z, c], lsem.at[0])
    mine.start()
    blk[...] = loc[...]
    send(rim, rimbuf, one_s.at[1], one_r.at[1], me.next(1), t).wait_recv()
    blk[0:16, :] = (head[...] + jnp.where(s > 0, rimbuf[...], 0.0)).astype(BF)
    for d in range(1, T):
        go(send(blk, cols(f, c, t), f_s.at[d], f_r.at[d], s, me.other_t(d)))
    go(send(blk, cols(f, c, t), x_s.at[0], x_r.at[0], sib, t))
    own = pltpu.make_async_copy(blk, cols(f, c, t), lsem.at[1])
    own.start()
    mine.wait()
    send(pay.at[c], g.at[h, z, 1 - c], one_s.at[0], one_r.at[0], sib, t).wait_recv()
    for d in range(1, H):
        go(send(g.at[h, z], g.at[h, z], h_s.at[d], h_r.at[d], me.seq(me.other_h(d), z, c), t))

    def step(way, k, d, first):
        hh = me.other_h(d)
        zz = me.other_z(-(k - 1) if way == 0 else k - 1)
        go(send(g.at[hh, zz], g.at[hh, zz], z_s.at[way, k, d], z_r.at[way, k, d], right if way == 0 else left, t))

    def arrived(way, k, d):
        hh = me.other_h(d)
        zz = me.other_z(-k if way == 0 else k)
        send(g.at[hh, zz], g.at[hh, zz], z_s.at[way, k, d], z_r.at[way, k, d], right, t).wait_recv()

    def used(way, k, d):
        if k < half:
            return True
        if k > half:
            return False
        return (d < H // 2) if way == 0 else (d >= H // 2)

    for d in range(H):
        if d:
            hh = me.other_h(H - d)
            send(g.at[hh, z], g.at[hh, z], h_s.at[d], h_r.at[d], sib, t).wait_recv()
        dd = (H - d) % H
        for way in (0, 1):
            if used(way, 1, dd):
                step(way, 1, dd, True)
    go(send(cot, cotx, one_s.at[2], one_r.at[2], sib, t))
    for k in range(1, half + 1):
        if k == max(half - 1, 1):
            for d in range(1, T):
                tt = me.other_t(-d)
                send(blk, cols(f, c, tt), f_s.at[d], f_r.at[d], sib, t).wait_recv()
                go(send(cols(f, c, tt), cols(f, c, tt), x_s.at[d], x_r.at[d], sib, t))
        for d in [0] + [(H - e) % H for e in range(1, H)]:
            for way in (0, 1):
                if used(way, k, d):
                    arrived(way, k, d)
                    if used(way, k + 1, d):
                        step(way, k + 1, d, False)
    own.wait()
    for d in range(T):
        tt = me.other_t(-d)
        send(blk, cols(f, 1 - c, tt), x_s.at[d], x_r.at[d], sib, t).wait_recv()
    send(cot, cotx, one_s.at[2], one_r.at[2], sib, t).wait_recv()
    for copy in outgoing:
        copy.wait_send()


def gather(n_seq, n_ten, pay, loc, head, rim, cot):
    H, Z = dims_of(n_seq)
    frames, width = loc.shape
    dma = pltpu.SemaphoreType.DMA
    vm = pl.BlockSpec(memory_space=pltpu.VMEM)
    anywhere = pl.BlockSpec(memory_space=pl.ANY)
    return pl.pallas_call(
        functools.partial(gather_kernel, n_seq, n_ten),
        out_shape=(
            jax.ShapeDtypeStruct((H, Z) + pay.shape, BF),
            jax.ShapeDtypeStruct((2, frames, width * n_ten), BF),
            jax.ShapeDtypeStruct(cot.shape, BF),
        ),
        in_specs=[vm, vm, vm, vm, anywhere],
        out_specs=(anywhere, anywhere, anywhere),
        scratch_shapes=[
            pltpu.VMEM(rim.shape, F32),
            pltpu.VMEM(loc.shape, BF),
            dma((2,)),
            dma((3,)), dma((3,)),
            dma((H,)), dma((H,)),
            dma((2, Z // 2 + 1, H)), dma((2, Z // 2 + 1, H)),
            dma((n_ten,)), dma((n_ten,)),
            dma((n_ten,)), dma((n_ten,)),
        ],
        compiler_params=pltpu.CompilerParams(collective_id=0, has_side_effects=True, vmem_limit_bytes=16 << 20),
    )(pay, loc, head, rim, cot)


def attention_kernel(
    n_seq, n_ten, kv, qd, tkv, tmask, att, dq, dk, dv, tkg, tvg,
    kx, qx, wbuf, wtbuf, st, cstat, lsem, k_s, k_r, q_s, q_r, t_s, t_r,
):
    me = Place(n_seq, n_ten)
    t, p = me.t, me.p
    B = kv.shape[0]
    q_rows = B // 2
    greet([(me.chip(k), t) for k in (1, -1, 2, -2, 3, -3)])
    outgoing = []

    def go(copy):
        copy.start()
        outgoing.append(copy)

    def kslot(k):
        return kx.at[pl.ds((3 - k) * B, B)]

    def qslot(k):
        return qx.at[pl.ds(k * B, B)]

    go(send(kv, kslot(1), k_s.at[0], k_r.at[0], me.chip(1), t))
    go(send(qd, qslot(1), q_s.at[0], q_r.at[0], me.chip(-1), t))
    a = pltpu.make_async_copy(kv, kslot(0), lsem.at[0])
    b = pltpu.make_async_copy(qd, qslot(0), lsem.at[1])
    a.start()
    b.start()
    a.wait()
    b.wait()
    for k in (1, 2, 3):
        send(kv, kslot(k), k_s.at[k - 1], k_r.at[k - 1], me.chip(1), t).wait_recv()
        if k < 3:
            go(send(kslot(k), kslot(k + 1), k_s.at[k], k_r.at[k], me.chip(1), t))
        send(qd, qslot(k), q_s.at[k - 1], q_r.at[k - 1], me.chip(-1), t).wait_recv()
        if k < 3:
            go(send(qslot(k), qslot(k + 1), q_s.at[k], q_r.at[k], me.chip(-1), t))

    lane = lax.broadcasted_iota(jnp.int32, (q_rows, 128), 1)
    row = lax.broadcasted_iota(jnp.int32, (q_rows, q_rows), 0)
    col = lax.broadcasted_iota(jnp.int32, (q_rows, q_rows), 1)
    heads = [lane < HD, lane >= HD]
    chunks = (WINDOW + q_rows - 2) // q_rows + 1
    lead = (chunks - 1) * q_rows
    scale = HD ** (-0.5)
    zero = jnp.zeros((), BF)
    live = tmask[0:1, :] > 0.0

    def forward(qb, carry):
        rows = pl.ds(pl.multiple_of(qb * q_rows, q_rows), q_rows)
        q_both = qx[rows, 0:128]
        d_both = qx[rows, 128:256]
        parts = []
        stats = []
        for hd in range(2):
            q = jnp.where(heads[hd], q_both, zero) * jnp.asarray(scale, BF)
            wt = jnp.where(live, jnp.exp(nt(q, tkv[:, 0:128])), 0.0)
            wtbuf[qb, hd] = wt
            total = wt
            mix = nn(wt.astype(BF), tkv[:, 128:256])
            for j in range(chunks):
                base = pl.multiple_of((qb + j) * q_rows, q_rows)
                w = jnp.exp(nt(q, kx[pl.ds(base, q_rows), 0:128]))
                ok = p * B - 3 * B + (qb + j) * q_rows >= 0
                if j * q_rows - lead + q_rows + WINDOW - 1 < q_rows + q_rows - 1:
                    ok = ok & (lead + row - j * q_rows - col < WINDOW)
                if j == chunks - 1:
                    ok = ok & (col <= row)
                w = jnp.where(ok, w, 0.0)
                wbuf[qb, hd, j] = w
                total = total + w[:, 0:128] + w[:, 128:256]
                mix = mix + nn(w.astype(BF), kx[pl.ds(base, q_rows), 128:256])
            total = jnp.sum(total, 1, keepdims=True)
            a_head = (mix / total).astype(BF)
            parts.append(a_head)
            inner = jnp.sum(
                jnp.where(heads[hd], d_both.astype(F32) * a_head.astype(F32), 0.0), 1, keepdims=True
            )
            stats.append((1.0 / total, inner))
        att[rows, :] = jnp.where(heads[0], parts[0], parts[1])
        (r0, i0), (r1, i1) = stats
        packed = jnp.where(lane == 0, r0, jnp.where(lane == 1, r1, jnp.where(lane == 2, i0, i1)))
        cstat[rows, :] = packed
        st[0, :, pl.ds(pl.multiple_of(qb * q_rows, q_rows), q_rows)] = packed.T[0:8, :]
        return carry

    lax.fori_loop(0, 2, forward, 0)
    for k in (1, 2, 3):
        go(send(st.at[0], st.at[k], t_s.at[k], t_r.at[k], me.chip(-k), t))

    tkg[...] = jnp.zeros_like(tkg)
    tvg[...] = jnp.zeros_like(tvg)

    def query_grads(qb, carry):
        rows = pl.ds(pl.multiple_of(qb * q_rows, q_rows), q_rows)
        q_both = qx[rows, 0:128]
        d_both = qx[rows, 128:256]
        parts = []
        for hd in range(2):
            q = jnp.where(heads[hd], q_both, zero)
            d = jnp.where(heads[hd], d_both, zero)
            r = cstat[rows, hd : hd + 1]
            inner = cstat[rows, 2 + hd : 3 + hd]
            sh = wtbuf[qb, hd] * r
            ds = (sh * (nt(d, tkv[:, 128:256]) - inner)).astype(BF)
            grad = nn(ds, tkv[:, 0:128])
            tkg[...] += tn(ds, q) * scale
            tvg[...] += tn(sh.astype(BF), d)
            for j in range(chunks):
                base = pl.multiple_of((qb + j) * q_rows, q_rows)
                keys = kx[pl.ds(base, q_rows), :]
                ds = (wbuf[qb, hd, j] * r * (nt(d, keys[:, 128:256]) - inner)).astype(BF)
                grad = grad + nn(ds, keys[:, 0:128])
            parts.append(grad)
        dq[rows, :] = (jnp.where(heads[0], parts[0], parts[1]) * scale).astype(BF)
        return carry

    lax.fori_loop(0, 2, query_grads, 0)
    for k in (1, 2, 3):
        send(st.at[0], st.at[k], t_s.at[k], t_r.at[k], me.chip(-k), t).wait_recv()

    def key_grads(kb, carry):
        rows = pl.ds(pl.multiple_of(kb * q_rows, q_rows), q_rows)
        k_both = kv[rows, 0:128]
        v_both = kv[rows, 128:256]
        kparts, vparts = [], []
        for hd in range(2):
            kh = jnp.where(heads[hd], k_both, zero) * jnp.asarray(scale, BF)
            vh = jnp.where(heads[hd], v_both, zero)
            gk = jnp.zeros((q_rows, 128), F32)
            gv = jnp.zeros((q_rows, 128), F32)
            for i in range(chunks):
                base = pl.multiple_of((kb + i) * q_rows, q_rows)
                qs = qx[pl.ds(base, q_rows), :]
                blk = lax.div(kb + i, 2)
                part = pl.ds(pl.multiple_of(lax.rem(kb + i, 2) * q_rows, q_rows), q_rows)
                r = st[blk, hd : hd + 1, part]
                inner = st[blk, 2 + hd : 3 + hd, part]
                ok = p * B + (kb + i) * q_rows < n_seq * q_rows
                if i == 0:
                    ok = ok & (col >= row)
                if i * q_rows + q_rows - 1 >= WINDOW:
                    ok = ok & (i * q_rows + col - row < WINDOW)
                sh = jnp.where(ok, jnp.exp(nt(kh, qs[:, 0:128])) * r, 0.0)
                ds = (sh * (nt(vh, qs[:, 128:256]) - inner)).astype(BF)
                gv = gv + nn(sh.astype(BF), qs[:, 128:256])
                gk = gk + nn(ds, qs[:, 0:128])
            kparts.append(gk)
            vparts.append(gv)
        dk[rows, :] = (jnp.where(heads[0], kparts[0], kparts[1]) * scale).astype(BF)
        dv[rows, :] = jnp.where(heads[0], vparts[0], vparts[1]).astype(BF)
        return carry

    lax.fori_loop(0, 2, key_grads, 0)
    for copy in outgoing:
        copy.wait_send()


def attention(n_seq, n_ten, kv, qd, tkv, tmask):
    B = kv.shape[0]
    Q = B // 2
    text = tkv.shape[0]
    chunks = (WINDOW + Q - 2) // Q + 1
    dma = pltpu.SemaphoreType.DMA
    vm = pl.BlockSpec(memory_space=pltpu.VMEM)
    rows = jax.ShapeDtypeStruct((B, 128), BF)
    small = jax.ShapeDtypeStruct((text, 128), F32)
    return pl.pallas_call(
        functools.partial(attention_kernel, n_seq, n_ten),
        out_shape=(rows, rows, rows, rows, small, small),
        in_specs=[vm] * 4,
        out_specs=(vm,) * 6,
        scratch_shapes=[
            pltpu.VMEM((4 * B, 256), BF),
            pltpu.VMEM((4 * B, 256), BF),
            pltpu.VMEM((2, 2, chunks, Q, Q), F32),
            pltpu.VMEM((2, 2, Q, text), F32),
            pltpu.VMEM((4, 8, B), F32),
            pltpu.VMEM((B, 128), F32),
            dma((2,)),
            dma((3,)), dma((3,)),
            dma((3,)), dma((3,)),
            dma((4,)), dma((4,)),
        ],
        compiler_params=pltpu.CompilerParams(collective_id=1, has_side_effects=True, vmem_limit_bytes=40 << 20),
    )(kv, qd, tkv, tmask)


def scatter_kernel(
    n_seq, n_ten, op, ip, sg, ns, unit, inv, gain, out, fg, rim, sgo,
    opx, ipx, nsx, ops, ips, nss, opr, ipr, nsr, sgz, sgh, sghr, sgs, sgx,
    x_s, x_r, z_s, z_r, h_s, h_r, o_s, o_r, i_s, i_r, n_s, n_r, l_s, l_r,
):
    me = Place(n_seq, n_ten)
    H, Z, T = me.H, me.Z, n_ten
    s, t, c, h, z = me.s, me.t, me.c, me.h, me.z
    sib = me.sibling()
    width = out.shape[1]
    partners = [(sib, t), (me.next(1), t), (me.next(-1), t)]
    partners += [(me.seq(me.other_h(d), z, c), t) for d in range(1, H)]
    partners += [(me.seq(h, me.other_z(d), c), t) for d in range(1, Z)]
    partners += [(s, me.other_t(d)) for d in range(1, T)]
    greet(partners)
    outgoing = []

    def go(copy):
        copy.start()
        outgoing.append(copy)

    def cols(ref, ten):
        return ref.at[:, pl.ds(pl.multiple_of(ten * width, width), width)]

    def window(ten):
        return pl.ds(pl.multiple_of(ten * width, width), width)

    for d in range(T):
        tt = me.other_t(d)
        go(send(cols(ip.at[1 - c], tt), cols(ipx, tt), x_s.at[0, d], x_r.at[0, d], sib, t))
    go(send(ns.at[1 - c], nsx, l_s.at[0], l_r.at[0], sib, t))
    for d in range(1, Z):
        zz = me.other_z(d)
        go(send(sg.at[zz], sgz.at[d], z_s.at[d], z_r.at[d], me.seq(h, zz, c), t))
    for d in range(T):
        tt = me.other_t(d)
        go(send(cols(op.at[1 - c], tt), cols(opx, tt), x_s.at[1, d], x_r.at[1, d], sib, t))

    def exchange(which, own, from_sib, summed, landing, ss, rr):
        for d in [*range(1, T), 0]:
            tt = me.other_t(d)
            send(cols(from_sib, tt), cols(from_sib, tt), x_s.at[which, d], x_r.at[which, d], sib, t).wait_recv()
            both = own[c, :, window(tt)].astype(F32) + from_sib[:, window(tt)].astype(F32)
            summed[d] = both.astype(BF)
            if d:
                go(send(summed.at[d], landing.at[d], ss.at[d], rr.at[d], s, tt))

    exchange(0, ip, ipx, ips, ipr, i_s, i_r)
    send(nsx, nsx, l_s.at[0], l_r.at[0], sib, t).wait_recv()
    nss[...] = ns[c] + nsx[...]
    for d in range(1, T):
        go(send(nss, nsr.at[d], n_s.at[d], n_r.at[d], s, me.other_t(d)))
    exchange(1, op, opx, ops, opr, o_s, o_r)
    acc = sg[z].astype(F32)
    for d in range(1, Z):
        send(sg.at[0], sgz.at[d], z_s.at[d], z_r.at[d], sib, t).wait_recv()
        acc = acc + sgz[d].astype(F32)
    sgh[...] = acc
    for d in range(1, H):
        hh = me.other_h(d)
        go(send(sgh.at[hh], sghr.at[d], h_s.at[d], h_r.at[d], me.seq(hh, z, c), t))
    total = ips[0].astype(F32)
    sums = nss[...]
    for d in range(1, T):
        send(ips.at[d], ipr.at[d], i_s.at[d], i_r.at[d], sib, t).wait_recv()
        total = total + ipr[d].astype(F32)
        send(nss, nsr.at[d], n_s.at[d], n_r.at[d], sib, t).wait_recv()
        sums = sums + nsr[d]
    full = width * T
    tall = jnp.concatenate([sums] * (128 // sums.shape[0]), 0).T
    mean_plain = tall[:, 0:1] / full
    mean_unit = tall[:, 1:2] / full
    grad = inv[:, 0:1] * (total * gain[0:1, :] - mean_plain - unit[...] * mean_unit)
    fg[...] = grad.astype(BF)
    go(send(fg.at[pl.ds(0, 16)], rim, l_s.at[1], l_r.at[1], me.next(-1), t))
    acc = sgh[h]
    for d in range(1, H):
        send(sgh.at[0], sghr.at[d], h_s.at[d], h_r.at[d], sib, t).wait_recv()
        acc = acc + sghr[d]
    sgs[...] = acc
    go(send(sgs.at[1 - c], sgx, l_s.at[2], l_r.at[2], sib, t))
    total = ops[0].astype(F32)
    for d in range(1, T):
        send(ops.at[d], opr.at[d], o_s.at[d], o_r.at[d], sib, t).wait_recv()
        total = total + opr[d].astype(F32)
    out[...] = total.astype(BF)
    send(sgs.at[0], sgx, l_s.at[2], l_r.at[2], sib, t).wait_recv()
    sgo[:, 0:128] = jnp.where(c == 0, sgs[c], sgx[...])
    sgo[:, 128:256] = jnp.where(c == 0, sgx[...], sgs[c])
    send(rim, rim, l_s.at[1], l_r.at[1], sib, t).wait_recv()
    for copy in outgoing:
        copy.wait_send()


def scatter(n_seq, n_ten, op, ip, sg, ns, unit, inv, gain):
    H, Z = dims_of(n_seq)
    T = n_ten
    frames, width = unit.shape
    rows = sg.shape[3]
    dma = pltpu.SemaphoreType.DMA
    vm = pl.BlockSpec(memory_space=pltpu.VMEM)
    block = pltpu.VMEM((T, frames, width), BF)
    return pl.pallas_call(
        functools.partial(scatter_kernel, n_seq, n_ten),
        out_shape=(
            jax.ShapeDtypeStruct((frames, width), BF),
            jax.ShapeDtypeStruct((frames, width), BF),
            jax.ShapeDtypeStruct((16, width), BF),
            jax.ShapeDtypeStruct((rows, 256), F32),
        ),
        in_specs=[vm] * 7,
        out_specs=(vm,) * 4,
        scratch_shapes=[
            pltpu.VMEM(op.shape[1:], BF),
            pltpu.VMEM(ip.shape[1:], BF),
            pltpu.VMEM(ns.shape[1:], F32),
            block, block,
            pltpu.VMEM(ns.shape[1:], F32),
            block, block,
            pltpu.VMEM((T,) + ns.shape[1:], F32),
            pltpu.VMEM(sg.shape, BF),
            pltpu.VMEM(sg.shape[1:], F32),
            pltpu.VMEM(sg.shape[1:], F32),
            pltpu.VMEM(sg.shape[2:], F32),
            pltpu.VMEM(sg.shape[3:], F32),
            dma((2, T)), dma((2, T)),
            dma((Z,)), dma((Z,)),
            dma((H,)), dma((H,)),
            dma((T,)), dma((T,)),
            dma((T,)), dma((T,)),
            dma((T,)), dma((T,)),
            dma((3,)), dma((3,)),
        ],
        compiler_params=pltpu.CompilerParams(collective_id=2, has_side_effects=True, vmem_limit_bytes=40 << 20),
    )(op, ip, sg, ns, unit, inv, gain)


def shards(
    n_seq, n_ten, embedded, delays, norm_gain, w_query, w_key, w_value, w_out,
    text_states, w_text_key, w_text_value, text_len, cotangent,
):
    H, Z = dims_of(n_seq)
    frames, books, width = embedded.shape
    full = width * n_ten
    seq = lax.axis_index("seq")
    core = lax.rem(seq, 2)
    ten = lax.axis_index("tensor")
    R = w_query.shape[0]
    tr = w_text_key.shape[0]
    text = text_states.shape[0] * n_seq
    tdim = text_states.shape[1]

    longer = jnp.zeros((frames + 16, width), F32)
    for d in range(books):
        book = jnp.zeros((frames, width), F32)
        for k in range(books):
            book = book + jnp.where(delays[k] == d, embedded[:, k].astype(F32), 0.0)
        longer = longer + jnp.pad(book, ((d, 16 - d), (0, 0)))
    local = longer[:frames]
    rim = longer[frames:]

    states_flat = text_states.reshape(-1)
    states_flat = jnp.pad(states_flat, (0, 2048 - states_flat.shape[0])).reshape(16, 128)
    pieces = [w_query, w_key, w_value, w_out.T]
    pieces += [jnp.pad(w, ((0, 16 - tr), (0, 0))) for w in (w_text_key, w_text_value)]
    pay = jnp.concatenate(pieces, 0)
    pay = jnp.stack(
        [jnp.concatenate([pay[:, i * 128 : (i + 1) * 128], states_flat], 0) for i in range(2)], 0
    )
    g, f, cotx = gather(n_seq, n_ten, pay, local.astype(BF), local[:16], rim, cotangent)

    def part(a, n):
        return g[:, :, :, a : a + n, :].reshape(-1, 128)

    wq, wk, wv, wo = (part(i * R, R) for i in range(4))
    wtk, wtv = part(4 * R, tr), part(4 * R + 16, tr)
    states = g[:, :, :, 4 * R + 32 : 4 * R + 48, :].reshape(n_seq, 2048)
    states = states[:, : text_states.size].reshape(text, tdim)

    x = f.reshape(2 * frames, full).astype(F32)
    mean = jnp.mean(x, -1, keepdims=True)
    centred = x - mean
    inv_std = lax.rsqrt(jnp.mean(centred * centred, -1, keepdims=True) + EPS)
    unit = centred * inv_std
    normed = (unit * norm_gain).astype(BF)
    cot = jnp.where(core == 0, jnp.stack([cotangent, cotx]), jnp.stack([cotx, cotangent]))
    cot = cot.reshape(2 * frames, full)
    kv = jnp.concatenate([nn(normed, wk).astype(BF), nn(normed, wv).astype(BF)], 1)
    qd = jnp.concatenate([nn(normed, wq).astype(BF), nn(cot, wo).astype(BF)], 1)
    tkv = jnp.concatenate([nn(states, wtk).astype(BF), nn(states, wtv).astype(BF)], 1)
    tmask = (lax.broadcasted_iota(jnp.int32, (8, text), 1) < text_len[0]).astype(F32)

    att, dq, dk, dv, tkg, tvg = attention(n_seq, n_ten, kv, qd, tkv, tmask)

    op = nt(att, wo).astype(BF).reshape(2, frames, full)
    ipf = nt(dq, wq) + nt(dk, wk) + nt(dv, wv)
    scaled = ipf * norm_gain
    ns = jnp.stack([jnp.sum(scaled, 1), jnp.sum(scaled * unit, 1)], 0).reshape(2, 2, frames)
    ns = jnp.pad(ns.transpose(1, 0, 2), ((0, 0), (0, 6), (0, 0)))
    ip = ipf.astype(BF).reshape(2, frames, full)

    def by_owner(grads, rows, padded):
        grads = grads.reshape(H, Z, 2, rows, 128)
        grads = jnp.pad(grads, ((0, 0), (0, 0), (0, 0), (0, padded - rows), (0, 0)))
        return grads.transpose(1, 0, 2, 3, 4)

    sg = jnp.concatenate(
        [
            by_owner(tn(cot, att), R, R),
            by_owner(tn(states, tkg.astype(BF)), tr, 16),
            by_owner(tn(states, tvg.astype(BF)), tr, 16),
        ],
        3,
    ).astype(BF)
    unit_here = lax.dynamic_slice(unit, (core * frames, ten * width), (frames, width))
    inv_here = jnp.broadcast_to(lax.dynamic_slice_in_dim(inv_std, core * frames, frames, 0), (frames, 128))
    gain_here = jnp.broadcast_to(lax.dynamic_slice_in_dim(norm_gain, ten * width, width, 0)[None], (8, width))
    out, fg, above, sgo = scatter(n_seq, n_ten, op, ip, sg, ns, unit_here, inv_here, gain_here)
    above = jnp.where(seq < n_seq - 1, above, jnp.zeros_like(above))
    longer = jnp.concatenate([fg, above], 0)
    d_embedded = jnp.stack(
        [
            functools.reduce(
                lambda x, d: jnp.where(delays[k] == d, longer[d : d + frames], x),
                range(1, books),
                longer[:frames],
            )
            for k in range(books)
        ],
        1,
    )
    return (out, d_embedded, sgo[:R].T, sgo[R : R + tr], sgo[R + 16 : R + 16 + tr])


def solution(mesh):
    placed = (
        P("seq", None, "tensor"), P(), P(),
        P("seq", "tensor"), P("seq", "tensor"), P("seq", "tensor"), P("tensor", "seq"),
        P("seq", None), P("seq", "tensor"), P("seq", "tensor"), P(), P("seq", None),
    )
    return jax.shard_map(
        functools.partial(shards, mesh.shape["seq"], mesh.shape["tensor"]),
        mesh=mesh,
        in_specs=placed,
        out_specs=(
            P("seq", "tensor"), P("seq", None, "tensor"), P("tensor", "seq"),
            P("seq", "tensor"), P("seq", "tensor"),
        ),
        check_vma=False,
    )
```

```python
import functools

import jax
import jax.numpy as jnp
from jax import lax
from jax.experimental import pallas as pl
from jax.experimental.pallas import tpu as pltpu
from jax.sharding import PartitionSpec as P

HD = 64
WINDOW = 1500
EPS = 1e-05
RING = 8
MESH = pl.DeviceIdType.MESH
BF = jnp.bfloat16
F32 = jnp.float32


def dims_of(n_seq):
    z = min(RING, n_seq // 2)
    return n_seq // (2 * z), z


def nt(a, b):
    return lax.dot_general(a, b, (((1,), (1,)), ((), ())), preferred_element_type=F32)


def nn(a, b):
    return lax.dot_general(a, b, (((1,), (0,)), ((), ())), preferred_element_type=F32)


def tn(a, b):
    return lax.dot_general(a, b, (((0,), (0,)), ((), ())), preferred_element_type=F32)


def send(src, dst, ssem, rsem, seq, ten):
    return pltpu.make_async_remote_copy(
        src_ref=src, dst_ref=dst, send_sem=ssem, recv_sem=rsem, device_id=(seq, ten), device_id_type=MESH
    )


def greet(partners):
    sem = pltpu.get_barrier_semaphore()
    for seq, ten in partners:
        pl.semaphore_signal(sem, inc=1, device_id=(seq, ten), device_id_type=MESH)
    pl.semaphore_wait(sem, len(partners))


class Place:
    def __init__(self, n_seq, n_ten):
        self.n_seq, self.n_ten = n_seq, n_ten
        self.H, self.Z = dims_of(n_seq)
        self.s = lax.axis_index("seq")
        self.t = lax.axis_index("tensor")
        self.c = lax.rem(self.s, 2)
        self.p = lax.div(self.s, 2)
        self.h = lax.div(self.p, self.Z)
        self.z = lax.rem(self.p, self.Z)
        self.chips = n_seq // 2

    def seq(self, h, z, c):
        return (h * self.Z + z) * 2 + c

    def sibling(self):
        return self.seq(self.h, self.z, 1 - self.c)

    def chip(self, k):
        return lax.rem(self.p + k + self.chips, self.chips) * 2 + self.c

    def other_h(self, d):
        return lax.rem(self.h + d, self.H)

    def other_z(self, d):
        return lax.rem(self.z + d + self.Z, self.Z)

    def other_t(self, d):
        return lax.rem(self.t + d + self.n_ten, self.n_ten)

    def next(self, d):
        return lax.rem(self.s + d + self.n_seq, self.n_seq)


def fused_kernel(
    n_seq, n_ten, delays, text_len, pay, emb, gain, cot, out, de, sgo,
    g, f, cots, rimbuf, blk, longer, nst, normed, states32, states,
    kv, qd, tkv, kx, qx, wbuf, wtbuf, mixbuf, totbuf, st, cstat,
    att, dq, dk, dv, tkg, tvg,
    opt, opx, opr, ipt, ipx, ipr, ops, ips, nst_out, nsx, nss, nsr,
    sga, sgza, sgb, sgzb, sgh, sghr, sgs, sgx, fg, rim,
    lsem, one_s, one_r, h_s, h_r, z_s, z_r, f_s, f_r, x_s, x_r,
    k_s, k_r, q_s, q_r, t_s, t_r, ox_s, ox_r, ix_s, ix_r, o_s, o_r, i_s, i_r, n_s, n_r,
    za_s, za_r, zb_s, zb_r, hh_s, hh_r,
):
    me = Place(n_seq, n_ten)
    H, Z, T = me.H, me.Z, n_ten
    s, t, c, h, z, p = me.s, me.t, me.c, me.h, me.z, me.p
    sib = me.sibling()
    half = Z // 2
    width = emb.shape[2]
    Q = emb.shape[1]
    B = 2 * Q
    R = sga.shape[3]
    text = states.shape[0]
    full = width * T
    scale = HD ** (-0.5)
    zero = jnp.zeros((), BF)
    right, left = me.seq(h, me.other_z(1), c), me.seq(h, me.other_z(-1), c)
    partners = [(sib, t), (me.next(1), t), (me.next(-1), t)]
    partners += [(me.seq(me.other_h(d), z, c), t) for d in range(1, H)]
    partners += [(me.seq(h, me.other_z(d), c), t) for d in range(1, Z)]
    partners += [(s, me.other_t(d)) for d in range(1, T)]
    partners += [(me.chip(k), t) for k in (1, -1, 2, -2, 3, -3)]
    greet(partners)
    outgoing = []

    def go(copy):
        copy.start()
        outgoing.append(copy)

    def half_rows(core):
        return pl.ds(pl.multiple_of(core * Q, Q), Q)

    go(send(pay.at[1 - c], g.at[p, c], one_s.at[0], one_r.at[0], sib, t))
    mine = pltpu.make_async_copy(pay.at[c], g.at[p, c], lsem.at[0])
    mine.start()
    longer[...] = jnp.zeros_like(longer)
    for d in range(4):
        book = jnp.zeros((Q, width), F32)
        for k in range(4):
            book = book + jnp.where(delays[k] == d, emb[k].astype(F32), 0.0)
        longer[d : d + Q, :] = longer[d : d + Q, :] + book
    go(send(longer.at[pl.ds(Q, 16)], rimbuf, one_s.at[1], one_r.at[1], me.next(1), t))
    mine.wait()
    send(pay.at[c], g.at[p, 1 - c], one_s.at[0], one_r.at[0], sib, t).wait_recv()
    for d in range(1, H):
        go(send(g.at[p], g.at[p], h_s.at[d], h_r.at[d], me.seq(me.other_h(d), z, c), t))

    def step(way, k, d):
        hh = me.other_h(d)
        zz = me.other_z(-(k - 1) if way == 0 else k - 1)
        go(send(g.at[hh * Z + zz], g.at[hh * Z + zz], z_s.at[way, k, d], z_r.at[way, k, d], right if way == 0 else left, t))

    def arrived(way, k, d):
        hh = me.other_h(d)
        zz = me.other_z(-k if way == 0 else k)
        send(g.at[hh * Z + zz], g.at[hh * Z + zz], z_s.at[way, k, d], z_r.at[way, k, d], right, t).wait_recv()

    def used(way, k, d):
        if k < half:
            return True
        if k > half:
            return False
        return (d < H // 2) if way == 0 else (d >= H // 2)

    for way in (0, 1):
        if used(way, 1, 0):
            step(way, 1, 0)
    send(longer.at[pl.ds(Q, 16)], rimbuf, one_s.at[1], one_r.at[1], me.next(1), t).wait_recv()
    blk[...] = longer[0:Q, :].astype(BF)
    blk[0:16, :] = (longer[0:16, :] + jnp.where(s > 0, rimbuf[...], 0.0)).astype(BF)
    for d in range(1, T):
        go(send(blk, f.at[c, t], f_s.at[d], f_r.at[d], s, me.other_t(d)))
    go(send(blk, f.at[c, t], x_s.at[0], x_r.at[0], sib, t))
    own = pltpu.make_async_copy(blk, f.at[c, t], lsem.at[1])
    own.start()
    for d in range(1, H):
        hh = me.other_h(H - d)
        send(g.at[hh * Z + z], g.at[hh * Z + z], h_s.at[d], h_r.at[d], sib, t).wait_recv()
        for way in (0, 1):
            if used(way, 1, H - d):
                step(way, 1, H - d)
    go(send(cot, cots.at[half_rows(c)], one_s.at[2], one_r.at[2], sib, t))
    mycot = pltpu.make_async_copy(cot, cots.at[half_rows(c)], lsem.at[2])
    mycot.start()
    order = [0] + [H - e for e in range(1, H)]
    ring_last = half

    def ring(k):
        for d in order:
            for way in (0, 1):
                if used(way, k, d):
                    arrived(way, k, d)
                    if used(way, k + 1, d):
                        step(way, k + 1, d)

    def pass_frames():
        for d in range(1, T):
            tt = me.other_t(-d)
            send(blk, f.at[c, tt], f_s.at[d], f_r.at[d], sib, t).wait_recv()
            go(send(f.at[c, tt], f.at[c, tt], x_s.at[d], x_r.at[d], sib, t))

    def norm(cc):
        def fold(v):
            return v[:, 0:128] + v[:, 128:256]

        acc = jnp.zeros((Q, 128), F32)
        acc = lax.fori_loop(0, T, lambda i, a: a + fold(f[cc, i].astype(F32)), acc)
        mean = jnp.sum(acc, 1, keepdims=True) / full

        def second(i, a):
            v = f[cc, i].astype(F32) - mean
            return a + fold(v * v)

        acc = lax.fori_loop(0, T, second, jnp.zeros((Q, 128), F32))
        inv = lax.rsqrt(jnp.sum(acc, 1, keepdims=True) / full + EPS)
        lane128 = lax.broadcasted_iota(jnp.int32, (Q, 128), 1)
        nst[cc] = jnp.where(lane128 == 0, mean, inv)

        def third(i, carry):
            w = pl.ds(pl.multiple_of(i * width, width), width)
            v = (f[cc, i].astype(F32) - mean) * inv
            normed[half_rows(cc), w] = (v * gain[0:1, w]).astype(BF)
            return carry

        lax.fori_loop(0, T, third, 0)

    for k in range(1, half):
        if k == max(half - 2, 1):
            pass_frames()
        ring(k)
    if half == 1:
        pass_frames()
    own.wait()
    norm(c)
    for d in range(T):
        tt = me.other_t(-d)
        send(blk, f.at[1 - c, tt], x_s.at[d], x_r.at[d], sib, t).wait_recv()
    norm(1 - c)
    ring(half)

    def weight(i):
        return g[:, :, i * R : (i + 1) * R, :].reshape(n_seq * R, 128)

    def project(src, i, dst, lanes):
        def go_rows(rb, carry):
            rows = half_rows(rb)
            dst[rows, lanes] = nn(src[rows, :], weight(i)).astype(BF)
            return carry

        lax.fori_loop(0, 2, go_rows, 0)

    lo, hi = slice(0, 128), slice(128, 256)

    def kslot(k):
        return kx.at[pl.ds((3 - k) * B, B)]

    def qslot(k):
        return qx.at[pl.ds(k * B, B)]

    project(normed, 1, kv, lo)
    project(normed, 2, kv, hi)
    go(send(kv, kslot(1), k_s.at[0], k_r.at[0], me.chip(1), t))
    project(normed, 0, qd, lo)
    mycot.wait()
    send(cot, cots.at[half_rows(c)], one_s.at[2], one_r.at[2], sib, t).wait_recv()
    project(cots, 3, qd, hi)
    go(send(qd, qslot(1), q_s.at[0], q_r.at[0], me.chip(-1), t))
    kx[pl.ds(3 * B, B), :] = kv[...]
    qx[pl.ds(0, B), :] = qd[...]

    states32[...] = g[:, :, 4 * R + 32 : 4 * R + 48, :].reshape(n_seq, 16, 128).astype(F32)
    per = text // n_seq
    qn = 16 // per
    for r in range(per):
        for qq in range(qn):
            states[r * n_seq : (r + 1) * n_seq, qq * 128 : (qq + 1) * 128] = states32[:, r * qn + qq, :].astype(BF)
    for i in range(2):
        w = g[:, :, 4 * R + 16 * i : 4 * R + 16 * (i + 1), :].reshape(n_seq * 16, 128)
        tkv[:, i * 128 : (i + 1) * 128] = nn(states[...], w).astype(BF)
    token = lax.broadcasted_iota(jnp.int32, (1, text), 1)
    live = lax.rem(token, n_seq) * per + lax.div(token, n_seq) < text_len[0]

    lane = lax.broadcasted_iota(jnp.int32, (Q, 128), 1)
    row = lax.broadcasted_iota(jnp.int32, (Q, Q), 0)
    col = lax.broadcasted_iota(jnp.int32, (Q, Q), 1)
    heads = [lane < HD, lane >= HD]
    chunks = (WINDOW + Q - 2) // Q + 1
    lead = (chunks - 1) * Q

    def forward_chunk(qb, hd, q, j):
        base = pl.multiple_of((qb + j) * Q, Q)
        w = jnp.exp(nt(q, kx[pl.ds(base, Q), lo]))
        ok = p * B - 3 * B + (qb + j) * Q >= 0
        if lead - j * Q + Q - 1 >= WINDOW:
            ok = ok & (lead + row - j * Q - col < WINDOW)
        if j == chunks - 1:
            ok = ok & (col <= row)
        w = jnp.where(ok, w, 0.0)
        wbuf[qb, hd, j] = w
        return w[:, 0:128] + w[:, 128:256], nn(w.astype(BF), kx[pl.ds(base, Q), hi])

    def forward(k):
        for qb in range(2):
            q_both = qd[qb * Q : (qb + 1) * Q, lo]
            for hd in range(2):
                q = jnp.where(heads[hd], q_both, zero) * jnp.asarray(scale, BF)
                if k == 0:
                    wt = jnp.where(live, jnp.exp(nt(q, tkv[:, lo])), 0.0)
                    wtbuf[qb, hd] = wt
                    total, mix = wt, nn(wt.astype(BF), tkv[:, hi])
                else:
                    total, mix = totbuf[qb, hd], mixbuf[qb, hd]
                for j in range(chunks):
                    if (qb + j) // 2 == 3 - k:
                        a, b = forward_chunk(qb, hd, q, j)
                        total, mix = total + a, mix + b
                totbuf[qb, hd], mixbuf[qb, hd] = total, mix

    def pass_keys(k):
        send(kv, kslot(k), k_s.at[k - 1], k_r.at[k - 1], me.chip(1), t).wait_recv()
        if k < 3:
            go(send(kslot(k), kslot(k + 1), k_s.at[k], k_r.at[k], me.chip(1), t))

    def pass_queries(k):
        send(qd, qslot(k), q_s.at[k - 1], q_r.at[k - 1], me.chip(-1), t).wait_recv()
        if k < 3:
            go(send(qslot(k), qslot(k + 1), q_s.at[k], q_r.at[k], me.chip(-1), t))

    forward(0)
    for k in (1, 2, 3):
        pass_keys(k)
        pass_queries(k)
        forward(k)
    for qb in range(2):
        rows = slice(qb * Q, (qb + 1) * Q)
        d_both = qd[rows, hi].astype(F32)
        parts, stats = [], []
        for hd in range(2):
            total = jnp.sum(totbuf[qb, hd], 1, keepdims=True)
            a_head = (mixbuf[qb, hd] / total).astype(BF)
            parts.append(a_head)
            inner = jnp.sum(jnp.where(heads[hd], d_both * a_head.astype(F32), 0.0), 1, keepdims=True)
            stats.append((1.0 / total, inner))
        att[rows, :] = jnp.where(heads[0], parts[0], parts[1])
        (r0, i0), (r1, i1) = stats
        packed = jnp.where(lane == 0, r0, jnp.where(lane == 1, r1, jnp.where(lane == 2, i0, i1)))
        cstat[rows, :] = packed
        st[0, :, rows] = packed.T[0:8, :]
    for k in (1, 2, 3):
        go(send(st.at[0], st.at[k], t_s.at[k], t_r.at[k], me.chip(-k), t))

    def w_block(i, tt):
        n = width // (2 * R)
        return g[pl.ds(tt * n, n), :, i * R : (i + 1) * R, :].reshape(width, 128)

    for d in range(T):
        tt = me.other_t(d)
        opt[d] = nt(att[half_rows(1 - c), :], w_block(3, tt)).astype(BF)
        go(send(opt.at[d], opx.at[d], ox_s.at[d], ox_r.at[d], sib, t))
    for e in range(full // B):
        piece = tn(att[...], cots[:, e * B : (e + 1) * B])
        n = B // R
        for a in range(B // 128):
            rows = piece[:, a * 128 : (a + 1) * 128].T.astype(BF).reshape(128 // R, R, 128)
            for b in range(128 // R):
                who = e * n + a * (128 // R) + b
                hh, zz, cc = who // (2 * Z), (who // 2) % Z, who % 2
                sga[zz, hh, cc] = rows[b]
    for d in range(1, Z):
        zz = me.other_z(d)
        go(send(sga.at[zz], sgza.at[d], za_s.at[d], za_r.at[d], me.seq(h, zz, c), t))

    tkg[...] = jnp.zeros_like(tkg)
    tvg[...] = jnp.zeros_like(tvg)

    def query_grads(qb, carry):
        rows = half_rows(qb)
        q_both = qd[rows, lo]
        d_both = qd[rows, hi]
        parts = []
        for hd in range(2):
            q = jnp.where(heads[hd], q_both, zero)
            d = jnp.where(heads[hd], d_both, zero)
            r = cstat[rows, hd : hd + 1]
            inner = cstat[rows, 2 + hd : 3 + hd]
            sh = wtbuf[qb, hd] * r
            ds = (sh * (nt(d, tkv[:, hi]) - inner)).astype(BF)
            grad = nn(ds, tkv[:, lo])
            tkg[...] += tn(ds, q) * scale
            tvg[...] += tn(sh.astype(BF), d)
            for j in range(chunks):
                base = pl.multiple_of((qb + j) * Q, Q)
                keys = kx[pl.ds(base, Q), :]
                ds = (wbuf[qb, hd, j] * r * (nt(d, keys[:, hi]) - inner)).astype(BF)
                grad = grad + nn(ds, keys[:, lo])
            parts.append(grad)
        dq[rows, :] = (jnp.where(heads[0], parts[0], parts[1]) * scale).astype(BF)
        return carry

    lax.fori_loop(0, 2, query_grads, 0)
    for i, grad in enumerate((tkg, tvg)):
        piece = tn(states[...], grad[...].astype(BF)).astype(BF).reshape(H, Z, 2, 16, 128)
        for zz in range(Z):
            sgb[zz, :, :, 16 * i : 16 * (i + 1), :] = piece[:, zz]
    for d in range(1, Z):
        zz = me.other_z(d)
        go(send(sgb.at[zz], sgzb.at[d], zb_s.at[d], zb_r.at[d], me.seq(h, zz, c), t))
    for d in [*range(1, T), 0]:
        tt = me.other_t(d)
        send(opt.at[d], opx.at[d], ox_s.at[d], ox_r.at[d], sib, t).wait_recv()
        ops[d] = (nt(att[half_rows(c), :], w_block(3, tt)) + opx[d].astype(F32)).astype(BF)
        if d:
            go(send(ops.at[d], opr.at[d], o_s.at[d], o_r.at[d], s, tt))
    for k in (1, 2, 3):
        send(st.at[0], st.at[k], t_s.at[k], t_r.at[k], me.chip(-k), t).wait_recv()

    def key_grads(kb, carry):
        rows = half_rows(kb)
        k_both = kv[rows, lo]
        v_both = kv[rows, hi]
        kparts, vparts = [], []
        for hd in range(2):
            kh = jnp.where(heads[hd], k_both, zero) * jnp.asarray(scale, BF)
            vh = jnp.where(heads[hd], v_both, zero)
            gk = jnp.zeros((Q, 128), F32)
            gv = jnp.zeros((Q, 128), F32)
            for i in range(chunks):
                base = pl.multiple_of((kb + i) * Q, Q)
                qs = qx[pl.ds(base, Q), :]
                at = lax.div(kb + i, 2)
                part = pl.ds(pl.multiple_of(lax.rem(kb + i, 2) * Q, Q), Q)
                r = st[at, hd : hd + 1, part]
                inner = st[at, 2 + hd : 3 + hd, part]
                ok = p * B + (kb + i) * Q < n_seq * Q
                if i == 0:
                    ok = ok & (col >= row)
                if i * Q + Q - 1 >= WINDOW:
                    ok = ok & (i * Q + col - row < WINDOW)
                sh = jnp.where(ok, jnp.exp(nt(kh, qs[:, lo])) * r, 0.0)
                ds = (sh * (nt(vh, qs[:, hi]) - inner)).astype(BF)
                gv = gv + nn(sh.astype(BF), qs[:, hi])
                gk = gk + nn(ds, qs[:, lo])
            kparts.append(gk)
            vparts.append(gv)
        dk[rows, :] = (jnp.where(heads[0], kparts[0], kparts[1]) * scale).astype(BF)
        dv[rows, :] = jnp.where(heads[0], vparts[0], vparts[1]).astype(BF)
        return carry

    lax.fori_loop(0, 2, key_grads, 0)

    def input_block(cc, tt):
        rows = half_rows(cc)
        grad = nt(dq[rows, :], w_block(0, tt)) + nt(dk[rows, :], w_block(1, tt)) + nt(dv[rows, :], w_block(2, tt))
        lanes = pl.ds(pl.multiple_of(tt * width, width), width)
        scaled = grad * gain[0:1, lanes]
        unit = (f[cc, tt].astype(F32) - nst[cc, :, 0:1]) * nst[cc, :, 1:2]
        both = scaled * unit
        return grad, scaled[:, 0:128] + scaled[:, 128:256], both[:, 0:128] + both[:, 128:256]

    def pack_sums(plain, unit):
        plain = jnp.sum(plain, 1, keepdims=True)
        unit = jnp.sum(unit, 1, keepdims=True)
        return jnp.where(lane == 0, plain, unit).T[0:8, :]

    plain = jnp.zeros((Q, 128), F32)
    unit = jnp.zeros((Q, 128), F32)
    for d in [*range(1, T), 0]:
        tt = me.other_t(d)
        grad, a, b = input_block(1 - c, tt)
        plain, unit = plain + a, unit + b
        ipt[d] = grad.astype(BF)
        go(send(ipt.at[d], ipx.at[d], ix_s.at[d], ix_r.at[d], sib, t))
    nst_out[...] = pack_sums(plain, unit)
    go(send(nst_out, nsx, n_s.at[0], n_r.at[0], sib, t))
    plain = jnp.zeros((Q, 128), F32)
    unit = jnp.zeros((Q, 128), F32)
    for d in [*range(1, T), 0]:
        tt = me.other_t(d)
        grad, a, b = input_block(c, tt)
        plain, unit = plain + a, unit + b
        send(ipt.at[d], ipx.at[d], ix_s.at[d], ix_r.at[d], sib, t).wait_recv()
        ips[d] = (grad + ipx[d].astype(F32)).astype(BF)
        if d:
            go(send(ips.at[d], ipr.at[d], i_s.at[d], i_r.at[d], s, tt))
    send(nst_out, nsx, n_s.at[0], n_r.at[0], sib, t).wait_recv()
    nss[...] = pack_sums(plain, unit) + nsx[...]
    for d in range(1, T):
        go(send(nss, nsr.at[d], n_s.at[d], n_r.at[d], s, me.other_t(d)))

    acc_a = sga[z].astype(F32)
    acc_b = sgb[z].astype(F32)
    for d in range(1, Z):
        send(sga.at[0], sgza.at[d], za_s.at[d], za_r.at[d], sib, t).wait_recv()
        send(sgb.at[0], sgzb.at[d], zb_s.at[d], zb_r.at[d], sib, t).wait_recv()
        acc_a = acc_a + sgza[d].astype(F32)
        acc_b = acc_b + sgzb[d].astype(F32)
    sgh[:, :, 0:R, :] = acc_a
    sgh[:, :, R : R + 32, :] = acc_b
    for d in range(1, H):
        hh = me.other_h(d)
        go(send(sgh.at[hh], sghr.at[d], hh_s.at[d], hh_r.at[d], me.seq(hh, z, c), t))

    total = ips[0].astype(F32)
    sums = nss[...]
    for d in range(1, T):
        send(nss, nsr.at[d], n_s.at[d], n_r.at[d], sib, t).wait_recv()
        sums = sums + nsr[d]
        send(ips.at[d], ipr.at[d], i_s.at[d], i_r.at[d], sib, t).wait_recv()
        total = total + ipr[d].astype(F32)
    tall = jnp.concatenate([sums] * 16, 0).T
    here = pl.ds(pl.multiple_of(t * width, width), width)
    inv = nst[c, :, 1:2]
    unit = (f[c, t].astype(F32) - nst[c, :, 0:1]) * inv
    grad = inv * (total * gain[0:1, here] - tall[:, 0:1] / full - unit * (tall[:, 1:2] / full))
    fg[...] = grad.astype(BF)
    go(send(fg.at[pl.ds(0, 16)], rim, one_s.at[3], one_r.at[3], me.next(-1), t))
    acc = sgh[h]
    for d in range(1, H):
        send(sgh.at[0], sghr.at[d], hh_s.at[d], hh_r.at[d], sib, t).wait_recv()
        acc = acc + sghr[d]
    sgs[...] = acc
    go(send(sgs.at[1 - c], sgx, one_s.at[4], one_r.at[4], sib, t))
    longer[0:Q, :] = fg[...].astype(F32)
    total = ops[0].astype(F32)
    for d in range(1, T):
        send(ops.at[d], opr.at[d], o_s.at[d], o_r.at[d], sib, t).wait_recv()
        total = total + opr[d].astype(F32)
    out[...] = total.astype(BF)
    send(fg.at[pl.ds(0, 16)], rim, one_s.at[3], one_r.at[3], sib, t).wait_recv()
    send(sgs.at[0], sgx, one_s.at[4], one_r.at[4], sib, t).wait_recv()
    sgo[:, lo] = jnp.where(c == 0, sgs[c], sgx[...])
    sgo[:, hi] = jnp.where(c == 0, sgx[...], sgs[c])
    for copy in outgoing:
        copy.wait_send()
    longer[Q : Q + 16, :] = jnp.where(s < n_seq - 1, rim[...].astype(F32), 0.0)
    for k in range(4):
        book = jnp.zeros((Q, width), F32)
        for d in range(4):
            book = jnp.where(delays[k] == d, longer[d : d + Q, :], book)
        de[k] = book.astype(BF)


def fused(n_seq, n_ten, delays, text_len, pay, emb, gain, cot, text):
    H, Z = dims_of(n_seq)
    T = n_ten
    _, Q, W = emb.shape
    B = 2 * Q
    full = W * T
    R = (pay.shape[1] - 48) // 4
    chunks = (WINDOW + Q - 2) // Q + 1
    dma = pltpu.SemaphoreType.DMA
    vm = pl.BlockSpec(memory_space=pltpu.VMEM)
    sm = pl.BlockSpec(memory_space=pltpu.SMEM)
    V = pltpu.VMEM
    block = V((T, Q, W), BF)
    rows = V((B, 128), BF)
    small = V((text, 128), F32)
    sums = V((8, Q), F32)

    def pair(*shape):
        return [dma(shape), dma(shape)]

    return pl.pallas_call(
        functools.partial(fused_kernel, n_seq, n_ten),
        out_shape=(
            jax.ShapeDtypeStruct((Q, W), BF),
            jax.ShapeDtypeStruct((4, Q, W), BF),
            jax.ShapeDtypeStruct((R + 32, 256), F32),
        ),
        in_specs=[sm, sm, vm, vm, vm, pl.BlockSpec(memory_space=pl.ANY)],
        out_specs=(vm,) * 3,
        scratch_shapes=[
            V((H * Z,) + pay.shape, BF), V((2, T, Q, W), BF), V((B, full), BF), V((16, W), F32), V((Q, W), BF),
            V((Q + 16, W), F32), V((2, Q, 128), F32), V((B, full), BF), V((n_seq, 16, 128), F32),
            V((text, n_seq * 16), BF),
            V((B, 256), BF), V((B, 256), BF), V((text, 256), BF), V((4 * B, 256), BF), V((4 * B, 256), BF),
            V((2, 2, chunks, Q, Q), F32), V((2, 2, Q, text), F32), V((2, 2, Q, 128), F32), V((2, 2, Q, 128), F32),
            V((4, 8, B), F32), V((B, 128), F32),
            rows, rows, rows, rows, small, small,
            block, block, block, block, block, block, block, block, sums, sums, sums, V((T, 8, Q), F32),
            V((Z, H, 2, R, 128), BF), V((Z, H, 2, R, 128), BF), V((Z, H, 2, 32, 128), BF), V((Z, H, 2, 32, 128), BF),
            V((H, 2, R + 32, 128), F32), V((H, 2, R + 32, 128), F32), V((2, R + 32, 128), F32), V((R + 32, 128), F32),
            V((Q, W), BF), V((16, W), BF),
            dma((3,)), *pair(5), *pair(H), *pair(2, Z // 2 + 1, H), *pair(T), *pair(T),
            *pair(3), *pair(3), *pair(4), *pair(T), *pair(T), *pair(T), *pair(T), *pair(T),
            *pair(Z), *pair(Z), *pair(H),
        ],
        compiler_params=pltpu.CompilerParams(collective_id=0, has_side_effects=True, vmem_limit_bytes=56 << 20),
    )(delays, text_len, pay, emb, gain, cot)


def shards(
    n_seq, n_ten, embedded, delays, norm_gain, w_query, w_key, w_value, w_out,
    text_states, w_text_key, w_text_value, text_len, cotangent,
):
    R = w_query.shape[0]
    tr = w_text_key.shape[0]
    per = text_states.shape[0]
    states = jnp.pad(text_states.reshape(per, n_seq, tr), ((0, 0), (0, 0), (0, 16 - tr))).reshape(16, 128)
    pieces = [w_query, w_key, w_value, w_out.T]
    pieces += [jnp.pad(w, ((0, 16 - tr), (0, 0))) for w in (w_text_key, w_text_value)]
    pay = jnp.concatenate(pieces, 0)
    pay = jnp.stack([jnp.concatenate([pay[:, i * 128 : (i + 1) * 128], states], 0) for i in range(2)], 0)
    out, de, sgo = fused(
        n_seq, n_ten, delays, text_len, pay, embedded.transpose(1, 0, 2), norm_gain.reshape(1, -1),
        cotangent, per * n_seq,
    )
    return (out, de.transpose(1, 0, 2), sgo[:R].T, sgo[R : R + tr], sgo[R + 16 : R + 16 + tr])


def solution(mesh):
    placed = (
        P("seq", None, "tensor"), P(), P(),
        P("seq", "tensor"), P("seq", "tensor"), P("seq", "tensor"), P("tensor", "seq"),
        P("seq", None), P("seq", "tensor"), P("seq", "tensor"), P(), P("seq", None),
    )
    return jax.shard_map(
        functools.partial(shards, mesh.shape["seq"], mesh.shape["tensor"]),
        mesh=mesh,
        in_specs=placed,
        out_specs=(
            P("seq", "tensor"), P("seq", None, "tensor"), P("tensor", "seq"),
            P("seq", "tensor"), P("seq", "tensor"),
        ),
        check_vma=False,
    )
```

```python
import functools

import jax
import jax.numpy as jnp
from jax import lax
from jax.experimental import pallas as pl
from jax.experimental.pallas import tpu as pltpu
from jax.sharding import PartitionSpec as P

HD = 64
WINDOW = 1500
EPS = 1e-05
RING = 8
RELAY = 1
MESH = pl.DeviceIdType.MESH
BF = jnp.bfloat16
F32 = jnp.float32


def dims_of(n_seq):
    z = min(RING, n_seq // 2)
    return n_seq // (2 * z), z


def nt(a, b):
    return lax.dot_general(a, b, (((1,), (1,)), ((), ())), preferred_element_type=F32)


def nn(a, b):
    return lax.dot_general(a, b, (((1,), (0,)), ((), ())), preferred_element_type=F32)


def tn(a, b):
    return lax.dot_general(a, b, (((0,), (0,)), ((), ())), preferred_element_type=F32)


def send(src, dst, ssem, rsem, seq, ten):
    return pltpu.make_async_remote_copy(
        src_ref=src, dst_ref=dst, send_sem=ssem, recv_sem=rsem, device_id=(seq, ten), device_id_type=MESH
    )


def greet(partners):
    sem = pltpu.get_barrier_semaphore()
    for seq, ten in partners:
        pl.semaphore_signal(sem, inc=1, device_id=(seq, ten), device_id_type=MESH)
    pl.semaphore_wait(sem, len(partners))


class Place:
    def __init__(self, n_seq, n_ten):
        self.n_seq, self.n_ten = n_seq, n_ten
        self.H, self.Z = dims_of(n_seq)
        self.s = lax.axis_index("seq")
        self.t = lax.axis_index("tensor")
        self.c = lax.rem(self.s, 2)
        self.p = lax.div(self.s, 2)
        self.h = lax.div(self.p, self.Z)
        self.z = lax.rem(self.p, self.Z)
        self.chips = n_seq // 2

    def seq(self, h, z, c):
        return (h * self.Z + z) * 2 + c

    def sibling(self):
        return self.seq(self.h, self.z, 1 - self.c)

    def chip(self, k):
        return lax.rem(self.p + k + self.chips, self.chips) * 2 + self.c

    def other_h(self, d):
        return lax.rem(self.h + d, self.H)

    def other_z(self, d):
        return lax.rem(self.z + d + self.Z, self.Z)

    def other_t(self, d):
        return lax.rem(self.t + d + self.n_ten, self.n_ten)

    def next(self, d):
        return lax.rem(self.s + d + self.n_seq, self.n_seq)


class Chain:
    def __init__(self, me, sign, at, relay, ss, rr, rs, rx):
        self.me, self.sign, self.at, self.relay, self.ss, self.rr, self.rs, self.rx = me, sign, at, relay, ss, rr, rs, rx
        self.edge, self.turn = (me.Z - 1, 0) if sign > 0 else (0, me.Z - 1)
        row = me.other_h(sign + me.H)
        if RELAY == 1:
            self.at_relay = me.z == self.turn
            self.via = me.seq(me.h, self.turn, me.c)
        else:
            self.at_relay = me.z == self.edge
            self.via = me.seq(row, self.edge, me.c)
        self.goal = me.seq(row if RELAY == 1 else me.h, self.turn, me.c)

    def copy(self, k, half):
        nxt = self.me.chip(self.sign)
        return send(
            self.at(k - 1, half), self.at(k, half), self.ss.at[half, k - 1], self.rr.at[half, k - 1], nxt, self.me.t
        )

    def push(self, k):
        self.copy(k, 0).start()

        @pl.when(self.me.z != self.edge)
        def _():
            self.copy(k, 1).start()

        @pl.when(self.me.z == self.edge)
        def _():
            send(
                self.at(k - 1, 1), self.relay.at[k - 1], self.ss.at[1, k - 1], self.rx.at[k - 1], self.via, self.me.t
            ).start()

    def on(self, k):
        return send(
            self.relay.at[k - 1], self.at(k, 1), self.rs.at[k - 1], self.rr.at[1, k - 1], self.goal, self.me.t
        )

    def take(self, k):
        @pl.when(self.at_relay)
        def _():
            send(
                self.relay.at[k - 1], self.relay.at[k - 1], self.rs.at[k - 1], self.rx.at[k - 1], self.via, self.me.t
            ).wait_recv()
            self.on(k).start()

        for half in (0, 1):
            self.copy(k, half).wait_recv()
        if k < 3:
            self.push(k + 1)

    def finish(self):
        for k in (1, 2, 3):
            for half in (0, 1):
                self.copy(k, half).wait_send()

        @pl.when(self.at_relay)
        def _():
            for k in (1, 2, 3):
                self.on(k).wait_send()


def fused_kernel(
    n_seq, n_ten, delays, text_len, w_in, t_in, s_in, emb, gain, cot, out, de, sgo,
    pay, tmp,
    g, f, cots, rimbuf, blk, longer, nst, normed, states32, states,
    tkv, kx, qx, k_relay, q_relay, wbuf, wtbuf, mixbuf, totbuf, st, cstat,
    att, dq, dk, dv, tkg, tvg,
    opt, opx, opr, ipt, ipx, ipr, ops, ips, nst_out, nsx, nss, nsr,
    sga, sgza, sgb, sgzb, sgh, sghr, sgs, sgx, fg, rim,
    lsem, one_s, one_r, h_s, h_r, z_s, z_r, f_s, f_r, x_s, x_r,
    k_s, k_r, k_rs, k_rx, q_s, q_r, q_rs, q_rx, t_s, t_r, ox_s, ox_r, ix_s, ix_r, o_s, o_r, i_s, i_r, n_s, n_r,
    za_s, za_r, zb_s, zb_r, hh_s, hh_r,
):
    me = Place(n_seq, n_ten)
    H, Z, T = me.H, me.Z, n_ten
    s, t, c, h, z, p = me.s, me.t, me.c, me.h, me.z, me.p
    sib = me.sibling()
    half = Z // 2
    width = emb.shape[2]
    Q = emb.shape[1]
    B = 2 * Q
    R = sga.shape[3]
    text = states.shape[0]
    full = width * T
    scale = HD ** (-0.5)
    zero = jnp.zeros((), BF)
    right, left = me.seq(h, me.other_z(1), c), me.seq(h, me.other_z(-1), c)
    partners = [(sib, t), (me.next(1), t), (me.next(-1), t)]
    partners += [(me.seq(me.other_h(d), z, c), t) for d in range(1, H)]
    partners += [(me.seq(h, me.other_z(d), c), t) for d in range(1, Z)]
    partners += [(s, me.other_t(d)) for d in range(1, T)]
    partners += [(me.chip(k), t) for k in (1, -1, 2, -2, 3, -3)]
    greet(partners)
    outgoing = []

    def go(copy):
        copy.start()
        outgoing.append(copy)

    def half_rows(core):
        return pl.ds(pl.multiple_of(core * Q, Q), Q)

    per = text // n_seq
    given = t_in[0].shape[0]
    tmp[...] = jnp.zeros_like(tmp)
    for i in range(2):
        tmp[i, 0:given, :] = t_in[i][...].astype(F32)
        for e in range(2):
            tmp[i, 12:16, e * 128 : (e + 1) * 128] = s_in[e * 8 + i * 4 : e * 8 + i * 4 + 4, :]
    for e in range(2):
        lanes = slice(e * 128, (e + 1) * 128)
        for i in range(4):
            pay[e, i * R : (i + 1) * R, :] = w_in[i][:, lanes]
        for i in range(2):
            pay[e, 4 * R + 16 * i : 4 * R + 16 * (i + 1), :] = tmp[i, :, lanes].astype(BF)
    go(send(pay.at[1 - c], g.at[p, c], one_s.at[0], one_r.at[0], sib, t))
    mine = pltpu.make_async_copy(pay.at[c], g.at[p, c], lsem.at[0])
    mine.start()
    longer[...] = jnp.zeros_like(longer)
    for d in range(4):
        book = jnp.zeros((Q, width), F32)
        for k in range(4):
            book = book + jnp.where(delays[k] == d, emb[k].astype(F32), 0.0)
        longer[d : d + Q, :] = longer[d : d + Q, :] + book
    go(send(longer.at[pl.ds(Q, 16)], rimbuf, one_s.at[1], one_r.at[1], me.next(1), t))
    mine.wait()
    send(pay.at[c], g.at[p, 1 - c], one_s.at[0], one_r.at[0], sib, t).wait_recv()
    for d in range(1, H):
        go(send(g.at[p], g.at[p], h_s.at[d], h_r.at[d], me.seq(me.other_h(d), z, c), t))

    def step(way, k, d):
        hh = me.other_h(d)
        zz = me.other_z(-(k - 1) if way == 0 else k - 1)
        go(send(g.at[hh * Z + zz], g.at[hh * Z + zz], z_s.at[way, k, d], z_r.at[way, k, d], right if way == 0 else left, t))

    def arrived(way, k, d):
        hh = me.other_h(d)
        zz = me.other_z(-k if way == 0 else k)
        send(g.at[hh * Z + zz], g.at[hh * Z + zz], z_s.at[way, k, d], z_r.at[way, k, d], right, t).wait_recv()

    def used(way, k, d):
        if k < half:
            return True
        if k > half:
            return False
        return (d < H // 2) if way == 0 else (d >= H // 2)

    for way in (0, 1):
        if used(way, 1, 0):
            step(way, 1, 0)
    send(longer.at[pl.ds(Q, 16)], rimbuf, one_s.at[1], one_r.at[1], me.next(1), t).wait_recv()
    blk[...] = longer[0:Q, :].astype(BF)
    blk[0:16, :] = (longer[0:16, :] + jnp.where(s > 0, rimbuf[...], 0.0)).astype(BF)
    for d in range(1, T):
        go(send(blk, f.at[c, t], f_s.at[d], f_r.at[d], s, me.other_t(d)))
    go(send(blk, f.at[c, t], x_s.at[0], x_r.at[0], sib, t))
    own = pltpu.make_async_copy(blk, f.at[c, t], lsem.at[1])
    own.start()
    for d in range(1, H):
        hh = me.other_h(H - d)
        send(g.at[hh * Z + z], g.at[hh * Z + z], h_s.at[d], h_r.at[d], sib, t).wait_recv()
        for way in (0, 1):
            if used(way, 1, H - d):
                step(way, 1, H - d)
    go(send(cot, cots.at[half_rows(c)], one_s.at[2], one_r.at[2], sib, t))
    mycot = pltpu.make_async_copy(cot, cots.at[half_rows(c)], lsem.at[2])
    mycot.start()
    order = [0] + [H - e for e in range(1, H)]
    ring_last = half

    def ring(k):
        for d in order:
            for way in (0, 1):
                if used(way, k, d):
                    arrived(way, k, d)
                    if used(way, k + 1, d):
                        step(way, k + 1, d)

    def pass_frames():
        for d in range(1, T):
            tt = me.other_t(-d)
            send(blk, f.at[c, tt], f_s.at[d], f_r.at[d], sib, t).wait_recv()
            go(send(f.at[c, tt], f.at[c, tt], x_s.at[d], x_r.at[d], sib, t))

    def norm(cc):
        def fold(v):
            return v[:, 0:128] + v[:, 128:256]

        acc = jnp.zeros((Q, 128), F32)
        acc = lax.fori_loop(0, T, lambda i, a: a + fold(f[cc, i].astype(F32)), acc)
        mean = jnp.sum(acc, 1, keepdims=True) / full

        def second(i, a):
            v = f[cc, i].astype(F32) - mean
            return a + fold(v * v)

        acc = lax.fori_loop(0, T, second, jnp.zeros((Q, 128), F32))
        inv = lax.rsqrt(jnp.sum(acc, 1, keepdims=True) / full + EPS)
        lane128 = lax.broadcasted_iota(jnp.int32, (Q, 128), 1)
        nst[cc] = jnp.where(lane128 == 0, mean, inv)

        def third(i, carry):
            w = pl.ds(pl.multiple_of(i * width, width), width)
            v = (f[cc, i].astype(F32) - mean) * inv
            normed[half_rows(cc), w] = (v * gain[0:1, w]).astype(BF)
            return carry

        lax.fori_loop(0, T, third, 0)

    for k in range(1, half):
        if k == max(half - 2, 1):
            pass_frames()
        ring(k)
    if half == 1:
        pass_frames()
    own.wait()
    norm(c)
    for d in range(T):
        tt = me.other_t(-d)
        send(blk, f.at[1 - c, tt], x_s.at[d], x_r.at[d], sib, t).wait_recv()
    norm(1 - c)
    ring(half)

    def weight(i):
        return g[:, :, i * R : (i + 1) * R, :].reshape(n_seq * R, 128)

    def project(src, i, dst, first, lanes):
        def go_rows(rb, carry):
            rows = pl.ds(pl.multiple_of(first + rb * Q, Q), Q)
            dst[rows, lanes] = nn(src[half_rows(rb), :], weight(i)).astype(BF)
            return carry

        lax.fori_loop(0, 2, go_rows, 0)

    lo, hi = slice(0, 128), slice(128, 256)
    keys = Chain(
        me, 1, lambda k, e: kx.at[pl.ds((3 - k) * B + e * Q, Q)], k_relay, k_s, k_r, k_rs, k_rx
    )
    queries = Chain(me, -1, lambda k, e: qx.at[pl.ds(k * B + e * Q, Q)], q_relay, q_s, q_r, q_rs, q_rx)
    kv = kx.at[pl.ds(3 * B, B)]
    qd = qx.at[pl.ds(0, B)]
    project(normed, 1, kx, 3 * B, lo)
    project(normed, 2, kx, 3 * B, hi)
    keys.push(1)
    project(normed, 0, qx, 0, lo)
    mycot.wait()
    send(cot, cots.at[half_rows(c)], one_s.at[2], one_r.at[2], sib, t).wait_recv()
    project(cots, 3, qx, 0, hi)
    queries.push(1)

    lane = lax.broadcasted_iota(jnp.int32, (Q, 128), 1)
    row = lax.broadcasted_iota(jnp.int32, (Q, Q), 0)
    col = lax.broadcasted_iota(jnp.int32, (Q, Q), 1)
    heads = [lane < HD, lane >= HD]
    chunks = (WINDOW + Q - 2) // Q + 1
    lead = (chunks - 1) * Q

    def forward_chunk(qb, hd, q, j):
        base = pl.multiple_of((qb + j) * Q, Q)
        w = jnp.exp(nt(q, kx[pl.ds(base, Q), lo]))
        ok = p * B - 3 * B + (qb + j) * Q >= 0
        if lead - j * Q + Q - 1 >= WINDOW:
            ok = ok & (lead + row - j * Q - col < WINDOW)
        if j == chunks - 1:
            ok = ok & (col <= row)
        w = jnp.where(ok, w, 0.0)
        wbuf[qb, hd, j] = w
        return w[:, 0:128] + w[:, 128:256], nn(w.astype(BF), kx[pl.ds(base, Q), hi])

    def forward(k):
        for qb in range(2):
            q_both = qd[qb * Q : (qb + 1) * Q, lo]
            for hd in range(2):
                q = jnp.where(heads[hd], q_both, zero) * jnp.asarray(scale, BF)
                if k == 0:
                    total, mix = jnp.zeros((Q, 128), F32), jnp.zeros((Q, 128), F32)
                else:
                    total, mix = totbuf[qb, hd], mixbuf[qb, hd]
                if k == 4:
                    wt = jnp.where(live, jnp.exp(nt(q, tkv[:, lo])), 0.0)
                    wtbuf[qb, hd] = wt
                    total, mix = total + wt, mix + nn(wt.astype(BF), tkv[:, hi])
                for j in range(chunks):
                    if (qb + j) // 2 == 3 - k:
                        a, b = forward_chunk(qb, hd, q, j)
                        total, mix = total + a, mix + b
                totbuf[qb, hd], mixbuf[qb, hd] = total, mix

    states32[...] = g[:, :, 4 * R : 4 * R + 32, :].reshape(n_seq, 32, 128).astype(F32)
    lanes_of = 8 // (per // 2)
    for e in range(8):
        at = 12 + e if e < 4 else 24 + e
        first = pl.multiple_of((c * (per // 2) + e // lanes_of) * n_seq, n_seq)
        x = (e % lanes_of) * 128
        states[pl.ds(first, n_seq), x : x + 128] = states32[:, at, :].astype(BF)
    my_states = states.at[pl.ds(pl.multiple_of(c * (text // 2), text // 2), text // 2)]
    go(send(my_states, my_states, one_s.at[5], one_r.at[5], sib, t))
    forward(0)
    send(my_states, my_states, one_s.at[5], one_r.at[5], sib, t).wait_recv()
    for i in range(2):
        w = g[:, :, 4 * R + 16 * i : 4 * R + 16 * (i + 1), :].reshape(n_seq * 16, 128)
        tkv[:, i * 128 : (i + 1) * 128] = nn(states[...], w).astype(BF)
    token = lax.broadcasted_iota(jnp.int32, (1, text), 1)
    live = lax.rem(token, n_seq) * per + lax.div(token, n_seq) < text_len[0]

    forward(4)
    for k in (1, 2, 3):
        keys.take(k)
        queries.take(k)
        forward(k)
    for qb in range(2):
        rows = slice(qb * Q, (qb + 1) * Q)
        d_both = qd[rows, hi].astype(F32)
        parts, stats = [], []
        for hd in range(2):
            total = jnp.sum(totbuf[qb, hd], 1, keepdims=True)
            a_head = (mixbuf[qb, hd] / total).astype(BF)
            parts.append(a_head)
            inner = jnp.sum(jnp.where(heads[hd], d_both * a_head.astype(F32), 0.0), 1, keepdims=True)
            stats.append((1.0 / total, inner))
        att[rows, :] = jnp.where(heads[0], parts[0], parts[1])
        (r0, i0), (r1, i1) = stats
        packed = jnp.where(lane == 0, r0, jnp.where(lane == 1, r1, jnp.where(lane == 2, i0, i1)))
        cstat[rows, :] = packed
        st[0, :, rows] = packed.T[0:8, :]
    for k in (1, 2, 3):
        go(send(st.at[0], st.at[k], t_s.at[k], t_r.at[k], me.chip(-k), t))

    def w_block(i, tt):
        n = width // (2 * R)
        return g[pl.ds(tt * n, n), :, i * R : (i + 1) * R, :].reshape(width, 128)

    for d in range(T):
        tt = me.other_t(d)
        opt[d] = nt(att[half_rows(1 - c), :], w_block(3, tt)).astype(BF)
        go(send(opt.at[d], opx.at[d], ox_s.at[d], ox_r.at[d], sib, t))
    for e in range(full // B):
        piece = tn(att[...], cots[:, e * B : (e + 1) * B])
        n = B // R
        for a in range(B // 128):
            rows = piece[:, a * 128 : (a + 1) * 128].T.astype(BF).reshape(128 // R, R, 128)
            for b in range(128 // R):
                who = e * n + a * (128 // R) + b
                hh, zz, cc = who // (2 * Z), (who // 2) % Z, who % 2
                sga[zz, hh, cc] = rows[b]
    for d in range(1, Z):
        zz = me.other_z(d)
        go(send(sga.at[zz], sgza.at[d], za_s.at[d], za_r.at[d], me.seq(h, zz, c), t))

    tkg[...] = jnp.zeros_like(tkg)
    tvg[...] = jnp.zeros_like(tvg)

    def query_grads(qb, carry):
        rows = half_rows(qb)
        q_both = qd[rows, lo]
        d_both = qd[rows, hi]
        parts = []
        for hd in range(2):
            q = jnp.where(heads[hd], q_both, zero)
            d = jnp.where(heads[hd], d_both, zero)
            r = cstat[rows, hd : hd + 1]
            inner = cstat[rows, 2 + hd : 3 + hd]
            sh = wtbuf[qb, hd] * r
            ds = (sh * (nt(d, tkv[:, hi]) - inner)).astype(BF)
            grad = nn(ds, tkv[:, lo])
            tkg[...] += tn(ds, q) * scale
            tvg[...] += tn(sh.astype(BF), d)
            for j in range(chunks):
                base = pl.multiple_of((qb + j) * Q, Q)
                around = kx[pl.ds(base, Q), :]
                ds = (wbuf[qb, hd, j] * r * (nt(d, around[:, hi]) - inner)).astype(BF)
                grad = grad + nn(ds, around[:, lo])
            parts.append(grad)
        dq[rows, :] = (jnp.where(heads[0], parts[0], parts[1]) * scale).astype(BF)
        return carry

    lax.fori_loop(0, 2, query_grads, 0)
    for i, grad in enumerate((tkg, tvg)):
        piece = tn(states[...], grad[...].astype(BF)).astype(BF).reshape(H, Z, 2, 16, 128)
        for zz in range(Z):
            sgb[zz, :, :, 16 * i : 16 * (i + 1), :] = piece[:, zz]
    for d in range(1, Z):
        zz = me.other_z(d)
        go(send(sgb.at[zz], sgzb.at[d], zb_s.at[d], zb_r.at[d], me.seq(h, zz, c), t))
    for d in [*range(1, T), 0]:
        tt = me.other_t(d)
        send(opt.at[d], opx.at[d], ox_s.at[d], ox_r.at[d], sib, t).wait_recv()
        ops[d] = (nt(att[half_rows(c), :], w_block(3, tt)) + opx[d].astype(F32)).astype(BF)
        if d:
            go(send(ops.at[d], opr.at[d], o_s.at[d], o_r.at[d], s, tt))
    for k in (1, 2, 3):
        send(st.at[0], st.at[k], t_s.at[k], t_r.at[k], me.chip(-k), t).wait_recv()

    def key_grads(kb, carry):
        rows = half_rows(kb)
        k_both = kv[rows, lo]
        v_both = kv[rows, hi]
        kparts, vparts = [], []
        for hd in range(2):
            kh = jnp.where(heads[hd], k_both, zero) * jnp.asarray(scale, BF)
            vh = jnp.where(heads[hd], v_both, zero)
            gk = jnp.zeros((Q, 128), F32)
            gv = jnp.zeros((Q, 128), F32)
            for i in range(chunks):
                base = pl.multiple_of((kb + i) * Q, Q)
                qs = qx[pl.ds(base, Q), :]
                at = lax.div(kb + i, 2)
                part = pl.ds(pl.multiple_of(lax.rem(kb + i, 2) * Q, Q), Q)
                r = st[at, hd : hd + 1, part]
                inner = st[at, 2 + hd : 3 + hd, part]
                ok = p * B + (kb + i) * Q < n_seq * Q
                if i == 0:
                    ok = ok & (col >= row)
                if i * Q + Q - 1 >= WINDOW:
                    ok = ok & (i * Q + col - row < WINDOW)
                sh = jnp.where(ok, jnp.exp(nt(kh, qs[:, lo])) * r, 0.0)
                ds = (sh * (nt(vh, qs[:, hi]) - inner)).astype(BF)
                gv = gv + nn(sh.astype(BF), qs[:, hi])
                gk = gk + nn(ds, qs[:, lo])
            kparts.append(gk)
            vparts.append(gv)
        dk[rows, :] = (jnp.where(heads[0], kparts[0], kparts[1]) * scale).astype(BF)
        dv[rows, :] = jnp.where(heads[0], vparts[0], vparts[1]).astype(BF)
        return carry

    key_grads(1 - c, 0)

    def input_block(cc, tt):
        rows = half_rows(cc)
        grad = nt(dq[rows, :], w_block(0, tt)) + nt(dk[rows, :], w_block(1, tt)) + nt(dv[rows, :], w_block(2, tt))
        lanes = pl.ds(pl.multiple_of(tt * width, width), width)
        scaled = grad * gain[0:1, lanes]
        unit = (f[cc, tt].astype(F32) - nst[cc, :, 0:1]) * nst[cc, :, 1:2]
        both = scaled * unit
        return grad, scaled[:, 0:128] + scaled[:, 128:256], both[:, 0:128] + both[:, 128:256]

    def pack_sums(plain, unit):
        plain = jnp.sum(plain, 1, keepdims=True)
        unit = jnp.sum(unit, 1, keepdims=True)
        return jnp.where(lane == 0, plain, unit).T[0:8, :]

    plain = jnp.zeros((Q, 128), F32)
    unit = jnp.zeros((Q, 128), F32)
    for d in [*range(1, T), 0]:
        tt = me.other_t(d)
        grad, a, b = input_block(1 - c, tt)
        plain, unit = plain + a, unit + b
        ipt[d] = grad.astype(BF)
        go(send(ipt.at[d], ipx.at[d], ix_s.at[d], ix_r.at[d], sib, t))
    nst_out[...] = pack_sums(plain, unit)
    go(send(nst_out, nsx, n_s.at[0], n_r.at[0], sib, t))
    key_grads(c, 0)
    plain = jnp.zeros((Q, 128), F32)
    unit = jnp.zeros((Q, 128), F32)
    for d in [*range(1, T), 0]:
        tt = me.other_t(d)
        grad, a, b = input_block(c, tt)
        plain, unit = plain + a, unit + b
        send(ipt.at[d], ipx.at[d], ix_s.at[d], ix_r.at[d], sib, t).wait_recv()
        ips[d] = (grad + ipx[d].astype(F32)).astype(BF)
        if d:
            go(send(ips.at[d], ipr.at[d], i_s.at[d], i_r.at[d], s, tt))
    send(nst_out, nsx, n_s.at[0], n_r.at[0], sib, t).wait_recv()
    nss[...] = pack_sums(plain, unit) + nsx[...]
    for d in range(1, T):
        go(send(nss, nsr.at[d], n_s.at[d], n_r.at[d], s, me.other_t(d)))

    acc_a = sga[z].astype(F32)
    acc_b = sgb[z].astype(F32)
    for d in range(1, Z):
        send(sga.at[0], sgza.at[d], za_s.at[d], za_r.at[d], sib, t).wait_recv()
        send(sgb.at[0], sgzb.at[d], zb_s.at[d], zb_r.at[d], sib, t).wait_recv()
        acc_a = acc_a + sgza[d].astype(F32)
        acc_b = acc_b + sgzb[d].astype(F32)
    sgh[:, :, 0:R, :] = acc_a
    sgh[:, :, R : R + 32, :] = acc_b
    for d in range(1, H):
        hh = me.other_h(d)
        go(send(sgh.at[hh], sghr.at[d], hh_s.at[d], hh_r.at[d], me.seq(hh, z, c), t))

    total = ips[0].astype(F32)
    sums = nss[...]
    for d in range(1, T):
        send(nss, nsr.at[d], n_s.at[d], n_r.at[d], sib, t).wait_recv()
        sums = sums + nsr[d]
        send(ips.at[d], ipr.at[d], i_s.at[d], i_r.at[d], sib, t).wait_recv()
        total = total + ipr[d].astype(F32)
    tall = jnp.concatenate([sums] * 16, 0).T
    here = pl.ds(pl.multiple_of(t * width, width), width)
    inv = nst[c, :, 1:2]
    unit = (f[c, t].astype(F32) - nst[c, :, 0:1]) * inv
    grad = inv * (total * gain[0:1, here] - tall[:, 0:1] / full - unit * (tall[:, 1:2] / full))
    fg[...] = grad.astype(BF)
    go(send(fg.at[pl.ds(0, 16)], rim, one_s.at[3], one_r.at[3], me.next(-1), t))
    acc = sgh[h]
    for d in range(1, H):
        send(sgh.at[0], sghr.at[d], hh_s.at[d], hh_r.at[d], sib, t).wait_recv()
        acc = acc + sghr[d]
    sgs[...] = acc
    go(send(sgs.at[1 - c], sgx, one_s.at[4], one_r.at[4], sib, t))
    longer[0:Q, :] = fg[...].astype(F32)
    total = ops[0].astype(F32)
    for d in range(1, T):
        send(ops.at[d], opr.at[d], o_s.at[d], o_r.at[d], sib, t).wait_recv()
        total = total + opr[d].astype(F32)
    out[...] = total.astype(BF)
    send(fg.at[pl.ds(0, 16)], rim, one_s.at[3], one_r.at[3], sib, t).wait_recv()
    send(sgs.at[0], sgx, one_s.at[4], one_r.at[4], sib, t).wait_recv()
    sgo[:, lo] = jnp.where(c == 0, sgs[c], sgx[...])
    sgo[:, hi] = jnp.where(c == 0, sgx[...], sgs[c])
    for copy in outgoing:
        copy.wait_send()
    for chain in (keys, queries):
        chain.finish()
    longer[Q : Q + 16, :] = jnp.where(s < n_seq - 1, rim[...].astype(F32), 0.0)
    later = [longer[d : d + Q, :] for d in range(4)]
    for k in range(4):
        book = later[0]
        for d in range(1, 4):
            book = jnp.where(delays[k] == d, later[d], book)
        de[k] = book.astype(BF)


def fused(n_seq, n_ten, delays, text_len, weights, text_weights, states, emb, gain, cot, text):
    H, Z = dims_of(n_seq)
    T = n_ten
    _, Q, W = emb.shape
    B = 2 * Q
    full = W * T
    R = weights[0].shape[0]
    pay_shape = (2, 4 * R + 32, 128)
    chunks = (WINDOW + Q - 2) // Q + 1
    dma = pltpu.SemaphoreType.DMA
    vm = pl.BlockSpec(memory_space=pltpu.VMEM)
    sm = pl.BlockSpec(memory_space=pltpu.SMEM)
    V = pltpu.VMEM
    block = V((T, Q, W), BF)
    rows = V((B, 128), BF)
    small = V((text, 128), F32)
    sums = V((8, Q), F32)

    def pair(*shape):
        return [dma(shape), dma(shape)]

    return pl.pallas_call(
        lambda a, b, *refs: fused_kernel(n_seq, n_ten, a, b, refs[0:4], refs[4:6], *refs[6:]),
        out_shape=(
            jax.ShapeDtypeStruct((Q, W), BF),
            jax.ShapeDtypeStruct((4, Q, W), BF),
            jax.ShapeDtypeStruct((R + 32, 256), F32),
        ),
        in_specs=[sm, sm] + [vm] * 9 + [pl.BlockSpec(memory_space=pl.ANY)],
        out_specs=(vm,) * 3,
        scratch_shapes=[
            V(pay_shape, BF), V((2, 16, 256), F32), V((H * Z,) + pay_shape, BF), V((2, T, Q, W), BF), V((B, full), BF), V((16, W), F32), V((Q, W), BF),
            V((Q + 16, W), F32), V((2, Q, 128), F32), V((B, full), BF), V((n_seq, 32, 128), F32),
            V((text, n_seq * 16), BF),
            V((text, 256), BF), V((4 * B, 256), BF), V((4 * B, 256), BF), V((3, Q, 256), BF), V((3, Q, 256), BF),
            V((2, 2, chunks, Q, Q), F32), V((2, 2, Q, text), F32), V((2, 2, Q, 128), F32), V((2, 2, Q, 128), F32),
            V((4, 8, B), F32), V((B, 128), F32),
            rows, rows, rows, rows, small, small,
            block, block, block, block, block, block, block, block, sums, sums, sums, V((T, 8, Q), F32),
            V((Z, H, 2, R, 128), BF), V((Z, H, 2, R, 128), BF), V((Z, H, 2, 32, 128), BF), V((Z, H, 2, 32, 128), BF),
            V((H, 2, R + 32, 128), F32), V((H, 2, R + 32, 128), F32), V((2, R + 32, 128), F32), V((R + 32, 128), F32),
            V((Q, W), BF), V((16, W), BF),
            dma((3,)), *pair(6), *pair(H), *pair(2, Z // 2 + 1, H), *pair(T), *pair(T),
            *pair(2, 3), *pair(3), *pair(2, 3), *pair(3), *pair(4), *pair(T), *pair(T), *pair(T), *pair(T), *pair(T),
            *pair(Z), *pair(Z), *pair(H),
        ],
        compiler_params=pltpu.CompilerParams(collective_id=0, has_side_effects=True, vmem_limit_bytes=56 << 20),
    )(delays, text_len, *weights, *text_weights, states, emb, gain, cot)


def shards(
    n_seq, n_ten, embedded, delays, norm_gain, w_query, w_key, w_value, w_out,
    text_states, w_text_key, w_text_value, text_len, cotangent,
):
    R = w_query.shape[0]
    tr = w_text_key.shape[0]
    per = text_states.shape[0]
    states = jnp.pad(text_states.reshape(per, n_seq, tr), ((0, 0), (0, 0), (0, 16 - tr))).reshape(16, 128)
    out, de, sgo = fused(
        n_seq, n_ten, delays, text_len, (w_query, w_key, w_value, w_out.T), (w_text_key, w_text_value),
        states.astype(F32), embedded.transpose(1, 0, 2), norm_gain.reshape(1, -1), cotangent, per * n_seq,
    )
    return (out, de.transpose(1, 0, 2), sgo[:R].T, sgo[R : R + tr], sgo[R + 16 : R + 16 + tr])


def solution(mesh):
    placed = (
        P("seq", None, "tensor"), P(), P(),
        P("seq", "tensor"), P("seq", "tensor"), P("seq", "tensor"), P("tensor", "seq"),
        P("seq", None), P("seq", "tensor"), P("seq", "tensor"), P(), P("seq", None),
    )
    return jax.shard_map(
        functools.partial(shards, mesh.shape["seq"], mesh.shape["tensor"]),
        mesh=mesh,
        in_specs=placed,
        out_specs=(
            P("seq", "tensor"), P("seq", None, "tensor"), P("tensor", "seq"),
            P("seq", "tensor"), P("seq", "tensor"),
        ),
        check_vma=False,
    )
```

```python
import functools

import jax
import jax.numpy as jnp
from jax import lax
from jax.experimental import pallas as pl
from jax.experimental.pallas import tpu as pltpu
from jax.sharding import PartitionSpec as P

HD = 64
WINDOW = 1500
EPS = 1e-05
RING = 8
RELAY = 1
MESH = pl.DeviceIdType.MESH
BF = jnp.bfloat16
F32 = jnp.float32


def dims_of(n_seq):
    z = min(RING, n_seq // 2)
    return n_seq // (2 * z), z


def nt(a, b):
    return lax.dot_general(a, b, (((1,), (1,)), ((), ())), preferred_element_type=F32)


def nn(a, b):
    return lax.dot_general(a, b, (((1,), (0,)), ((), ())), preferred_element_type=F32)


def tn(a, b):
    return lax.dot_general(a, b, (((0,), (0,)), ((), ())), preferred_element_type=F32)


def send(src, dst, ssem, rsem, seq, ten):
    return pltpu.make_async_remote_copy(
        src_ref=src, dst_ref=dst, send_sem=ssem, recv_sem=rsem, device_id=(seq, ten), device_id_type=MESH
    )


def greet(partners):
    sem = pltpu.get_barrier_semaphore()
    for seq, ten in partners:
        pl.semaphore_signal(sem, inc=1, device_id=(seq, ten), device_id_type=MESH)
    return lambda: pl.semaphore_wait(sem, len(partners))


class Place:
    def __init__(self, n_seq, n_ten):
        self.n_seq, self.n_ten = n_seq, n_ten
        self.H, self.Z = dims_of(n_seq)
        self.s = lax.axis_index("seq")
        self.t = lax.axis_index("tensor")
        self.c = lax.rem(self.s, 2)
        self.p = lax.div(self.s, 2)
        self.h = lax.div(self.p, self.Z)
        self.z = lax.rem(self.p, self.Z)
        self.chips = n_seq // 2

    def seq(self, h, z, c):
        return (h * self.Z + z) * 2 + c

    def sibling(self):
        return self.seq(self.h, self.z, 1 - self.c)

    def chip(self, k):
        return lax.rem(self.p + k + self.chips, self.chips) * 2 + self.c

    def other_h(self, d):
        return lax.rem(self.h + d, self.H)

    def other_z(self, d):
        return lax.rem(self.z + d + self.Z, self.Z)

    def other_t(self, d):
        return lax.rem(self.t + d + self.n_ten, self.n_ten)

    def next(self, d):
        return lax.rem(self.s + d + self.n_seq, self.n_seq)


class Chain:
    def __init__(self, me, sign, at, relay, ss, rr, rs, rx):
        self.me, self.sign, self.at, self.relay, self.ss, self.rr, self.rs, self.rx = me, sign, at, relay, ss, rr, rs, rx
        self.edge, self.turn = (me.Z - 1, 0) if sign > 0 else (0, me.Z - 1)
        row = me.other_h(sign + me.H)
        if RELAY == 1:
            self.at_relay = me.z == self.turn
            self.via = me.seq(me.h, self.turn, me.c)
        else:
            self.at_relay = me.z == self.edge
            self.via = me.seq(row, self.edge, me.c)
        self.goal = me.seq(row if RELAY == 1 else me.h, self.turn, me.c)

    def copy(self, k, half):
        nxt = self.me.chip(self.sign)
        return send(
            self.at(k - 1, half), self.at(k, half), self.ss.at[half, k - 1], self.rr.at[half, k - 1], nxt, self.me.t
        )

    def push(self, k, half):
        if half == 0:
            self.copy(k, 0).start()
            return

        @pl.when(self.me.z != self.edge)
        def _():
            self.copy(k, 1).start()

        @pl.when(self.me.z == self.edge)
        def _():
            send(
                self.at(k - 1, 1), self.relay.at[k - 1], self.ss.at[1, k - 1], self.rx.at[k - 1], self.via, self.me.t
            ).start()

    def on(self, k):
        return send(
            self.relay.at[k - 1], self.at(k, 1), self.rs.at[k - 1], self.rr.at[1, k - 1], self.goal, self.me.t
        )

    def take(self, k, half):
        if half == 1:

            @pl.when(self.at_relay)
            def _():
                send(
                    self.relay.at[k - 1], self.relay.at[k - 1], self.rs.at[k - 1], self.rx.at[k - 1], self.via, self.me.t
                ).wait_recv()
                self.on(k).start()

        self.copy(k, half).wait_recv()
        if k < 3:
            self.push(k + 1, half)

    def finish(self):
        for k in (1, 2, 3):
            for half in (0, 1):
                self.copy(k, half).wait_send()

        @pl.when(self.at_relay)
        def _():
            for k in (1, 2, 3):
                self.on(k).wait_send()


def fused_kernel(
    n_seq, n_ten, delays, text_len, w_in, t_in, s_in, emb, gain, cot, out, de, sgo,
    pay, tmp, wide,
    g, f, cots, rimbuf, blk, longer, nst, normed, states32, states,
    tkv, kx, qx, k_relay, q_relay, wbuf, wtbuf, mixbuf, totbuf, st, cstat,
    att, dq, dk, dv, tkg, tvg,
    opt, opx, opr, ipt, ipx, ipr, ops, ips, nst_out, nsx, nss, nsr,
    sga, sgza, sgb, sgzb, sgh, sghr, sgs, sgx, fg, rim,
    lsem, one_s, one_r, h_s, h_r, z_s, z_r, f_s, f_r, x_s, x_r,
    k_s, k_r, k_rs, k_rx, q_s, q_r, q_rs, q_rx, t_s, t_r, ox_s, ox_r, ix_s, ix_r, o_s, o_r, i_s, i_r, n_s, n_r,
    za_s, za_r, zb_s, zb_r, hh_s, hh_r,
):
    me = Place(n_seq, n_ten)
    H, Z, T = me.H, me.Z, n_ten
    s, t, c, h, z, p = me.s, me.t, me.c, me.h, me.z, me.p
    sib = me.sibling()
    half = Z // 2
    width = emb.shape[2]
    Q = emb.shape[0]
    B = 2 * Q
    R = sga.shape[3]
    text = states.shape[0]
    full = width * T
    scale = HD ** (-0.5)
    zero = jnp.zeros((), BF)
    right, left = me.seq(h, me.other_z(1), c), me.seq(h, me.other_z(-1), c)
    partners = [(sib, t), (me.next(1), t), (me.next(-1), t)]
    partners += [(me.seq(me.other_h(d), z, c), t) for d in range(1, H)]
    partners += [(me.seq(h, me.other_z(d), c), t) for d in range(1, Z)]
    partners += [(s, me.other_t(d)) for d in range(1, T)]
    partners += [(me.chip(k), t) for k in (1, -1, 2, -2, 3, -3)]
    all_here = greet(partners)
    outgoing = []

    def go(copy):
        copy.start()
        outgoing.append(copy)

    def half_rows(core):
        return pl.ds(pl.multiple_of(core * Q, Q), Q)

    per = text // n_seq
    given = t_in[0].shape[0]
    tmp[...] = jnp.zeros_like(tmp)
    ours = s_in[...].astype(F32)
    for i in range(2):
        tmp[i, 0:given, :] = t_in[i][...].astype(F32)
        for e in range(2):
            tmp[i, 12:16, e * 128 : (e + 1) * 128] = ours[e * 8 + i * 4 : e * 8 + i * 4 + 4, :]
    for e in range(2):
        lanes = slice(e * 128, (e + 1) * 128)
        for i in range(4):
            pay[e, i * R : (i + 1) * R, :] = w_in[i][:, lanes]
        for i in range(2):
            pay[e, 4 * R + 16 * i : 4 * R + 16 * (i + 1), :] = tmp[i, :, lanes].astype(BF)
    all_here()
    go(send(pay.at[1 - c], g.at[p, c], one_s.at[0], one_r.at[0], sib, t))
    mine = pltpu.make_async_copy(pay.at[c], g.at[p, c], lsem.at[0])
    mine.start()
    mine.wait()
    send(pay.at[c], g.at[p, 1 - c], one_s.at[0], one_r.at[0], sib, t).wait_recv()
    for d in range(1, H):
        go(send(g.at[p], g.at[p], h_s.at[d], h_r.at[d], me.seq(me.other_h(d), z, c), t))

    def step(way, k, d):
        hh = me.other_h(d)
        zz = me.other_z(-(k - 1) if way == 0 else k - 1)
        go(send(g.at[hh * Z + zz], g.at[hh * Z + zz], z_s.at[way, k, d], z_r.at[way, k, d], right if way == 0 else left, t))

    def arrived(way, k, d):
        hh = me.other_h(d)
        zz = me.other_z(-k if way == 0 else k)
        send(g.at[hh * Z + zz], g.at[hh * Z + zz], z_s.at[way, k, d], z_r.at[way, k, d], right, t).wait_recv()

    def used(way, k, d):
        if k < half:
            return True
        if k > half:
            return False
        return (d < H // 2) if way == 0 else (d >= H // 2)

    for way in (0, 1):
        if used(way, 1, 0):
            step(way, 1, 0)
    wide[...] = emb[...].astype(F32)
    longer[...] = jnp.zeros_like(longer)
    for d in range(4):
        book = jnp.zeros((Q, width), F32)
        for k in range(4):
            book = book + jnp.where(delays[k] == d, wide[:, k, :], 0.0)
        longer[d : d + Q, :] = longer[d : d + Q, :] + book
    go(send(longer.at[pl.ds(Q, 16)], rimbuf, one_s.at[1], one_r.at[1], me.next(1), t))
    for d in range(1, H):
        hh = me.other_h(H - d)
        send(g.at[hh * Z + z], g.at[hh * Z + z], h_s.at[d], h_r.at[d], sib, t).wait_recv()
        for way in (0, 1):
            if used(way, 1, H - d):
                step(way, 1, H - d)
    send(longer.at[pl.ds(Q, 16)], rimbuf, one_s.at[1], one_r.at[1], me.next(1), t).wait_recv()
    blk[...] = longer[0:Q, :].astype(BF)
    blk[0:16, :] = (longer[0:16, :] + jnp.where(s > 0, rimbuf[...], 0.0)).astype(BF)
    for d in range(1, T):
        go(send(blk, f.at[c, t], f_s.at[d], f_r.at[d], s, me.other_t(d)))
    go(send(blk, f.at[c, t], x_s.at[0], x_r.at[0], sib, t))
    own = pltpu.make_async_copy(blk, f.at[c, t], lsem.at[1])
    own.start()
    go(send(cot, cots.at[half_rows(c)], one_s.at[2], one_r.at[2], sib, t))
    mycot = pltpu.make_async_copy(cot, cots.at[half_rows(c)], lsem.at[2])
    mycot.start()
    order = [0] + [H - e for e in range(1, H)]
    ring_last = half

    def ring(k):
        for d in order:
            for way in (0, 1):
                if used(way, k, d):
                    arrived(way, k, d)
                    if used(way, k + 1, d):
                        step(way, k + 1, d)

    def pass_frames():
        for d in range(1, T):
            tt = me.other_t(-d)
            send(blk, f.at[c, tt], f_s.at[d], f_r.at[d], sib, t).wait_recv()
            go(send(f.at[c, tt], f.at[c, tt], x_s.at[d], x_r.at[d], sib, t))

    def norm(cc):
        def fold(v):
            return v[:, 0:128] + v[:, 128:256]

        acc = jnp.zeros((Q, 128), F32)
        acc = lax.fori_loop(0, T, lambda i, a: a + fold(f[cc, i].astype(F32)), acc)
        mean = jnp.sum(acc, 1, keepdims=True) / full

        def second(i, a):
            v = f[cc, i].astype(F32) - mean
            return a + fold(v * v)

        acc = lax.fori_loop(0, T, second, jnp.zeros((Q, 128), F32))
        inv = lax.rsqrt(jnp.sum(acc, 1, keepdims=True) / full + EPS)
        lane128 = lax.broadcasted_iota(jnp.int32, (Q, 128), 1)
        nst[cc] = jnp.where(lane128 == 0, mean, inv)

        def third(i, carry):
            w = pl.ds(pl.multiple_of(i * width, width), width)
            v = (f[cc, i].astype(F32) - mean) * inv
            normed[half_rows(cc), w] = (v * gain[0:1, w]).astype(BF)
            return carry

        lax.fori_loop(0, T, third, 0)

    for k in range(1, half):
        if k == max(half - 2, 1):
            pass_frames()
        ring(k)
    if half == 1:
        pass_frames()
    own.wait()
    norm(c)
    for d in range(T):
        tt = me.other_t(-d)
        send(blk, f.at[1 - c, tt], x_s.at[d], x_r.at[d], sib, t).wait_recv()
    norm(1 - c)
    ring(half)

    def weight(i):
        return g[:, :, i * R : (i + 1) * R, :].reshape(n_seq * R, 128)

    def project(src, i, dst, first, lanes):
        def go_rows(rb, carry):
            rows = pl.ds(pl.multiple_of(first + rb * Q, Q), Q)
            dst[rows, lanes] = nn(src[half_rows(rb), :], weight(i)).astype(BF)
            return carry

        lax.fori_loop(0, 2, go_rows, 0)

    lo, hi = slice(0, 128), slice(128, 256)
    keys = Chain(
        me, 1, lambda k, e: kx.at[pl.ds((3 - k) * B + e * Q, Q)], k_relay, k_s, k_r, k_rs, k_rx
    )
    queries = Chain(me, -1, lambda k, e: qx.at[pl.ds(k * B + e * Q, Q)], q_relay, q_s, q_r, q_rs, q_rx)
    kv = kx.at[pl.ds(3 * B, B)]
    qd = qx.at[pl.ds(0, B)]
    project(normed, 1, kx, 3 * B, lo)
    project(normed, 2, kx, 3 * B, hi)
    keys.push(1, 1)
    keys.push(1, 0)
    project(normed, 0, qx, 0, lo)
    mycot.wait()
    send(cot, cots.at[half_rows(c)], one_s.at[2], one_r.at[2], sib, t).wait_recv()
    project(cots, 3, qx, 0, hi)
    queries.push(1, 1)
    queries.push(1, 0)

    lane = lax.broadcasted_iota(jnp.int32, (Q, 128), 1)
    row = lax.broadcasted_iota(jnp.int32, (Q, Q), 0)
    col = lax.broadcasted_iota(jnp.int32, (Q, Q), 1)
    heads = [lane < HD, lane >= HD]
    chunks = (WINDOW + Q - 2) // Q + 1
    lead = (chunks - 1) * Q

    def forward_chunk(qb, hd, q, j):
        base = pl.multiple_of((qb + j) * Q, Q)
        w = jnp.exp(nt(q, kx[pl.ds(base, Q), lo]))
        ok = p * B - 3 * B + (qb + j) * Q >= 0
        if lead - j * Q + Q - 1 >= WINDOW:
            ok = ok & (lead + row - j * Q - col < WINDOW)
        if j == chunks - 1:
            ok = ok & (col <= row)
        w = jnp.where(ok, w, 0.0)
        wbuf[qb, hd, j] = w
        return w[:, 0:128] + w[:, 128:256], nn(w.astype(BF), kx[pl.ds(base, Q), hi])

    def forward(k):
        for qb in range(2):
            q_both = qd[qb * Q : (qb + 1) * Q, lo]
            for hd in range(2):
                q = jnp.where(heads[hd], q_both, zero) * jnp.asarray(scale, BF)
                if k == 0:
                    total, mix = jnp.zeros((Q, 128), F32), jnp.zeros((Q, 128), F32)
                else:
                    total, mix = totbuf[qb, hd], mixbuf[qb, hd]
                if k == 4:
                    wt = jnp.where(live, jnp.exp(nt(q, tkv[:, lo])), 0.0)
                    wtbuf[qb, hd] = wt
                    total, mix = total + wt, mix + nn(wt.astype(BF), tkv[:, hi])
                for j in range(chunks):
                    if (qb + j) // 2 == 3 - k:
                        a, b = forward_chunk(qb, hd, q, j)
                        total, mix = total + a, mix + b
                totbuf[qb, hd], mixbuf[qb, hd] = total, mix

    states32[...] = g[:, :, 4 * R : 4 * R + 32, :].reshape(n_seq, 32, 128).astype(F32)
    lanes_of = 8 // (per // 2)
    for e in range(8):
        at = 12 + e if e < 4 else 24 + e
        first = pl.multiple_of((c * (per // 2) + e // lanes_of) * n_seq, n_seq)
        x = (e % lanes_of) * 128
        states[pl.ds(first, n_seq), x : x + 128] = states32[:, at, :].astype(BF)
    my_states = states.at[pl.ds(pl.multiple_of(c * (text // 2), text // 2), text // 2)]
    go(send(my_states, my_states, one_s.at[5], one_r.at[5], sib, t))
    forward(0)
    send(my_states, my_states, one_s.at[5], one_r.at[5], sib, t).wait_recv()
    for i in range(2):
        w = g[:, :, 4 * R + 16 * i : 4 * R + 16 * (i + 1), :].reshape(n_seq * 16, 128)
        tkv[:, i * 128 : (i + 1) * 128] = nn(states[...], w).astype(BF)
    token = lax.broadcasted_iota(jnp.int32, (1, text), 1)
    live = lax.rem(token, n_seq) * per + lax.div(token, n_seq) < text_len[0]

    forward(4)
    for k in (1, 2, 3):
        for e in (1, 0):
            keys.take(k, e)
            queries.take(k, e)
        forward(k)
    for qb in range(2):
        rows = slice(qb * Q, (qb + 1) * Q)
        d_both = qd[rows, hi].astype(F32)
        parts, stats = [], []
        for hd in range(2):
            total = jnp.sum(totbuf[qb, hd], 1, keepdims=True)
            a_head = (mixbuf[qb, hd] / total).astype(BF)
            parts.append(a_head)
            inner = jnp.sum(jnp.where(heads[hd], d_both * a_head.astype(F32), 0.0), 1, keepdims=True)
            stats.append((1.0 / total, inner))
        att[rows, :] = jnp.where(heads[0], parts[0], parts[1])
        (r0, i0), (r1, i1) = stats
        packed = jnp.where(lane == 0, r0, jnp.where(lane == 1, r1, jnp.where(lane == 2, i0, i1)))
        cstat[rows, :] = packed
        st[0, :, rows] = packed.T[0:8, :]
    for k in (1, 2, 3):
        go(send(st.at[0], st.at[k], t_s.at[k], t_r.at[k], me.chip(-k), t))

    def w_block(i, tt):
        n = width // (2 * R)
        return g[pl.ds(tt * n, n), :, i * R : (i + 1) * R, :].reshape(width, 128)

    for d in range(T):
        tt = me.other_t(d)
        opt[d] = nt(att[half_rows(1 - c), :], w_block(3, tt)).astype(BF)
        go(send(opt.at[d], opx.at[d], ox_s.at[d], ox_r.at[d], sib, t))
    for e in range(full // B):
        piece = tn(att[...], cots[:, e * B : (e + 1) * B])
        n = B // R
        for a in range(B // 128):
            rows = piece[:, a * 128 : (a + 1) * 128].T.astype(BF).reshape(128 // R, R, 128)
            for b in range(128 // R):
                who = e * n + a * (128 // R) + b
                hh, zz, cc = who // (2 * Z), (who // 2) % Z, who % 2
                sga[zz, hh, cc] = rows[b]
    for d in range(1, Z):
        zz = me.other_z(d)
        go(send(sga.at[zz], sgza.at[d], za_s.at[d], za_r.at[d], me.seq(h, zz, c), t))

    tkg[...] = jnp.zeros_like(tkg)
    tvg[...] = jnp.zeros_like(tvg)

    def query_grads(qb, carry):
        rows = half_rows(qb)
        q_both = qd[rows, lo]
        d_both = qd[rows, hi]
        parts = []
        for hd in range(2):
            q = jnp.where(heads[hd], q_both, zero)
            d = jnp.where(heads[hd], d_both, zero)
            r = cstat[rows, hd : hd + 1]
            inner = cstat[rows, 2 + hd : 3 + hd]
            sh = wtbuf[qb, hd] * r
            ds = (sh * (nt(d, tkv[:, hi]) - inner)).astype(BF)
            grad = nn(ds, tkv[:, lo])
            tkg[...] += tn(ds, q) * scale
            tvg[...] += tn(sh.astype(BF), d)
            for j in range(chunks):
                base = pl.multiple_of((qb + j) * Q, Q)
                around = kx[pl.ds(base, Q), :]
                ds = (wbuf[qb, hd, j] * r * (nt(d, around[:, hi]) - inner)).astype(BF)
                grad = grad + nn(ds, around[:, lo])
            parts.append(grad)
        dq[rows, :] = (jnp.where(heads[0], parts[0], parts[1]) * scale).astype(BF)
        return carry

    lax.fori_loop(0, 2, query_grads, 0)
    for i, grad in enumerate((tkg, tvg)):
        piece = tn(states[...], grad[...].astype(BF)).astype(BF).reshape(H, Z, 2, 16, 128)
        for zz in range(Z):
            sgb[zz, :, :, 16 * i : 16 * (i + 1), :] = piece[:, zz]
    for d in range(1, Z):
        zz = me.other_z(d)
        go(send(sgb.at[zz], sgzb.at[d], zb_s.at[d], zb_r.at[d], me.seq(h, zz, c), t))
    for d in [*range(1, T), 0]:
        tt = me.other_t(d)
        send(opt.at[d], opx.at[d], ox_s.at[d], ox_r.at[d], sib, t).wait_recv()
        ops[d] = (nt(att[half_rows(c), :], w_block(3, tt)) + opx[d].astype(F32)).astype(BF)
        if d:
            go(send(ops.at[d], opr.at[d], o_s.at[d], o_r.at[d], s, tt))
    for k in (1, 2, 3):
        send(st.at[0], st.at[k], t_s.at[k], t_r.at[k], me.chip(-k), t).wait_recv()

    def key_grads(kb, carry):
        rows = half_rows(kb)
        k_both = kv[rows, lo]
        v_both = kv[rows, hi]
        kparts, vparts = [], []
        for hd in range(2):
            kh = jnp.where(heads[hd], k_both, zero) * jnp.asarray(scale, BF)
            vh = jnp.where(heads[hd], v_both, zero)
            gk = jnp.zeros((Q, 128), F32)
            gv = jnp.zeros((Q, 128), F32)
            for i in range(chunks):
                base = pl.multiple_of((kb + i) * Q, Q)
                qs = qx[pl.ds(base, Q), :]
                at = lax.div(kb + i, 2)
                part = pl.ds(pl.multiple_of(lax.rem(kb + i, 2) * Q, Q), Q)
                r = st[at, hd : hd + 1, part]
                inner = st[at, 2 + hd : 3 + hd, part]
                ok = p * B + (kb + i) * Q < n_seq * Q
                if i == 0:
                    ok = ok & (col >= row)
                if i * Q + Q - 1 >= WINDOW:
                    ok = ok & (i * Q + col - row < WINDOW)
                sh = jnp.where(ok, jnp.exp(nt(kh, qs[:, lo])) * r, 0.0)
                ds = (sh * (nt(vh, qs[:, hi]) - inner)).astype(BF)
                gv = gv + nn(sh.astype(BF), qs[:, hi])
                gk = gk + nn(ds, qs[:, lo])
            kparts.append(gk)
            vparts.append(gv)
        dk[rows, :] = (jnp.where(heads[0], kparts[0], kparts[1]) * scale).astype(BF)
        dv[rows, :] = jnp.where(heads[0], vparts[0], vparts[1]).astype(BF)
        return carry

    key_grads(1 - c, 0)

    def input_block(cc, tt):
        rows = half_rows(cc)
        grad = nt(dq[rows, :], w_block(0, tt)) + nt(dk[rows, :], w_block(1, tt)) + nt(dv[rows, :], w_block(2, tt))
        lanes = pl.ds(pl.multiple_of(tt * width, width), width)
        scaled = grad * gain[0:1, lanes]
        unit = (f[cc, tt].astype(F32) - nst[cc, :, 0:1]) * nst[cc, :, 1:2]
        both = scaled * unit
        return grad, scaled[:, 0:128] + scaled[:, 128:256], both[:, 0:128] + both[:, 128:256]

    def pack_sums(plain, unit):
        plain = jnp.sum(plain, 1, keepdims=True)
        unit = jnp.sum(unit, 1, keepdims=True)
        return jnp.where(lane == 0, plain, unit).T[0:8, :]

    plain = jnp.zeros((Q, 128), F32)
    unit = jnp.zeros((Q, 128), F32)
    for d in [*range(1, T), 0]:
        tt = me.other_t(d)
        grad, a, b = input_block(1 - c, tt)
        plain, unit = plain + a, unit + b
        ipt[d] = grad.astype(BF)
        go(send(ipt.at[d], ipx.at[d], ix_s.at[d], ix_r.at[d], sib, t))
    nst_out[...] = pack_sums(plain, unit)
    go(send(nst_out, nsx, n_s.at[0], n_r.at[0], sib, t))
    key_grads(c, 0)
    plain = jnp.zeros((Q, 128), F32)
    unit = jnp.zeros((Q, 128), F32)
    for d in [*range(1, T), 0]:
        tt = me.other_t(d)
        grad, a, b = input_block(c, tt)
        plain, unit = plain + a, unit + b
        send(ipt.at[d], ipx.at[d], ix_s.at[d], ix_r.at[d], sib, t).wait_recv()
        ips[d] = (grad + ipx[d].astype(F32)).astype(BF)
        if d:
            go(send(ips.at[d], ipr.at[d], i_s.at[d], i_r.at[d], s, tt))
    send(nst_out, nsx, n_s.at[0], n_r.at[0], sib, t).wait_recv()
    nss[...] = pack_sums(plain, unit) + nsx[...]
    for d in range(1, T):
        go(send(nss, nsr.at[d], n_s.at[d], n_r.at[d], s, me.other_t(d)))

    acc_a = sga[z].astype(F32)
    acc_b = sgb[z].astype(F32)
    for d in range(1, Z):
        send(sga.at[0], sgza.at[d], za_s.at[d], za_r.at[d], sib, t).wait_recv()
        send(sgb.at[0], sgzb.at[d], zb_s.at[d], zb_r.at[d], sib, t).wait_recv()
        acc_a = acc_a + sgza[d].astype(F32)
        acc_b = acc_b + sgzb[d].astype(F32)
    sgh[:, :, 0:R, :] = acc_a
    sgh[:, :, R : R + 32, :] = acc_b
    for d in range(1, H):
        hh = me.other_h(d)
        go(send(sgh.at[hh], sghr.at[d], hh_s.at[d], hh_r.at[d], me.seq(hh, z, c), t))

    total = ips[0].astype(F32)
    sums = nss[...]
    for d in range(1, T):
        send(nss, nsr.at[d], n_s.at[d], n_r.at[d], sib, t).wait_recv()
        sums = sums + nsr[d]
        send(ips.at[d], ipr.at[d], i_s.at[d], i_r.at[d], sib, t).wait_recv()
        total = total + ipr[d].astype(F32)
    tall = jnp.concatenate([sums] * 16, 0).T
    here = pl.ds(pl.multiple_of(t * width, width), width)
    inv = nst[c, :, 1:2]
    unit = (f[c, t].astype(F32) - nst[c, :, 0:1]) * inv
    grad = inv * (total * gain[0:1, here] - tall[:, 0:1] / full - unit * (tall[:, 1:2] / full))
    fg[...] = grad.astype(BF)
    go(send(fg.at[pl.ds(0, 16)], rim, one_s.at[3], one_r.at[3], me.next(-1), t))
    acc = sgh[h]
    for d in range(1, H):
        send(sgh.at[0], sghr.at[d], hh_s.at[d], hh_r.at[d], sib, t).wait_recv()
        acc = acc + sghr[d]
    sgs[...] = acc
    go(send(sgs.at[1 - c], sgx, one_s.at[4], one_r.at[4], sib, t))
    longer[0:Q, :] = fg[...].astype(F32)
    total = ops[0].astype(F32)
    for d in range(1, T):
        send(ops.at[d], opr.at[d], o_s.at[d], o_r.at[d], sib, t).wait_recv()
        total = total + opr[d].astype(F32)
    out[...] = total.astype(BF)
    send(fg.at[pl.ds(0, 16)], rim, one_s.at[3], one_r.at[3], sib, t).wait_recv()
    send(sgs.at[0], sgx, one_s.at[4], one_r.at[4], sib, t).wait_recv()
    sgo[:, lo] = jnp.where(c == 0, sgs[c], sgx[...])
    sgo[:, hi] = jnp.where(c == 0, sgx[...], sgs[c])
    for copy in outgoing:
        copy.wait_send()
    for chain in (keys, queries):
        chain.finish()
    longer[Q : Q + 16, :] = jnp.where(s < n_seq - 1, rim[...].astype(F32), 0.0)
    later = [longer[d : d + Q, :] for d in range(4)]
    for k in range(4):
        book = later[0]
        for d in range(1, 4):
            book = jnp.where(delays[k] == d, later[d], book)
        wide[:, k, :] = book
    de[...] = wide[...].astype(BF)


def fused(n_seq, n_ten, delays, text_len, weights, text_weights, states, emb, gain, cot, text):
    H, Z = dims_of(n_seq)
    T = n_ten
    Q, _, W = emb.shape
    B = 2 * Q
    full = W * T
    R = weights[0].shape[0]
    pay_shape = (2, 4 * R + 32, 128)
    chunks = (WINDOW + Q - 2) // Q + 1
    dma = pltpu.SemaphoreType.DMA
    vm = pl.BlockSpec(memory_space=pltpu.VMEM)
    sm = pl.BlockSpec(memory_space=pltpu.SMEM)
    V = pltpu.VMEM
    block = V((T, Q, W), BF)
    rows = V((B, 128), BF)
    small = V((text, 128), F32)
    sums = V((8, Q), F32)

    def pair(*shape):
        return [dma(shape), dma(shape)]

    return pl.pallas_call(
        lambda a, b, *refs: fused_kernel(n_seq, n_ten, a, b, refs[0:4], refs[4:6], *refs[6:]),
        out_shape=(
            jax.ShapeDtypeStruct((Q, W), BF),
            jax.ShapeDtypeStruct((Q, 4, W), BF),
            jax.ShapeDtypeStruct((R + 32, 256), F32),
        ),
        in_specs=[sm, sm] + [vm] * 9 + [pl.BlockSpec(memory_space=pl.ANY)],
        out_specs=(vm,) * 3,
        scratch_shapes=[
            V(pay_shape, BF), V((2, 16, 256), F32), V((Q, 4, W), F32), V((H * Z,) + pay_shape, BF), V((2, T, Q, W), BF), V((B, full), BF), V((16, W), F32), V((Q, W), BF),
            V((Q + 16, W), F32), V((2, Q, 128), F32), V((B, full), BF), V((n_seq, 32, 128), F32),
            V((text, n_seq * 16), BF),
            V((text, 256), BF), V((4 * B, 256), BF), V((4 * B, 256), BF), V((3, Q, 256), BF), V((3, Q, 256), BF),
            V((2, 2, chunks, Q, Q), F32), V((2, 2, Q, text), F32), V((2, 2, Q, 128), F32), V((2, 2, Q, 128), F32),
            V((4, 8, B), F32), V((B, 128), F32),
            rows, rows, rows, rows, small, small,
            block, block, block, block, block, block, block, block, sums, sums, sums, V((T, 8, Q), F32),
            V((Z, H, 2, R, 128), BF), V((Z, H, 2, R, 128), BF), V((Z, H, 2, 32, 128), BF), V((Z, H, 2, 32, 128), BF),
            V((H, 2, R + 32, 128), F32), V((H, 2, R + 32, 128), F32), V((2, R + 32, 128), F32), V((R + 32, 128), F32),
            V((Q, W), BF), V((16, W), BF),
            dma((3,)), *pair(6), *pair(H), *pair(2, Z // 2 + 1, H), *pair(T), *pair(T),
            *pair(2, 3), *pair(3), *pair(2, 3), *pair(3), *pair(4), *pair(T), *pair(T), *pair(T), *pair(T), *pair(T),
            *pair(Z), *pair(Z), *pair(H),
        ],
        compiler_params=pltpu.CompilerParams(collective_id=0, has_side_effects=True, vmem_limit_bytes=56 << 20),
    )(delays, text_len, *weights, *text_weights, states, emb, gain, cot)


def shards(
    n_seq, n_ten, embedded, delays, norm_gain, w_query, w_key, w_value, w_out,
    text_states, w_text_key, w_text_value, text_len, cotangent,
):
    R = w_query.shape[0]
    tr = w_text_key.shape[0]
    per = text_states.shape[0]
    states = jnp.pad(text_states.reshape(per, n_seq, tr), ((0, 0), (0, 0), (0, 16 - tr))).reshape(16, 128)
    out, de, sgo = fused(
        n_seq, n_ten, delays, text_len, (w_query, w_key, w_value, w_out.T), (w_text_key, w_text_value),
        states, embedded, norm_gain.reshape(1, -1), cotangent, per * n_seq,
    )
    return (out, de, sgo[:R].T, sgo[R : R + tr], sgo[R + 16 : R + 16 + tr])


def solution(mesh):
    placed = (
        P("seq", None, "tensor"), P(), P(),
        P("seq", "tensor"), P("seq", "tensor"), P("seq", "tensor"), P("tensor", "seq"),
        P("seq", None), P("seq", "tensor"), P("seq", "tensor"), P(), P("seq", None),
    )
    return jax.shard_map(
        functools.partial(shards, mesh.shape["seq"], mesh.shape["tensor"]),
        mesh=mesh,
        in_specs=placed,
        out_specs=(
            P("seq", "tensor"), P("seq", None, "tensor"), P("tensor", "seq"),
            P("seq", "tensor"), P("seq", "tensor"),
        ),
        check_vma=False,
    )
```

```python
import functools

import jax
import jax.numpy as jnp
from jax import lax
from jax.experimental import pallas as pl
from jax.experimental.pallas import tpu as pltpu
from jax.sharding import PartitionSpec as P

HD = 64
WINDOW = 1500
EPS = 1e-05
RING = 8
RELAY = 1
MESH = pl.DeviceIdType.MESH
BF = jnp.bfloat16
F32 = jnp.float32


def dims_of(n_seq):
    z = min(RING, n_seq // 2)
    return n_seq // (2 * z), z


def nt(a, b):
    return lax.dot_general(a, b, (((1,), (1,)), ((), ())), preferred_element_type=F32)


def nn(a, b):
    return lax.dot_general(a, b, (((1,), (0,)), ((), ())), preferred_element_type=F32)


def tn(a, b):
    return lax.dot_general(a, b, (((0,), (0,)), ((), ())), preferred_element_type=F32)


def send(src, dst, ssem, rsem, seq, ten):
    return pltpu.make_async_remote_copy(
        src_ref=src, dst_ref=dst, send_sem=ssem, recv_sem=rsem, device_id=(seq, ten), device_id_type=MESH
    )


def greet(partners):
    sem = pltpu.get_barrier_semaphore()
    for seq, ten in partners:
        pl.semaphore_signal(sem, inc=1, device_id=(seq, ten), device_id_type=MESH)
    pl.semaphore_wait(sem, len(partners))


class Place:
    def __init__(self, n_seq, n_ten):
        self.n_seq, self.n_ten = n_seq, n_ten
        self.H, self.Z = dims_of(n_seq)
        self.s = lax.axis_index("seq")
        self.t = lax.axis_index("tensor")
        self.c = lax.rem(self.s, 2)
        self.p = lax.div(self.s, 2)
        self.h = lax.div(self.p, self.Z)
        self.z = lax.rem(self.p, self.Z)
        self.chips = n_seq // 2

    def seq(self, h, z, c):
        return (h * self.Z + z) * 2 + c

    def sibling(self):
        return self.seq(self.h, self.z, 1 - self.c)

    def chip(self, k):
        return lax.rem(self.p + k + self.chips, self.chips) * 2 + self.c

    def other_h(self, d):
        return lax.rem(self.h + d, self.H)

    def other_z(self, d):
        return lax.rem(self.z + d + self.Z, self.Z)

    def other_t(self, d):
        return lax.rem(self.t + d + self.n_ten, self.n_ten)

    def next(self, d):
        return lax.rem(self.s + d + self.n_seq, self.n_seq)


class Chain:
    def __init__(self, me, sign, at, relay, ss, rr, rs, rx):
        self.me, self.sign, self.at, self.relay, self.ss, self.rr, self.rs, self.rx = me, sign, at, relay, ss, rr, rs, rx
        self.edge, self.turn = (me.Z - 1, 0) if sign > 0 else (0, me.Z - 1)
        row = me.other_h(sign + me.H)
        if RELAY == 1:
            self.at_relay = me.z == self.turn
            self.via = me.seq(me.h, self.turn, me.c)
        else:
            self.at_relay = me.z == self.edge
            self.via = me.seq(row, self.edge, me.c)
        self.goal = me.seq(row if RELAY == 1 else me.h, self.turn, me.c)

    def copy(self, k, half):
        nxt = self.me.chip(self.sign)
        return send(
            self.at(k - 1, half), self.at(k, half), self.ss.at[half, k - 1], self.rr.at[half, k - 1], nxt, self.me.t
        )

    def push(self, k):
        self.copy(k, 0).start()

        @pl.when(self.me.z != self.edge)
        def _():
            self.copy(k, 1).start()

        @pl.when(self.me.z == self.edge)
        def _():
            send(
                self.at(k - 1, 1), self.relay.at[k - 1], self.ss.at[1, k - 1], self.rx.at[k - 1], self.via, self.me.t
            ).start()

    def on(self, k):
        return send(
            self.relay.at[k - 1], self.at(k, 1), self.rs.at[k - 1], self.rr.at[1, k - 1], self.goal, self.me.t
        )

    def take(self, k):
        @pl.when(self.at_relay)
        def _():
            send(
                self.relay.at[k - 1], self.relay.at[k - 1], self.rs.at[k - 1], self.rx.at[k - 1], self.via, self.me.t
            ).wait_recv()
            self.on(k).start()

        for half in (0, 1):
            self.copy(k, half).wait_recv()
        if k < 3:
            self.push(k + 1)

    def finish(self):
        for k in (1, 2, 3):
            for half in (0, 1):
                self.copy(k, half).wait_send()

        @pl.when(self.at_relay)
        def _():
            for k in (1, 2, 3):
                self.on(k).wait_send()


def fused_kernel(
    n_seq, n_ten, delays, text_len, w_in, t_in, s_in, emb, gain, cot, out, de, sgo,
    pay, tmp, sums_p, sums_u,
    g, f, cots, rimbuf, blk, longer, nst, normed, states32, states,
    tkv, kx, qx, k_relay, q_relay, wbuf, wtbuf, mixbuf, totbuf, st, cstat,
    att, dq, dk, dv, tkg, tvg,
    opt, opx, opr, ipt, ipx, ipr, ops, ips, nst_out, nsx, nss, nsr,
    sga, sgza, sgb, sgzb, sgh, sghr, sgs, sgx, fg, rim,
    lsem, one_s, one_r, h_s, h_r, z_s, z_r, f_s, f_r, x_s, x_r,
    k_s, k_r, k_rs, k_rx, q_s, q_r, q_rs, q_rx, t_s, t_r, ox_s, ox_r, ix_s, ix_r, o_s, o_r, i_s, i_r, n_s, n_r,
    za_s, za_r, zb_s, zb_r, hh_s, hh_r,
):
    me = Place(n_seq, n_ten)
    H, Z, T = me.H, me.Z, n_ten
    s, t, c, h, z, p = me.s, me.t, me.c, me.h, me.z, me.p
    sib = me.sibling()
    half = Z // 2
    width = emb.shape[2]
    Q = emb.shape[1]
    B = 2 * Q
    R = sga.shape[3]
    text = states.shape[0]
    full = width * T
    scale = HD ** (-0.5)
    zero = jnp.zeros((), BF)
    right, left = me.seq(h, me.other_z(1), c), me.seq(h, me.other_z(-1), c)
    partners = [(sib, t), (me.next(1), t), (me.next(-1), t)]
    partners += [(me.seq(me.other_h(d), z, c), t) for d in range(1, H)]
    partners += [(me.seq(h, me.other_z(d), c), t) for d in range(1, Z)]
    partners += [(s, me.other_t(d)) for d in range(1, T)]
    partners += [(me.chip(k), t) for k in (1, -1, 2, -2, 3, -3)]
    greet(partners)
    outgoing = []

    def go(copy):
        copy.start()
        outgoing.append(copy)

    def half_rows(core):
        return pl.ds(pl.multiple_of(core * Q, Q), Q)

    per = text // n_seq
    given = t_in[0].shape[0]
    tmp[...] = jnp.zeros_like(tmp)
    for i in range(2):
        tmp[i, 0:given, :] = t_in[i][...].astype(F32)
        for e in range(2):
            tmp[i, 12:16, e * 128 : (e + 1) * 128] = s_in[e * 8 + i * 4 : e * 8 + i * 4 + 4, :]
    for e in range(2):
        lanes = slice(e * 128, (e + 1) * 128)
        for i in range(4):
            pay[e, i * R : (i + 1) * R, :] = w_in[i][:, lanes]
        for i in range(2):
            pay[e, 4 * R + 16 * i : 4 * R + 16 * (i + 1), :] = tmp[i, :, lanes].astype(BF)
    go(send(pay.at[1 - c], g.at[p, c], one_s.at[0], one_r.at[0], sib, t))
    mine = pltpu.make_async_copy(pay.at[c], g.at[p, c], lsem.at[0])
    mine.start()
    longer[...] = jnp.zeros_like(longer)
    for d in range(4):
        book = jnp.zeros((Q, width), F32)
        for k in range(4):
            book = book + jnp.where(delays[k] == d, emb[k].astype(F32), 0.0)
        longer[d : d + Q, :] = longer[d : d + Q, :] + book
    go(send(longer.at[pl.ds(Q, 16)], rimbuf, one_s.at[1], one_r.at[1], me.next(1), t))
    mine.wait()
    send(pay.at[c], g.at[p, 1 - c], one_s.at[0], one_r.at[0], sib, t).wait_recv()
    for d in range(1, H):
        go(send(g.at[p], g.at[p], h_s.at[d], h_r.at[d], me.seq(me.other_h(d), z, c), t))

    def step(way, k, d):
        hh = me.other_h(d)
        zz = me.other_z(-(k - 1) if way == 0 else k - 1)
        go(send(g.at[hh * Z + zz], g.at[hh * Z + zz], z_s.at[way, k, d], z_r.at[way, k, d], right if way == 0 else left, t))

    def arrived(way, k, d):
        hh = me.other_h(d)
        zz = me.other_z(-k if way == 0 else k)
        send(g.at[hh * Z + zz], g.at[hh * Z + zz], z_s.at[way, k, d], z_r.at[way, k, d], right, t).wait_recv()

    def used(way, k, d):
        if k < half:
            return True
        if k > half:
            return False
        return (d < H // 2) if way == 0 else (d >= H // 2)

    for way in (0, 1):
        if used(way, 1, 0):
            step(way, 1, 0)
    send(longer.at[pl.ds(Q, 16)], rimbuf, one_s.at[1], one_r.at[1], me.next(1), t).wait_recv()
    blk[...] = longer[0:Q, :].astype(BF)
    blk[0:16, :] = (longer[0:16, :] + jnp.where(s > 0, rimbuf[...], 0.0)).astype(BF)
    for d in range(1, T):
        go(send(blk, f.at[c, t], f_s.at[d], f_r.at[d], s, me.other_t(d)))
    go(send(blk, f.at[c, t], x_s.at[0], x_r.at[0], sib, t))
    own = pltpu.make_async_copy(blk, f.at[c, t], lsem.at[1])
    own.start()
    for d in range(1, H):
        hh = me.other_h(H - d)
        send(g.at[hh * Z + z], g.at[hh * Z + z], h_s.at[d], h_r.at[d], sib, t).wait_recv()
        for way in (0, 1):
            if used(way, 1, H - d):
                step(way, 1, H - d)
    go(send(cot, cots.at[half_rows(c)], one_s.at[2], one_r.at[2], sib, t))
    mycot = pltpu.make_async_copy(cot, cots.at[half_rows(c)], lsem.at[2])
    mycot.start()
    order = [0] + [H - e for e in range(1, H)]
    ring_last = half

    def ring(k):
        for d in order:
            for way in (0, 1):
                if used(way, k, d):
                    arrived(way, k, d)
                    if used(way, k + 1, d):
                        step(way, k + 1, d)

    def pass_frames():
        for d in range(1, T):
            tt = me.other_t(-d)
            send(blk, f.at[c, tt], f_s.at[d], f_r.at[d], sib, t).wait_recv()
            go(send(f.at[c, tt], f.at[c, tt], x_s.at[d], x_r.at[d], sib, t))

    def norm(cc):
        def fold(v):
            return v[:, 0:128] + v[:, 128:256]

        acc = jnp.zeros((Q, 128), F32)
        acc = lax.fori_loop(0, T, lambda i, a: a + fold(f[cc, i].astype(F32)), acc)
        mean = jnp.sum(acc, 1, keepdims=True) / full

        def second(i, a):
            v = f[cc, i].astype(F32) - mean
            return a + fold(v * v)

        acc = lax.fori_loop(0, T, second, jnp.zeros((Q, 128), F32))
        inv = lax.rsqrt(jnp.sum(acc, 1, keepdims=True) / full + EPS)
        lane128 = lax.broadcasted_iota(jnp.int32, (Q, 128), 1)
        nst[cc] = jnp.where(lane128 == 0, mean, inv)

        def third(i, carry):
            w = pl.ds(pl.multiple_of(i * width, width), width)
            v = (f[cc, i].astype(F32) - mean) * inv
            normed[half_rows(cc), w] = (v * gain[0:1, w]).astype(BF)
            return carry

        lax.fori_loop(0, T, third, 0)

    for k in range(1, half):
        if k == max(half - 2, 1):
            pass_frames()
        ring(k)
    if half == 1:
        pass_frames()
    own.wait()
    norm(c)
    for d in range(T):
        tt = me.other_t(-d)
        send(blk, f.at[1 - c, tt], x_s.at[d], x_r.at[d], sib, t).wait_recv()
    norm(1 - c)
    ring(half)

    def weight(i):
        return g[:, :, i * R : (i + 1) * R, :].reshape(n_seq * R, 128)

    def project(src, i, dst, first, lanes):
        def go_rows(rb, carry):
            rows = pl.ds(pl.multiple_of(first + rb * Q, Q), Q)
            dst[rows, lanes] = nn(src[half_rows(rb), :], weight(i)).astype(BF)
            return carry

        lax.fori_loop(0, 2, go_rows, 0)

    lo, hi = slice(0, 128), slice(128, 256)
    keys = Chain(
        me, 1, lambda k, e: kx.at[pl.ds((3 - k) * B + e * Q, Q)], k_relay, k_s, k_r, k_rs, k_rx
    )
    queries = Chain(me, -1, lambda k, e: qx.at[pl.ds(k * B + e * Q, Q)], q_relay, q_s, q_r, q_rs, q_rx)
    kv = kx.at[pl.ds(3 * B, B)]
    qd = qx.at[pl.ds(0, B)]
    project(normed, 1, kx, 3 * B, lo)
    project(normed, 2, kx, 3 * B, hi)
    keys.push(1)
    project(normed, 0, qx, 0, lo)
    mycot.wait()
    send(cot, cots.at[half_rows(c)], one_s.at[2], one_r.at[2], sib, t).wait_recv()
    project(cots, 3, qx, 0, hi)
    queries.push(1)

    lane = lax.broadcasted_iota(jnp.int32, (Q, 128), 1)
    row = lax.broadcasted_iota(jnp.int32, (Q, Q), 0)
    col = lax.broadcasted_iota(jnp.int32, (Q, Q), 1)
    heads = [lane < HD, lane >= HD]
    chunks = (WINDOW + Q - 2) // Q + 1
    lead = (chunks - 1) * Q

    def forward_chunk(qb, hd, q, j):
        base = pl.multiple_of((qb + j) * Q, Q)
        w = jnp.exp(nt(q, kx[pl.ds(base, Q), lo]))
        ok = p * B - 3 * B + (qb + j) * Q >= 0
        if lead - j * Q + Q - 1 >= WINDOW:
            ok = ok & (lead + row - j * Q - col < WINDOW)
        if j == chunks - 1:
            ok = ok & (col <= row)
        w = jnp.where(ok, w, 0.0)
        wbuf[qb, hd, j] = w
        return w[:, 0:128] + w[:, 128:256], nn(w.astype(BF), kx[pl.ds(base, Q), hi])

    def forward(k):
        for qb in range(2):
            q_both = qd[qb * Q : (qb + 1) * Q, lo]
            for hd in range(2):
                q = jnp.where(heads[hd], q_both, zero) * jnp.asarray(scale, BF)
                if k == 0:
                    total, mix = jnp.zeros((Q, 128), F32), jnp.zeros((Q, 128), F32)
                else:
                    total, mix = totbuf[qb, hd], mixbuf[qb, hd]
                if k == 4:
                    wt = jnp.where(live, jnp.exp(nt(q, tkv[:, lo])), 0.0)
                    wtbuf[qb, hd] = wt
                    total, mix = total + wt, mix + nn(wt.astype(BF), tkv[:, hi])
                for j in range(chunks):
                    if (qb + j) // 2 == 3 - k:
                        a, b = forward_chunk(qb, hd, q, j)
                        total, mix = total + a, mix + b
                totbuf[qb, hd], mixbuf[qb, hd] = total, mix

    states32[...] = g[:, :, 4 * R : 4 * R + 32, :].reshape(n_seq, 32, 128).astype(F32)
    lanes_of = 8 // (per // 2)
    for e in range(8):
        at = 12 + e if e < 4 else 24 + e
        first = pl.multiple_of((c * (per // 2) + e // lanes_of) * n_seq, n_seq)
        x = (e % lanes_of) * 128
        states[pl.ds(first, n_seq), x : x + 128] = states32[:, at, :].astype(BF)
    my_states = states.at[pl.ds(pl.multiple_of(c * (text // 2), text // 2), text // 2)]
    go(send(my_states, my_states, one_s.at[5], one_r.at[5], sib, t))
    forward(0)
    send(my_states, my_states, one_s.at[5], one_r.at[5], sib, t).wait_recv()
    for i in range(2):
        w = g[:, :, 4 * R + 16 * i : 4 * R + 16 * (i + 1), :].reshape(n_seq * 16, 128)
        tkv[:, i * 128 : (i + 1) * 128] = nn(states[...], w).astype(BF)
    token = lax.broadcasted_iota(jnp.int32, (1, text), 1)
    live = lax.rem(token, n_seq) * per + lax.div(token, n_seq) < text_len[0]

    forward(4)
    for k in (1, 2, 3):
        keys.take(k)
        queries.take(k)
        forward(k)
    for qb in range(2):
        rows = slice(qb * Q, (qb + 1) * Q)
        d_both = qd[rows, hi].astype(F32)
        parts, stats = [], []
        for hd in range(2):
            total = jnp.sum(totbuf[qb, hd], 1, keepdims=True)
            a_head = (mixbuf[qb, hd] / total).astype(BF)
            parts.append(a_head)
            inner = jnp.sum(jnp.where(heads[hd], d_both * a_head.astype(F32), 0.0), 1, keepdims=True)
            stats.append((1.0 / total, inner))
        att[rows, :] = jnp.where(heads[0], parts[0], parts[1])
        (r0, i0), (r1, i1) = stats
        packed = jnp.where(lane == 0, r0, jnp.where(lane == 1, r1, jnp.where(lane == 2, i0, i1)))
        cstat[rows, :] = packed
        st[0, :, rows] = packed.T[0:8, :]
    for k in (1, 2, 3):
        go(send(st.at[0], st.at[k], t_s.at[k], t_r.at[k], me.chip(-k), t))

    def w_block(i, tt):
        n = width // (2 * R)
        return g[pl.ds(tt * n, n), :, i * R : (i + 1) * R, :].reshape(width, 128)

    for d in range(T):
        tt = me.other_t(d)
        opt[d] = nt(att[half_rows(1 - c), :], w_block(3, tt)).astype(BF)
        go(send(opt.at[d], opx.at[d], ox_s.at[d], ox_r.at[d], sib, t))
    for e in range(full // B):
        piece = tn(att[...], cots[:, e * B : (e + 1) * B])
        n = B // R
        for a in range(B // 128):
            rows = piece[:, a * 128 : (a + 1) * 128].T.astype(BF).reshape(128 // R, R, 128)
            for b in range(128 // R):
                who = e * n + a * (128 // R) + b
                hh, zz, cc = who // (2 * Z), (who // 2) % Z, who % 2
                sga[zz, hh, cc] = rows[b]
    for d in range(1, Z):
        zz = me.other_z(d)
        go(send(sga.at[zz], sgza.at[d], za_s.at[d], za_r.at[d], me.seq(h, zz, c), t))

    tkg[...] = jnp.zeros_like(tkg)
    tvg[...] = jnp.zeros_like(tvg)

    def query_grads(qb, carry):
        rows = half_rows(qb)
        q_both = qd[rows, lo]
        d_both = qd[rows, hi]
        parts = []
        for hd in range(2):
            q = jnp.where(heads[hd], q_both, zero)
            d = jnp.where(heads[hd], d_both, zero)
            r = cstat[rows, hd : hd + 1]
            inner = cstat[rows, 2 + hd : 3 + hd]
            sh = wtbuf[qb, hd] * r
            ds = (sh * (nt(d, tkv[:, hi]) - inner)).astype(BF)
            grad = nn(ds, tkv[:, lo])
            tkg[...] += tn(ds, q) * scale
            tvg[...] += tn(sh.astype(BF), d)
            for j in range(chunks):
                base = pl.multiple_of((qb + j) * Q, Q)
                around = kx[pl.ds(base, Q), :]
                ds = (wbuf[qb, hd, j] * r * (nt(d, around[:, hi]) - inner)).astype(BF)
                grad = grad + nn(ds, around[:, lo])
            parts.append(grad)
        dq[rows, :] = (jnp.where(heads[0], parts[0], parts[1]) * scale).astype(BF)
        return carry

    lax.fori_loop(0, 2, query_grads, 0)
    for i, grad in enumerate((tkg, tvg)):
        piece = tn(states[...], grad[...].astype(BF)).astype(BF).reshape(H, Z, 2, 16, 128)
        for zz in range(Z):
            sgb[zz, :, :, 16 * i : 16 * (i + 1), :] = piece[:, zz]
    for d in range(1, Z):
        zz = me.other_z(d)
        go(send(sgb.at[zz], sgzb.at[d], zb_s.at[d], zb_r.at[d], me.seq(h, zz, c), t))
    for d in [*range(1, T), 0]:
        tt = me.other_t(d)
        send(opt.at[d], opx.at[d], ox_s.at[d], ox_r.at[d], sib, t).wait_recv()
        ops[d] = (nt(att[half_rows(c), :], w_block(3, tt)) + opx[d].astype(F32)).astype(BF)
        if d:
            go(send(ops.at[d], opr.at[d], o_s.at[d], o_r.at[d], s, tt))
    for k in (1, 2, 3):
        send(st.at[0], st.at[k], t_s.at[k], t_r.at[k], me.chip(-k), t).wait_recv()

    K = Q // 2

    def quarter(kb, e):
        return pl.ds(pl.multiple_of(kb * Q + e * K, K), K)

    krow = lax.broadcasted_iota(jnp.int32, (K, Q), 0)
    qcol = lax.broadcasted_iota(jnp.int32, (K, Q), 1)
    klane = lax.broadcasted_iota(jnp.int32, (K, 128), 1)
    kheads = [klane < HD, klane >= HD]

    def key_grads(kb, e):
        rows = quarter(kb, e)
        k_both = kv[rows, lo]
        v_both = kv[rows, hi]
        kparts, vparts = [], []
        for hd in range(2):
            kh = jnp.where(kheads[hd], k_both, zero) * jnp.asarray(scale, BF)
            vh = jnp.where(kheads[hd], v_both, zero)
            gk = jnp.zeros((K, 128), F32)
            gv = jnp.zeros((K, 128), F32)
            for i in range(chunks):
                base = pl.multiple_of((kb + i) * Q, Q)
                qs = qx[pl.ds(base, Q), :]
                at = lax.div(kb + i, 2)
                part = pl.ds(pl.multiple_of(lax.rem(kb + i, 2) * Q, Q), Q)
                r = st[at, hd : hd + 1, part]
                inner = st[at, 2 + hd : 3 + hd, part]
                ok = p * B + (kb + i) * Q < n_seq * Q
                if i == 0:
                    ok = ok & (qcol >= e * K + krow)
                if i * Q + Q - 1 - e * K >= WINDOW:
                    ok = ok & (i * Q + qcol - (e * K + krow) < WINDOW)
                sh = jnp.where(ok, jnp.exp(nt(kh, qs[:, lo])) * r, 0.0)
                ds = (sh * (nt(vh, qs[:, hi]) - inner)).astype(BF)
                gv = gv + nn(sh.astype(BF), qs[:, hi])
                gk = gk + nn(ds, qs[:, lo])
            kparts.append(gk)
            vparts.append(gv)
        dk[rows, :] = (jnp.where(kheads[0], kparts[0], kparts[1]) * scale).astype(BF)
        dv[rows, :] = jnp.where(kheads[0], vparts[0], vparts[1]).astype(BF)

    def input_block(cc, e, tt):
        rows = quarter(cc, e)
        grad = nt(dq[rows, :], w_block(0, tt)) + nt(dk[rows, :], w_block(1, tt)) + nt(dv[rows, :], w_block(2, tt))
        lanes = pl.ds(pl.multiple_of(tt * width, width), width)
        here = slice(e * K, (e + 1) * K)
        scaled = grad * gain[0:1, lanes]
        unit = (f[cc, tt, here, :].astype(F32) - nst[cc, here, 0:1]) * nst[cc, here, 1:2]
        both = scaled * unit
        return grad, scaled[:, 0:128] + scaled[:, 128:256], both[:, 0:128] + both[:, 128:256]

    def pack_sums(which):
        plain = jnp.sum(sums_p[which], 1, keepdims=True)
        unit = jnp.sum(sums_u[which], 1, keepdims=True)
        return jnp.where(lane == 0, plain, unit).T[0:8, :]

    def to_sib(d, e):
        rows = pl.ds(e * K, K)
        return send(ipt.at[d, rows], ipx.at[d, rows], ix_s.at[d, e], ix_r.at[d, e], sib, t)

    def to_owner(d, e):
        rows = pl.ds(e * K, K)
        return send(ips.at[d, rows], ipr.at[d, rows], i_s.at[d, e], i_r.at[d, e], s, me.other_t(d))

    for e in range(2):
        here = slice(e * K, (e + 1) * K)
        key_grads(1 - c, e)
        plain = jnp.zeros((K, 128), F32)
        unit = jnp.zeros((K, 128), F32)
        for d in [*range(1, T), 0]:
            grad, a, b = input_block(1 - c, e, me.other_t(d))
            plain, unit = plain + a, unit + b
            ipt[d, here, :] = grad.astype(BF)
            go(to_sib(d, e))
        sums_p[0, here, :], sums_u[0, here, :] = plain, unit
        if e == 1:
            nst_out[...] = pack_sums(0)
            go(send(nst_out, nsx, n_s.at[0], n_r.at[0], sib, t))
        key_grads(c, e)
        plain = jnp.zeros((K, 128), F32)
        unit = jnp.zeros((K, 128), F32)
        for d in [*range(1, T), 0]:
            grad, a, b = input_block(c, e, me.other_t(d))
            plain, unit = plain + a, unit + b
            to_sib(d, e).wait_recv()
            ips[d, here, :] = (grad + ipx[d, here, :].astype(F32)).astype(BF)
            if d:
                go(to_owner(d, e))
        sums_p[1, here, :], sums_u[1, here, :] = plain, unit
    send(nst_out, nsx, n_s.at[0], n_r.at[0], sib, t).wait_recv()
    nss[...] = pack_sums(1) + nsx[...]
    for d in range(1, T):
        go(send(nss, nsr.at[d], n_s.at[d], n_r.at[d], s, me.other_t(d)))

    acc_a = sga[z].astype(F32)
    acc_b = sgb[z].astype(F32)
    for d in range(1, Z):
        send(sga.at[0], sgza.at[d], za_s.at[d], za_r.at[d], sib, t).wait_recv()
        send(sgb.at[0], sgzb.at[d], zb_s.at[d], zb_r.at[d], sib, t).wait_recv()
        acc_a = acc_a + sgza[d].astype(F32)
        acc_b = acc_b + sgzb[d].astype(F32)
    sgh[:, :, 0:R, :] = acc_a
    sgh[:, :, R : R + 32, :] = acc_b
    for d in range(1, H):
        hh = me.other_h(d)
        go(send(sgh.at[hh], sghr.at[d], hh_s.at[d], hh_r.at[d], me.seq(hh, z, c), t))

    total = ips[0].astype(F32)
    sums = nss[...]
    for d in range(1, T):
        send(nss, nsr.at[d], n_s.at[d], n_r.at[d], sib, t).wait_recv()
        sums = sums + nsr[d]
        to_owner(d, 0).wait_recv()
        to_owner(d, 1).wait_recv()
        total = total + ipr[d].astype(F32)
    tall = jnp.concatenate([sums] * 16, 0).T
    here = pl.ds(pl.multiple_of(t * width, width), width)
    inv = nst[c, :, 1:2]
    unit = (f[c, t].astype(F32) - nst[c, :, 0:1]) * inv
    grad = inv * (total * gain[0:1, here] - tall[:, 0:1] / full - unit * (tall[:, 1:2] / full))
    fg[...] = grad.astype(BF)
    go(send(fg.at[pl.ds(0, 16)], rim, one_s.at[3], one_r.at[3], me.next(-1), t))
    acc = sgh[h]
    for d in range(1, H):
        send(sgh.at[0], sghr.at[d], hh_s.at[d], hh_r.at[d], sib, t).wait_recv()
        acc = acc + sghr[d]
    sgs[...] = acc
    go(send(sgs.at[1 - c], sgx, one_s.at[4], one_r.at[4], sib, t))
    longer[0:Q, :] = fg[...].astype(F32)
    total = ops[0].astype(F32)
    for d in range(1, T):
        send(ops.at[d], opr.at[d], o_s.at[d], o_r.at[d], sib, t).wait_recv()
        total = total + opr[d].astype(F32)
    out[...] = total.astype(BF)
    send(fg.at[pl.ds(0, 16)], rim, one_s.at[3], one_r.at[3], sib, t).wait_recv()
    send(sgs.at[0], sgx, one_s.at[4], one_r.at[4], sib, t).wait_recv()
    sgo[:, lo] = jnp.where(c == 0, sgs[c], sgx[...])
    sgo[:, hi] = jnp.where(c == 0, sgx[...], sgs[c])
    for copy in outgoing:
        copy.wait_send()
    for chain in (keys, queries):
        chain.finish()
    longer[Q : Q + 16, :] = jnp.where(s < n_seq - 1, rim[...].astype(F32), 0.0)
    later = [longer[d : d + Q, :] for d in range(4)]
    for k in range(4):
        book = later[0]
        for d in range(1, 4):
            book = jnp.where(delays[k] == d, later[d], book)
        de[k] = book.astype(BF)


def fused(n_seq, n_ten, delays, text_len, weights, text_weights, states, emb, gain, cot, text):
    H, Z = dims_of(n_seq)
    T = n_ten
    _, Q, W = emb.shape
    B = 2 * Q
    full = W * T
    R = weights[0].shape[0]
    pay_shape = (2, 4 * R + 32, 128)
    chunks = (WINDOW + Q - 2) // Q + 1
    dma = pltpu.SemaphoreType.DMA
    vm = pl.BlockSpec(memory_space=pltpu.VMEM)
    sm = pl.BlockSpec(memory_space=pltpu.SMEM)
    V = pltpu.VMEM
    block = V((T, Q, W), BF)
    rows = V((B, 128), BF)
    small = V((text, 128), F32)
    sums = V((8, Q), F32)

    def pair(*shape):
        return [dma(shape), dma(shape)]

    return pl.pallas_call(
        lambda a, b, *refs: fused_kernel(n_seq, n_ten, a, b, refs[0:4], refs[4:6], *refs[6:]),
        out_shape=(
            jax.ShapeDtypeStruct((Q, W), BF),
            jax.ShapeDtypeStruct((4, Q, W), BF),
            jax.ShapeDtypeStruct((R + 32, 256), F32),
        ),
        in_specs=[sm, sm] + [vm] * 9 + [pl.BlockSpec(memory_space=pl.ANY)],
        out_specs=(vm,) * 3,
        scratch_shapes=[
            V(pay_shape, BF), V((2, 16, 256), F32), V((2, Q, 128), F32), V((2, Q, 128), F32), V((H * Z,) + pay_shape, BF), V((2, T, Q, W), BF), V((B, full), BF), V((16, W), F32), V((Q, W), BF),
            V((Q + 16, W), F32), V((2, Q, 128), F32), V((B, full), BF), V((n_seq, 32, 128), F32),
            V((text, n_seq * 16), BF),
            V((text, 256), BF), V((4 * B, 256), BF), V((4 * B, 256), BF), V((3, Q, 256), BF), V((3, Q, 256), BF),
            V((2, 2, chunks, Q, Q), F32), V((2, 2, Q, text), F32), V((2, 2, Q, 128), F32), V((2, 2, Q, 128), F32),
            V((4, 8, B), F32), V((B, 128), F32),
            rows, rows, rows, rows, small, small,
            block, block, block, block, block, block, block, block, sums, sums, sums, V((T, 8, Q), F32),
            V((Z, H, 2, R, 128), BF), V((Z, H, 2, R, 128), BF), V((Z, H, 2, 32, 128), BF), V((Z, H, 2, 32, 128), BF),
            V((H, 2, R + 32, 128), F32), V((H, 2, R + 32, 128), F32), V((2, R + 32, 128), F32), V((R + 32, 128), F32),
            V((Q, W), BF), V((16, W), BF),
            dma((3,)), *pair(6), *pair(H), *pair(2, Z // 2 + 1, H), *pair(T), *pair(T),
            *pair(2, 3), *pair(3), *pair(2, 3), *pair(3), *pair(4), *pair(T), *pair(T, 2), *pair(T), *pair(T, 2), *pair(T),
            *pair(Z), *pair(Z), *pair(H),
        ],
        compiler_params=pltpu.CompilerParams(collective_id=0, has_side_effects=True, vmem_limit_bytes=56 << 20),
    )(delays, text_len, *weights, *text_weights, states, emb, gain, cot)


def shards(
    n_seq, n_ten, embedded, delays, norm_gain, w_query, w_key, w_value, w_out,
    text_states, w_text_key, w_text_value, text_len, cotangent,
):
    R = w_query.shape[0]
    tr = w_text_key.shape[0]
    per = text_states.shape[0]
    states = jnp.pad(text_states.reshape(per, n_seq, tr), ((0, 0), (0, 0), (0, 16 - tr))).reshape(16, 128)
    out, de, sgo = fused(
        n_seq, n_ten, delays, text_len, (w_query, w_key, w_value, w_out.T), (w_text_key, w_text_value),
        states.astype(F32), embedded.transpose(1, 0, 2), norm_gain.reshape(1, -1), cotangent, per * n_seq,
    )
    return (out, de.transpose(1, 0, 2), sgo[:R].T, sgo[R : R + tr], sgo[R + 16 : R + 16 + tr])


def solution(mesh):
    placed = (
        P("seq", None, "tensor"), P(), P(),
        P("seq", "tensor"), P("seq", "tensor"), P("seq", "tensor"), P("tensor", "seq"),
        P("seq", None), P("seq", "tensor"), P("seq", "tensor"), P(), P("seq", None),
    )
    return jax.shard_map(
        functools.partial(shards, mesh.shape["seq"], mesh.shape["tensor"]),
        mesh=mesh,
        in_specs=placed,
        out_specs=(
            P("seq", "tensor"), P("seq", None, "tensor"), P("tensor", "seq"),
            P("seq", "tensor"), P("seq", "tensor"),
        ),
        check_vma=False,
    )
```

```python
import functools

import jax
import jax.numpy as jnp
from jax import lax
from jax.experimental import pallas as pl
from jax.experimental.pallas import tpu as pltpu
from jax.sharding import PartitionSpec as P

HD = 64
WINDOW = 1500
EPS = 1e-05
RING = 8
RELAY = 1
MESH = pl.DeviceIdType.MESH
BF = jnp.bfloat16
F32 = jnp.float32


def dims_of(n_seq):
    z = min(RING, n_seq // 2)
    return n_seq // (2 * z), z


def nt(a, b):
    return lax.dot_general(a, b, (((1,), (1,)), ((), ())), preferred_element_type=F32)


def nn(a, b):
    return lax.dot_general(a, b, (((1,), (0,)), ((), ())), preferred_element_type=F32)


def tn(a, b):
    return lax.dot_general(a, b, (((0,), (0,)), ((), ())), preferred_element_type=F32)


def send(src, dst, ssem, rsem, seq, ten):
    return pltpu.make_async_remote_copy(
        src_ref=src, dst_ref=dst, send_sem=ssem, recv_sem=rsem, device_id=(seq, ten), device_id_type=MESH
    )


def greet(partners):
    sem = pltpu.get_barrier_semaphore()
    for seq, ten in partners:
        pl.semaphore_signal(sem, inc=1, device_id=(seq, ten), device_id_type=MESH)
    return lambda: pl.semaphore_wait(sem, len(partners))


class Place:
    def __init__(self, n_seq, n_ten):
        self.n_seq, self.n_ten = n_seq, n_ten
        self.H, self.Z = dims_of(n_seq)
        self.s = lax.axis_index("seq")
        self.t = lax.axis_index("tensor")
        self.c = lax.rem(self.s, 2)
        self.p = lax.div(self.s, 2)
        self.h = lax.div(self.p, self.Z)
        self.z = lax.rem(self.p, self.Z)
        self.chips = n_seq // 2

    def seq(self, h, z, c):
        return (h * self.Z + z) * 2 + c

    def sibling(self):
        return self.seq(self.h, self.z, 1 - self.c)

    def chip(self, k):
        return lax.rem(self.p + k + self.chips, self.chips) * 2 + self.c

    def other_h(self, d):
        return lax.rem(self.h + d, self.H)

    def other_z(self, d):
        return lax.rem(self.z + d + self.Z, self.Z)

    def other_t(self, d):
        return lax.rem(self.t + d + self.n_ten, self.n_ten)

    def next(self, d):
        return lax.rem(self.s + d + self.n_seq, self.n_seq)


class Chain:
    def __init__(self, me, sign, at, relay, ss, rr, rs, rx):
        self.me, self.sign, self.at, self.relay, self.ss, self.rr, self.rs, self.rx = me, sign, at, relay, ss, rr, rs, rx
        self.edge, self.turn = (me.Z - 1, 0) if sign > 0 else (0, me.Z - 1)
        row = me.other_h(sign + me.H)
        if RELAY == 1:
            self.at_relay = me.z == self.turn
            self.via = me.seq(me.h, self.turn, me.c)
        else:
            self.at_relay = me.z == self.edge
            self.via = me.seq(row, self.edge, me.c)
        self.goal = me.seq(row if RELAY == 1 else me.h, self.turn, me.c)

    def copy(self, k, half):
        nxt = self.me.chip(self.sign)
        return send(
            self.at(k - 1, half), self.at(k, half), self.ss.at[half, k - 1], self.rr.at[half, k - 1], nxt, self.me.t
        )

    def push(self, k, half):
        if half == 0:
            self.copy(k, 0).start()
            return

        @pl.when(self.me.z != self.edge)
        def _():
            self.copy(k, 1).start()

        @pl.when(self.me.z == self.edge)
        def _():
            send(
                self.at(k - 1, 1), self.relay.at[k - 1], self.ss.at[1, k - 1], self.rx.at[k - 1], self.via, self.me.t
            ).start()

    def on(self, k):
        return send(
            self.relay.at[k - 1], self.at(k, 1), self.rs.at[k - 1], self.rr.at[1, k - 1], self.goal, self.me.t
        )

    def take(self, k, half):
        if half == 1:

            @pl.when(self.at_relay)
            def _():
                send(
                    self.relay.at[k - 1], self.relay.at[k - 1], self.rs.at[k - 1], self.rx.at[k - 1], self.via, self.me.t
                ).wait_recv()
                self.on(k).start()

        self.copy(k, half).wait_recv()
        if k < 3:
            self.push(k + 1, half)

    def finish(self):
        for k in (1, 2, 3):
            for half in (0, 1):
                self.copy(k, half).wait_send()

        @pl.when(self.at_relay)
        def _():
            for k in (1, 2, 3):
                self.on(k).wait_send()


def fused_kernel(
    n_seq, n_ten, delays, text_len, w_in, t_in, s_in, emb, gain, cot, out, de, sgo,
    pay, tmp,
    g, f, cots, rimbuf, blk, longer, nst, normed, states32, states,
    tkv, kx, qx, k_relay, q_relay, wbuf, wtbuf, mixbuf, totbuf, st, cstat,
    att, dq, dk, dv, tkg, tvg,
    opt, opx, opr, ipt, ipx, ipr, ops, ips, nst_out, nsx, nss, nsr,
    sga, sgza, sgb, sgzb, sgh, sghr, sgs, sgx, fg, rim,
    lsem, one_s, one_r, h_s, h_r, z_s, z_r, f_s, f_r, x_s, x_r,
    k_s, k_r, k_rs, k_rx, q_s, q_r, q_rs, q_rx, t_s, t_r, ox_s, ox_r, ix_s, ix_r, o_s, o_r, i_s, i_r, n_s, n_r,
    za_s, za_r, zb_s, zb_r, hh_s, hh_r,
):
    me = Place(n_seq, n_ten)
    H, Z, T = me.H, me.Z, n_ten
    s, t, c, h, z, p = me.s, me.t, me.c, me.h, me.z, me.p
    sib = me.sibling()
    half = Z // 2
    width = emb.shape[2]
    Q = emb.shape[1]
    B = 2 * Q
    R = sga.shape[3]
    text = states.shape[0]
    full = width * T
    scale = HD ** (-0.5)
    zero = jnp.zeros((), BF)
    right, left = me.seq(h, me.other_z(1), c), me.seq(h, me.other_z(-1), c)
    partners = [(sib, t), (me.next(1), t), (me.next(-1), t)]
    partners += [(me.seq(me.other_h(d), z, c), t) for d in range(1, H)]
    partners += [(me.seq(h, me.other_z(d), c), t) for d in range(1, Z)]
    partners += [(s, me.other_t(d)) for d in range(1, T)]
    partners += [(me.chip(k), t) for k in (1, -1, 2, -2, 3, -3)]
    all_here = greet(partners)
    outgoing = []

    def go(copy):
        copy.start()
        outgoing.append(copy)

    def half_rows(core):
        return pl.ds(pl.multiple_of(core * Q, Q), Q)

    per = text // n_seq
    given = t_in[0].shape[0]
    tmp[...] = jnp.zeros_like(tmp)
    for i in range(2):
        tmp[i, 0:given, :] = t_in[i][...].astype(F32)
        for e in range(2):
            tmp[i, 12:16, e * 128 : (e + 1) * 128] = s_in[e * 8 + i * 4 : e * 8 + i * 4 + 4, :]
    for e in range(2):
        lanes = slice(e * 128, (e + 1) * 128)
        for i in range(4):
            pay[e, i * R : (i + 1) * R, :] = w_in[i][:, lanes]
        for i in range(2):
            pay[e, 4 * R + 16 * i : 4 * R + 16 * (i + 1), :] = tmp[i, :, lanes].astype(BF)
    all_here()
    go(send(pay.at[1 - c], g.at[p, c], one_s.at[0], one_r.at[0], sib, t))
    mine = pltpu.make_async_copy(pay.at[c], g.at[p, c], lsem.at[0])
    mine.start()
    mine.wait()
    send(pay.at[c], g.at[p, 1 - c], one_s.at[0], one_r.at[0], sib, t).wait_recv()
    for d in range(1, H):
        go(send(g.at[p], g.at[p], h_s.at[d], h_r.at[d], me.seq(me.other_h(d), z, c), t))

    def step(way, k, d):
        hh = me.other_h(d)
        zz = me.other_z(-(k - 1) if way == 0 else k - 1)
        go(send(g.at[hh * Z + zz], g.at[hh * Z + zz], z_s.at[way, k, d], z_r.at[way, k, d], right if way == 0 else left, t))

    def arrived(way, k, d):
        hh = me.other_h(d)
        zz = me.other_z(-k if way == 0 else k)
        send(g.at[hh * Z + zz], g.at[hh * Z + zz], z_s.at[way, k, d], z_r.at[way, k, d], right, t).wait_recv()

    def used(way, k, d):
        if k < half:
            return True
        if k > half:
            return False
        return (d < H // 2) if way == 0 else (d >= H // 2)

    for way in (0, 1):
        if used(way, 1, 0):
            step(way, 1, 0)
    longer[...] = jnp.zeros_like(longer)
    for d in range(4):
        book = jnp.zeros((Q, width), F32)
        for k in range(4):
            book = book + jnp.where(delays[k] == d, emb[k].astype(F32), 0.0)
        longer[d : d + Q, :] = longer[d : d + Q, :] + book
    go(send(longer.at[pl.ds(Q, 16)], rimbuf, one_s.at[1], one_r.at[1], me.next(1), t))
    for d in range(1, H):
        hh = me.other_h(H - d)
        send(g.at[hh * Z + z], g.at[hh * Z + z], h_s.at[d], h_r.at[d], sib, t).wait_recv()
        for way in (0, 1):
            if used(way, 1, H - d):
                step(way, 1, H - d)
    send(longer.at[pl.ds(Q, 16)], rimbuf, one_s.at[1], one_r.at[1], me.next(1), t).wait_recv()
    blk[...] = longer[0:Q, :].astype(BF)
    blk[0:16, :] = (longer[0:16, :] + jnp.where(s > 0, rimbuf[...], 0.0)).astype(BF)
    for d in range(1, T):
        go(send(blk, f.at[c, t], f_s.at[d], f_r.at[d], s, me.other_t(d)))
    go(send(blk, f.at[c, t], x_s.at[0], x_r.at[0], sib, t))
    own = pltpu.make_async_copy(blk, f.at[c, t], lsem.at[1])
    own.start()
    go(send(cot, cots.at[half_rows(c)], one_s.at[2], one_r.at[2], sib, t))
    mycot = pltpu.make_async_copy(cot, cots.at[half_rows(c)], lsem.at[2])
    mycot.start()
    order = [0] + [H - e for e in range(1, H)]
    ring_last = half

    def ring(k):
        for d in order:
            for way in (0, 1):
                if used(way, k, d):
                    arrived(way, k, d)
                    if used(way, k + 1, d):
                        step(way, k + 1, d)

    def pass_frames():
        for d in range(1, T):
            tt = me.other_t(-d)
            send(blk, f.at[c, tt], f_s.at[d], f_r.at[d], sib, t).wait_recv()
            go(send(f.at[c, tt], f.at[c, tt], x_s.at[d], x_r.at[d], sib, t))

    def norm(cc):
        def fold(v):
            return v[:, 0:128] + v[:, 128:256]

        acc = jnp.zeros((Q, 128), F32)
        acc = lax.fori_loop(0, T, lambda i, a: a + fold(f[cc, i].astype(F32)), acc)
        mean = jnp.sum(acc, 1, keepdims=True) / full

        def second(i, a):
            v = f[cc, i].astype(F32) - mean
            return a + fold(v * v)

        acc = lax.fori_loop(0, T, second, jnp.zeros((Q, 128), F32))
        inv = lax.rsqrt(jnp.sum(acc, 1, keepdims=True) / full + EPS)
        lane128 = lax.broadcasted_iota(jnp.int32, (Q, 128), 1)
        nst[cc] = jnp.where(lane128 == 0, mean, inv)

        def third(i, carry):
            w = pl.ds(pl.multiple_of(i * width, width), width)
            v = (f[cc, i].astype(F32) - mean) * inv
            normed[half_rows(cc), w] = (v * gain[0:1, w]).astype(BF)
            return carry

        lax.fori_loop(0, T, third, 0)

    for k in range(1, half):
        if k == max(half - 2, 1):
            pass_frames()
        ring(k)
    if half == 1:
        pass_frames()
    own.wait()
    norm(c)
    for d in range(T):
        tt = me.other_t(-d)
        send(blk, f.at[1 - c, tt], x_s.at[d], x_r.at[d], sib, t).wait_recv()
    norm(1 - c)
    ring(half)

    def weight(i):
        return g[:, :, i * R : (i + 1) * R, :].reshape(n_seq * R, 128)

    def project(src, i, dst, first, lanes):
        def go_rows(rb, carry):
            rows = pl.ds(pl.multiple_of(first + rb * Q, Q), Q)
            dst[rows, lanes] = nn(src[half_rows(rb), :], weight(i)).astype(BF)
            return carry

        lax.fori_loop(0, 2, go_rows, 0)

    lo, hi = slice(0, 128), slice(128, 256)
    keys = Chain(
        me, 1, lambda k, e: kx.at[pl.ds((3 - k) * B + e * Q, Q)], k_relay, k_s, k_r, k_rs, k_rx
    )
    queries = Chain(me, -1, lambda k, e: qx.at[pl.ds(k * B + e * Q, Q)], q_relay, q_s, q_r, q_rs, q_rx)
    kv = kx.at[pl.ds(3 * B, B)]
    qd = qx.at[pl.ds(0, B)]
    project(normed, 1, kx, 3 * B, lo)
    project(normed, 2, kx, 3 * B, hi)
    keys.push(1, 1)
    keys.push(1, 0)
    project(normed, 0, qx, 0, lo)
    mycot.wait()
    send(cot, cots.at[half_rows(c)], one_s.at[2], one_r.at[2], sib, t).wait_recv()
    project(cots, 3, qx, 0, hi)
    queries.push(1, 1)
    queries.push(1, 0)

    lane = lax.broadcasted_iota(jnp.int32, (Q, 128), 1)
    row = lax.broadcasted_iota(jnp.int32, (Q, Q), 0)
    col = lax.broadcasted_iota(jnp.int32, (Q, Q), 1)
    heads = [lane < HD, lane >= HD]
    chunks = (WINDOW + Q - 2) // Q + 1
    lead = (chunks - 1) * Q

    def forward_chunk(qb, hd, q, j):
        base = pl.multiple_of((qb + j) * Q, Q)
        w = jnp.exp(nt(q, kx[pl.ds(base, Q), lo]))
        ok = p * B - 3 * B + (qb + j) * Q >= 0
        if lead - j * Q + Q - 1 >= WINDOW:
            ok = ok & (lead + row - j * Q - col < WINDOW)
        if j == chunks - 1:
            ok = ok & (col <= row)
        w = jnp.where(ok, w, 0.0)
        wbuf[qb, hd, j] = w
        return w[:, 0:128] + w[:, 128:256], nn(w.astype(BF), kx[pl.ds(base, Q), hi])

    def forward(k):
        for qb in range(2):
            q_both = qd[qb * Q : (qb + 1) * Q, lo]
            for hd in range(2):
                q = jnp.where(heads[hd], q_both, zero) * jnp.asarray(scale, BF)
                if k == 0:
                    total, mix = jnp.zeros((Q, 128), F32), jnp.zeros((Q, 128), F32)
                else:
                    total, mix = totbuf[qb, hd], mixbuf[qb, hd]
                if k == 4:
                    wt = jnp.where(live, jnp.exp(nt(q, tkv[:, lo])), 0.0)
                    wtbuf[qb, hd] = wt
                    total, mix = total + wt, mix + nn(wt.astype(BF), tkv[:, hi])
                for j in range(chunks):
                    if (qb + j) // 2 == 3 - k:
                        a, b = forward_chunk(qb, hd, q, j)
                        total, mix = total + a, mix + b
                totbuf[qb, hd], mixbuf[qb, hd] = total, mix

    states32[...] = g[:, :, 4 * R : 4 * R + 32, :].reshape(n_seq, 32, 128).astype(F32)
    lanes_of = 8 // (per // 2)
    for e in range(8):
        at = 12 + e if e < 4 else 24 + e
        first = pl.multiple_of((c * (per // 2) + e // lanes_of) * n_seq, n_seq)
        x = (e % lanes_of) * 128
        states[pl.ds(first, n_seq), x : x + 128] = states32[:, at, :].astype(BF)
    my_states = states.at[pl.ds(pl.multiple_of(c * (text // 2), text // 2), text // 2)]
    go(send(my_states, my_states, one_s.at[5], one_r.at[5], sib, t))
    forward(0)
    send(my_states, my_states, one_s.at[5], one_r.at[5], sib, t).wait_recv()
    for i in range(2):
        w = g[:, :, 4 * R + 16 * i : 4 * R + 16 * (i + 1), :].reshape(n_seq * 16, 128)
        tkv[:, i * 128 : (i + 1) * 128] = nn(states[...], w).astype(BF)
    token = lax.broadcasted_iota(jnp.int32, (1, text), 1)
    live = lax.rem(token, n_seq) * per + lax.div(token, n_seq) < text_len[0]

    forward(4)
    for k in (1, 2, 3):
        for e in (1, 0):
            keys.take(k, e)
            queries.take(k, e)
        forward(k)
    for qb in range(2):
        rows = slice(qb * Q, (qb + 1) * Q)
        d_both = qd[rows, hi].astype(F32)
        parts, stats = [], []
        for hd in range(2):
            total = jnp.sum(totbuf[qb, hd], 1, keepdims=True)
            a_head = (mixbuf[qb, hd] / total).astype(BF)
            parts.append(a_head)
            inner = jnp.sum(jnp.where(heads[hd], d_both * a_head.astype(F32), 0.0), 1, keepdims=True)
            stats.append((1.0 / total, inner))
        att[rows, :] = jnp.where(heads[0], parts[0], parts[1])
        (r0, i0), (r1, i1) = stats
        packed = jnp.where(lane == 0, r0, jnp.where(lane == 1, r1, jnp.where(lane == 2, i0, i1)))
        cstat[rows, :] = packed
        st[0, :, rows] = packed.T[0:8, :]
    for k in (1, 2, 3):
        go(send(st.at[0], st.at[k], t_s.at[k], t_r.at[k], me.chip(-k), t))

    def w_block(i, tt):
        n = width // (2 * R)
        return g[pl.ds(tt * n, n), :, i * R : (i + 1) * R, :].reshape(width, 128)

    for d in range(T):
        tt = me.other_t(d)
        opt[d] = nt(att[half_rows(1 - c), :], w_block(3, tt)).astype(BF)
        go(send(opt.at[d], opx.at[d], ox_s.at[d], ox_r.at[d], sib, t))
    for e in range(full // B):
        piece = tn(att[...], cots[:, e * B : (e + 1) * B])
        n = B // R
        for a in range(B // 128):
            rows = piece[:, a * 128 : (a + 1) * 128].T.astype(BF).reshape(128 // R, R, 128)
            for b in range(128 // R):
                who = e * n + a * (128 // R) + b
                hh, zz, cc = who // (2 * Z), (who // 2) % Z, who % 2
                sga[zz, hh, cc] = rows[b]
    for d in range(1, Z):
        zz = me.other_z(d)
        go(send(sga.at[zz], sgza.at[d], za_s.at[d], za_r.at[d], me.seq(h, zz, c), t))

    tkg[...] = jnp.zeros_like(tkg)
    tvg[...] = jnp.zeros_like(tvg)

    def query_grads(qb, carry):
        rows = half_rows(qb)
        q_both = qd[rows, lo]
        d_both = qd[rows, hi]
        parts = []
        for hd in range(2):
            q = jnp.where(heads[hd], q_both, zero)
            d = jnp.where(heads[hd], d_both, zero)
            r = cstat[rows, hd : hd + 1]
            inner = cstat[rows, 2 + hd : 3 + hd]
            sh = wtbuf[qb, hd] * r
            ds = (sh * (nt(d, tkv[:, hi]) - inner)).astype(BF)
            grad = nn(ds, tkv[:, lo])
            tkg[...] += tn(ds, q) * scale
            tvg[...] += tn(sh.astype(BF), d)
            for j in range(chunks):
                base = pl.multiple_of((qb + j) * Q, Q)
                around = kx[pl.ds(base, Q), :]
                ds = (wbuf[qb, hd, j] * r * (nt(d, around[:, hi]) - inner)).astype(BF)
                grad = grad + nn(ds, around[:, lo])
            parts.append(grad)
        dq[rows, :] = (jnp.where(heads[0], parts[0], parts[1]) * scale).astype(BF)
        return carry

    lax.fori_loop(0, 2, query_grads, 0)
    for i, grad in enumerate((tkg, tvg)):
        piece = tn(states[...], grad[...].astype(BF)).astype(BF).reshape(H, Z, 2, 16, 128)
        for zz in range(Z):
            sgb[zz, :, :, 16 * i : 16 * (i + 1), :] = piece[:, zz]
    for d in range(1, Z):
        zz = me.other_z(d)
        go(send(sgb.at[zz], sgzb.at[d], zb_s.at[d], zb_r.at[d], me.seq(h, zz, c), t))
    for d in [*range(1, T), 0]:
        tt = me.other_t(d)
        send(opt.at[d], opx.at[d], ox_s.at[d], ox_r.at[d], sib, t).wait_recv()
        ops[d] = (nt(att[half_rows(c), :], w_block(3, tt)) + opx[d].astype(F32)).astype(BF)
        if d:
            go(send(ops.at[d], opr.at[d], o_s.at[d], o_r.at[d], s, tt))
    for k in (1, 2, 3):
        send(st.at[0], st.at[k], t_s.at[k], t_r.at[k], me.chip(-k), t).wait_recv()

    def key_grads(kb, carry):
        rows = half_rows(kb)
        k_both = kv[rows, lo]
        v_both = kv[rows, hi]
        kparts, vparts = [], []
        for hd in range(2):
            kh = jnp.where(heads[hd], k_both, zero) * jnp.asarray(scale, BF)
            vh = jnp.where(heads[hd], v_both, zero)
            gk = jnp.zeros((Q, 128), F32)
            gv = jnp.zeros((Q, 128), F32)
            for i in range(chunks):
                base = pl.multiple_of((kb + i) * Q, Q)
                qs = qx[pl.ds(base, Q), :]
                at = lax.div(kb + i, 2)
                part = pl.ds(pl.multiple_of(lax.rem(kb + i, 2) * Q, Q), Q)
                r = st[at, hd : hd + 1, part]
                inner = st[at, 2 + hd : 3 + hd, part]
                ok = p * B + (kb + i) * Q < n_seq * Q
                if i == 0:
                    ok = ok & (col >= row)
                if i * Q + Q - 1 >= WINDOW:
                    ok = ok & (i * Q + col - row < WINDOW)
                sh = jnp.where(ok, jnp.exp(nt(kh, qs[:, lo])) * r, 0.0)
                ds = (sh * (nt(vh, qs[:, hi]) - inner)).astype(BF)
                gv = gv + nn(sh.astype(BF), qs[:, hi])
                gk = gk + nn(ds, qs[:, lo])
            kparts.append(gk)
            vparts.append(gv)
        dk[rows, :] = (jnp.where(heads[0], kparts[0], kparts[1]) * scale).astype(BF)
        dv[rows, :] = jnp.where(heads[0], vparts[0], vparts[1]).astype(BF)
        return carry

    key_grads(1 - c, 0)

    def input_block(cc, tt):
        rows = half_rows(cc)
        grad = nt(dq[rows, :], w_block(0, tt)) + nt(dk[rows, :], w_block(1, tt)) + nt(dv[rows, :], w_block(2, tt))
        lanes = pl.ds(pl.multiple_of(tt * width, width), width)
        scaled = grad * gain[0:1, lanes]
        unit = (f[cc, tt].astype(F32) - nst[cc, :, 0:1]) * nst[cc, :, 1:2]
        both = scaled * unit
        return grad, scaled[:, 0:128] + scaled[:, 128:256], both[:, 0:128] + both[:, 128:256]

    def pack_sums(plain, unit):
        plain = jnp.sum(plain, 1, keepdims=True)
        unit = jnp.sum(unit, 1, keepdims=True)
        return jnp.where(lane == 0, plain, unit).T[0:8, :]

    plain = jnp.zeros((Q, 128), F32)
    unit = jnp.zeros((Q, 128), F32)
    for d in [*range(1, T), 0]:
        tt = me.other_t(d)
        grad, a, b = input_block(1 - c, tt)
        plain, unit = plain + a, unit + b
        ipt[d] = grad.astype(BF)
        go(send(ipt.at[d], ipx.at[d], ix_s.at[d], ix_r.at[d], sib, t))
    nst_out[...] = pack_sums(plain, unit)
    go(send(nst_out, nsx, n_s.at[0], n_r.at[0], sib, t))
    key_grads(c, 0)
    plain = jnp.zeros((Q, 128), F32)
    unit = jnp.zeros((Q, 128), F32)
    for d in [*range(1, T), 0]:
        tt = me.other_t(d)
        grad, a, b = input_block(c, tt)
        plain, unit = plain + a, unit + b
        send(ipt.at[d], ipx.at[d], ix_s.at[d], ix_r.at[d], sib, t).wait_recv()
        ips[d] = (grad + ipx[d].astype(F32)).astype(BF)
        if d:
            go(send(ips.at[d], ipr.at[d], i_s.at[d], i_r.at[d], s, tt))
    send(nst_out, nsx, n_s.at[0], n_r.at[0], sib, t).wait_recv()
    nss[...] = pack_sums(plain, unit) + nsx[...]
    for d in range(1, T):
        go(send(nss, nsr.at[d], n_s.at[d], n_r.at[d], s, me.other_t(d)))

    acc_a = sga[z].astype(F32)
    acc_b = sgb[z].astype(F32)
    for d in range(1, Z):
        send(sga.at[0], sgza.at[d], za_s.at[d], za_r.at[d], sib, t).wait_recv()
        send(sgb.at[0], sgzb.at[d], zb_s.at[d], zb_r.at[d], sib, t).wait_recv()
        acc_a = acc_a + sgza[d].astype(F32)
        acc_b = acc_b + sgzb[d].astype(F32)
    sgh[:, :, 0:R, :] = acc_a
    sgh[:, :, R : R + 32, :] = acc_b
    for d in range(1, H):
        hh = me.other_h(d)
        go(send(sgh.at[hh], sghr.at[d], hh_s.at[d], hh_r.at[d], me.seq(hh, z, c), t))

    total = ips[0].astype(F32)
    sums = nss[...]
    for d in range(1, T):
        send(nss, nsr.at[d], n_s.at[d], n_r.at[d], sib, t).wait_recv()
        sums = sums + nsr[d]
        send(ips.at[d], ipr.at[d], i_s.at[d], i_r.at[d], sib, t).wait_recv()
        total = total + ipr[d].astype(F32)
    tall = jnp.concatenate([sums] * 16, 0).T
    here = pl.ds(pl.multiple_of(t * width, width), width)
    inv = nst[c, :, 1:2]
    unit = (f[c, t].astype(F32) - nst[c, :, 0:1]) * inv
    grad = inv * (total * gain[0:1, here] - tall[:, 0:1] / full - unit * (tall[:, 1:2] / full))
    fg[...] = grad.astype(BF)
    go(send(fg.at[pl.ds(0, 16)], rim, one_s.at[3], one_r.at[3], me.next(-1), t))
    acc = sgh[h]
    for d in range(1, H):
        send(sgh.at[0], sghr.at[d], hh_s.at[d], hh_r.at[d], sib, t).wait_recv()
        acc = acc + sghr[d]
    sgs[...] = acc
    go(send(sgs.at[1 - c], sgx, one_s.at[4], one_r.at[4], sib, t))
    longer[0:Q, :] = fg[...].astype(F32)
    total = ops[0].astype(F32)
    for d in range(1, T):
        send(ops.at[d], opr.at[d], o_s.at[d], o_r.at[d], sib, t).wait_recv()
        total = total + opr[d].astype(F32)
    out[...] = total.astype(BF)
    send(fg.at[pl.ds(0, 16)], rim, one_s.at[3], one_r.at[3], sib, t).wait_recv()
    send(sgs.at[0], sgx, one_s.at[4], one_r.at[4], sib, t).wait_recv()
    sgo[:, lo] = jnp.where(c == 0, sgs[c], sgx[...])
    sgo[:, hi] = jnp.where(c == 0, sgx[...], sgs[c])
    for copy in outgoing:
        copy.wait_send()
    for chain in (keys, queries):
        chain.finish()
    longer[Q : Q + 16, :] = jnp.where(s < n_seq - 1, rim[...].astype(F32), 0.0)
    later = [longer[d : d + Q, :] for d in range(4)]
    for k in range(4):
        book = later[0]
        for d in range(1, 4):
            book = jnp.where(delays[k] == d, later[d], book)
        de[k] = book.astype(BF)


def fused(n_seq, n_ten, delays, text_len, weights, text_weights, states, emb, gain, cot, text):
    H, Z = dims_of(n_seq)
    T = n_ten
    _, Q, W = emb.shape
    B = 2 * Q
    full = W * T
    R = weights[0].shape[0]
    pay_shape = (2, 4 * R + 32, 128)
    chunks = (WINDOW + Q - 2) // Q + 1
    dma = pltpu.SemaphoreType.DMA
    vm = pl.BlockSpec(memory_space=pltpu.VMEM)
    sm = pl.BlockSpec(memory_space=pltpu.SMEM)
    V = pltpu.VMEM
    block = V((T, Q, W), BF)
    rows = V((B, 128), BF)
    small = V((text, 128), F32)
    sums = V((8, Q), F32)

    def pair(*shape):
        return [dma(shape), dma(shape)]

    return pl.pallas_call(
        lambda a, b, *refs: fused_kernel(n_seq, n_ten, a, b, refs[0:4], refs[4:6], *refs[6:]),
        out_shape=(
            jax.ShapeDtypeStruct((Q, W), BF),
            jax.ShapeDtypeStruct((4, Q, W), BF),
            jax.ShapeDtypeStruct((R + 32, 256), F32),
        ),
        in_specs=[sm, sm] + [vm] * 9 + [pl.BlockSpec(memory_space=pl.ANY)],
        out_specs=(vm,) * 3,
        scratch_shapes=[
            V(pay_shape, BF), V((2, 16, 256), F32), V((H * Z,) + pay_shape, BF), V((2, T, Q, W), BF), V((B, full), BF), V((16, W), F32), V((Q, W), BF),
            V((Q + 16, W), F32), V((2, Q, 128), F32), V((B, full), BF), V((n_seq, 32, 128), F32),
            V((text, n_seq * 16), BF),
            V((text, 256), BF), V((4 * B, 256), BF), V((4 * B, 256), BF), V((3, Q, 256), BF), V((3, Q, 256), BF),
            V((2, 2, chunks, Q, Q), F32), V((2, 2, Q, text), F32), V((2, 2, Q, 128), F32), V((2, 2, Q, 128), F32),
            V((4, 8, B), F32), V((B, 128), F32),
            rows, rows, rows, rows, small, small,
            block, block, block, block, block, block, block, block, sums, sums, sums, V((T, 8, Q), F32),
            V((Z, H, 2, R, 128), BF), V((Z, H, 2, R, 128), BF), V((Z, H, 2, 32, 128), BF), V((Z, H, 2, 32, 128), BF),
            V((H, 2, R + 32, 128), F32), V((H, 2, R + 32, 128), F32), V((2, R + 32, 128), F32), V((R + 32, 128), F32),
            V((Q, W), BF), V((16, W), BF),
            dma((3,)), *pair(6), *pair(H), *pair(2, Z // 2 + 1, H), *pair(T), *pair(T),
            *pair(2, 3), *pair(3), *pair(2, 3), *pair(3), *pair(4), *pair(T), *pair(T), *pair(T), *pair(T), *pair(T),
            *pair(Z), *pair(Z), *pair(H),
        ],
        compiler_params=pltpu.CompilerParams(collective_id=0, has_side_effects=True, vmem_limit_bytes=56 << 20),
    )(delays, text_len, *weights, *text_weights, states, emb, gain, cot)


def shards(
    n_seq, n_ten, embedded, delays, norm_gain, w_query, w_key, w_value, w_out,
    text_states, w_text_key, w_text_value, text_len, cotangent,
):
    R = w_query.shape[0]
    tr = w_text_key.shape[0]
    per = text_states.shape[0]
    states = jnp.pad(text_states.reshape(per, n_seq, tr), ((0, 0), (0, 0), (0, 16 - tr))).reshape(16, 128)
    out, de, sgo = fused(
        n_seq, n_ten, delays, text_len, (w_query, w_key, w_value, w_out.T), (w_text_key, w_text_value),
        states.astype(F32), embedded.transpose(1, 0, 2), norm_gain.reshape(1, -1), cotangent, per * n_seq,
    )
    return (out, de.transpose(1, 0, 2), sgo[:R].T, sgo[R : R + tr], sgo[R + 16 : R + 16 + tr])


def solution(mesh):
    placed = (
        P("seq", None, "tensor"), P(), P(),
        P("seq", "tensor"), P("seq", "tensor"), P("seq", "tensor"), P("tensor", "seq"),
        P("seq", None), P("seq", "tensor"), P("seq", "tensor"), P(), P("seq", None),
    )
    return jax.shard_map(
        functools.partial(shards, mesh.shape["seq"], mesh.shape["tensor"]),
        mesh=mesh,
        in_specs=placed,
        out_specs=(
            P("seq", "tensor"), P("seq", None, "tensor"), P("tensor", "seq"),
            P("seq", "tensor"), P("seq", "tensor"),
        ),
        check_vma=False,
    )
```

```python
import functools

import jax
import jax.numpy as jnp
from jax import lax
from jax.experimental import pallas as pl
from jax.experimental.pallas import tpu as pltpu
from jax.sharding import PartitionSpec as P

HD = 64
WINDOW = 1500
EPS = 1e-05
RING = 8
RELAY = 1
MESH = pl.DeviceIdType.MESH
BF = jnp.bfloat16
F32 = jnp.float32


def dims_of(n_seq):
    z = min(RING, n_seq // 2)
    return n_seq // (2 * z), z


def nt(a, b):
    return lax.dot_general(a, b, (((1,), (1,)), ((), ())), preferred_element_type=F32)


def nn(a, b):
    return lax.dot_general(a, b, (((1,), (0,)), ((), ())), preferred_element_type=F32)


def tn(a, b):
    return lax.dot_general(a, b, (((0,), (0,)), ((), ())), preferred_element_type=F32)


def send(src, dst, ssem, rsem, seq, ten):
    return pltpu.make_async_remote_copy(
        src_ref=src, dst_ref=dst, send_sem=ssem, recv_sem=rsem, device_id=(seq, ten), device_id_type=MESH
    )


def greet(partners):
    sem = pltpu.get_barrier_semaphore()
    for seq, ten in partners:
        pl.semaphore_signal(sem, inc=1, device_id=(seq, ten), device_id_type=MESH)
    pl.semaphore_wait(sem, len(partners))


class Place:
    def __init__(self, n_seq, n_ten):
        self.n_seq, self.n_ten = n_seq, n_ten
        self.H, self.Z = dims_of(n_seq)
        self.s = lax.axis_index("seq")
        self.t = lax.axis_index("tensor")
        self.c = lax.rem(self.s, 2)
        self.p = lax.div(self.s, 2)
        self.h = lax.div(self.p, self.Z)
        self.z = lax.rem(self.p, self.Z)
        self.chips = n_seq // 2

    def seq(self, h, z, c):
        return (h * self.Z + z) * 2 + c

    def sibling(self):
        return self.seq(self.h, self.z, 1 - self.c)

    def chip(self, k):
        return lax.rem(self.p + k + self.chips, self.chips) * 2 + self.c

    def other_h(self, d):
        return lax.rem(self.h + d, self.H)

    def other_z(self, d):
        return lax.rem(self.z + d + self.Z, self.Z)

    def other_t(self, d):
        return lax.rem(self.t + d + self.n_ten, self.n_ten)

    def next(self, d):
        return lax.rem(self.s + d + self.n_seq, self.n_seq)


class Chain:
    def __init__(self, me, sign, at, relay, ss, rr, rs, rx):
        self.me, self.sign, self.at, self.relay, self.ss, self.rr, self.rs, self.rx = me, sign, at, relay, ss, rr, rs, rx
        self.edge, self.turn = (me.Z - 1, 0) if sign > 0 else (0, me.Z - 1)
        row = me.other_h(sign + me.H)
        if RELAY == 1:
            self.at_relay = me.z == self.turn
            self.via = me.seq(me.h, self.turn, me.c)
        else:
            self.at_relay = me.z == self.edge
            self.via = me.seq(row, self.edge, me.c)
        self.goal = me.seq(row if RELAY == 1 else me.h, self.turn, me.c)

    def copy(self, k, half):
        nxt = self.me.chip(self.sign)
        return send(
            self.at(k - 1, half), self.at(k, half), self.ss.at[half, k - 1], self.rr.at[half, k - 1], nxt, self.me.t
        )

    def push(self, k):
        self.copy(k, 0).start()

        @pl.when(self.me.z != self.edge)
        def _():
            self.copy(k, 1).start()

        @pl.when(self.me.z == self.edge)
        def _():
            send(
                self.at(k - 1, 1), self.relay.at[k - 1], self.ss.at[1, k - 1], self.rx.at[k - 1], self.via, self.me.t
            ).start()

    def on(self, k):
        return send(
            self.relay.at[k - 1], self.at(k, 1), self.rs.at[k - 1], self.rr.at[1, k - 1], self.goal, self.me.t
        )

    def take(self, k):
        @pl.when(self.at_relay)
        def _():
            send(
                self.relay.at[k - 1], self.relay.at[k - 1], self.rs.at[k - 1], self.rx.at[k - 1], self.via, self.me.t
            ).wait_recv()
            self.on(k).start()

        for half in (0, 1):
            self.copy(k, half).wait_recv()
        if k < 3:
            self.push(k + 1)

    def finish(self):
        for k in (1, 2, 3):
            for half in (0, 1):
                self.copy(k, half).wait_send()

        @pl.when(self.at_relay)
        def _():
            for k in (1, 2, 3):
                self.on(k).wait_send()


def fused_kernel(
    n_seq, n_ten, delays, text_len, w_in, t_in, s_in, emb, gain, cot, out, de, sgo,
    pay, tmp,
    g, f, cots, rimbuf, blk, longer, nst, normed, states32, states,
    tkv, kx, qx, k_relay, q_relay, wbuf, wtbuf, mixbuf, totbuf, st, cstat,
    att, dq, dk, dv, tkg, tvg,
    opt, opx, opr, ipt, ipx, ipr, ops, ips, nst_out, nsx, nss, nsr,
    sga, sgza, sgb, sgzb, sgh, sghr, sgs, sgx, fg, rim,
    lsem, one_s, one_r, h_s, h_r, z_s, z_r, f_s, f_r, x_s, x_r,
    k_s, k_r, k_rs, k_rx, q_s, q_r, q_rs, q_rx, t_s, t_r, ox_s, ox_r, ix_s, ix_r, o_s, o_r, i_s, i_r, n_s, n_r,
    za_s, za_r, zb_s, zb_r, hh_s, hh_r,
):
    me = Place(n_seq, n_ten)
    H, Z, T = me.H, me.Z, n_ten
    s, t, c, h, z, p = me.s, me.t, me.c, me.h, me.z, me.p
    sib = me.sibling()
    half = Z // 2
    width = emb.shape[2]
    Q = emb.shape[1]
    B = 2 * Q
    R = sga.shape[3]
    text = states.shape[0]
    full = width * T
    scale = HD ** (-0.5)
    zero = jnp.zeros((), BF)
    right, left = me.seq(h, me.other_z(1), c), me.seq(h, me.other_z(-1), c)
    partners = [(sib, t), (me.next(1), t), (me.next(-1), t)]
    partners += [(me.seq(me.other_h(d), z, c), t) for d in range(1, H)]
    partners += [(me.seq(h, me.other_z(d), c), t) for d in range(1, Z)]
    partners += [(s, me.other_t(d)) for d in range(1, T)]
    partners += [(me.chip(k), t) for k in (1, -1, 2, -2, 3, -3)]
    greet(partners)
    outgoing = []

    def go(copy):
        copy.start()
        outgoing.append(copy)

    def half_rows(core):
        return pl.ds(pl.multiple_of(core * Q, Q), Q)

    per = text // n_seq
    given = t_in[0].shape[0]
    tmp[...] = jnp.zeros_like(tmp)
    for i in range(2):
        tmp[i, 0:given, :] = t_in[i][...].astype(F32)
        for e in range(2):
            tmp[i, 12:16, e * 128 : (e + 1) * 128] = s_in[e * 8 + i * 4 : e * 8 + i * 4 + 4, :]
    for e in range(2):
        lanes = slice(e * 128, (e + 1) * 128)
        for i in range(4):
            pay[e, i * R : (i + 1) * R, :] = w_in[i][:, lanes]
        for i in range(2):
            pay[e, 4 * R + 16 * i : 4 * R + 16 * (i + 1), :] = tmp[i, :, lanes].astype(BF)
    go(send(pay.at[1 - c], g.at[p, c], one_s.at[0], one_r.at[0], sib, t))
    mine = pltpu.make_async_copy(pay.at[c], g.at[p, c], lsem.at[0])
    mine.start()
    longer[...] = jnp.zeros_like(longer)
    for d in range(4):
        book = jnp.zeros((Q, width), F32)
        for k in range(4):
            book = book + jnp.where(delays[k] == d, emb[k].astype(F32), 0.0)
        longer[d : d + Q, :] = longer[d : d + Q, :] + book
    go(send(longer.at[pl.ds(Q, 16)], rimbuf, one_s.at[1], one_r.at[1], me.next(1), t))
    mine.wait()
    send(pay.at[c], g.at[p, 1 - c], one_s.at[0], one_r.at[0], sib, t).wait_recv()
    for d in range(1, H):
        go(send(g.at[p], g.at[p], h_s.at[d], h_r.at[d], me.seq(me.other_h(d), z, c), t))

    def step(way, k, d):
        hh = me.other_h(d)
        zz = me.other_z(-(k - 1) if way == 0 else k - 1)
        go(send(g.at[hh * Z + zz], g.at[hh * Z + zz], z_s.at[way, k, d], z_r.at[way, k, d], right if way == 0 else left, t))

    def arrived(way, k, d):
        hh = me.other_h(d)
        zz = me.other_z(-k if way == 0 else k)
        send(g.at[hh * Z + zz], g.at[hh * Z + zz], z_s.at[way, k, d], z_r.at[way, k, d], right, t).wait_recv()

    def used(way, k, d):
        if k < half:
            return True
        if k > half:
            return False
        return (d < H // 2) if way == 0 else (d >= H // 2)

    for way in (0, 1):
        if used(way, 1, 0):
            step(way, 1, 0)
    send(longer.at[pl.ds(Q, 16)], rimbuf, one_s.at[1], one_r.at[1], me.next(1), t).wait_recv()
    blk[...] = longer[0:Q, :].astype(BF)
    blk[0:16, :] = (longer[0:16, :] + jnp.where(s > 0, rimbuf[...], 0.0)).astype(BF)
    for d in range(1, T):
        go(send(blk, f.at[c, t], f_s.at[d], f_r.at[d], s, me.other_t(d)))
    go(send(blk, f.at[c, t], x_s.at[0], x_r.at[0], sib, t))
    own = pltpu.make_async_copy(blk, f.at[c, t], lsem.at[1])
    own.start()
    for d in range(1, H):
        hh = me.other_h(H - d)
        send(g.at[hh * Z + z], g.at[hh * Z + z], h_s.at[d], h_r.at[d], sib, t).wait_recv()
        for way in (0, 1):
            if used(way, 1, H - d):
                step(way, 1, H - d)
    go(send(cot, cots.at[half_rows(c)], one_s.at[2], one_r.at[2], sib, t))
    mycot = pltpu.make_async_copy(cot, cots.at[half_rows(c)], lsem.at[2])
    mycot.start()
    order = [0] + [H - e for e in range(1, H)]
    ring_last = half

    def ring(k):
        for d in order:
            for way in (0, 1):
                if used(way, k, d):
                    arrived(way, k, d)
                    if used(way, k + 1, d):
                        step(way, k + 1, d)

    def pass_frames():
        for d in range(1, T):
            tt = me.other_t(-d)
            send(blk, f.at[c, tt], f_s.at[d], f_r.at[d], sib, t).wait_recv()
            go(send(f.at[c, tt], f.at[c, tt], x_s.at[d], x_r.at[d], sib, t))

    def norm(cc):
        def fold(v):
            return v[:, 0:128] + v[:, 128:256]

        acc = jnp.zeros((Q, 128), F32)
        acc = lax.fori_loop(0, T, lambda i, a: a + fold(f[cc, i].astype(F32)), acc)
        mean = jnp.sum(acc, 1, keepdims=True) / full

        def second(i, a):
            v = f[cc, i].astype(F32) - mean
            return a + fold(v * v)

        acc = lax.fori_loop(0, T, second, jnp.zeros((Q, 128), F32))
        inv = lax.rsqrt(jnp.sum(acc, 1, keepdims=True) / full + EPS)
        lane128 = lax.broadcasted_iota(jnp.int32, (Q, 128), 1)
        nst[cc] = jnp.where(lane128 == 0, mean, inv)

        def third(i, carry):
            w = pl.ds(pl.multiple_of(i * width, width), width)
            v = (f[cc, i].astype(F32) - mean) * inv
            normed[half_rows(cc), w] = (v * gain[0:1, w]).astype(BF)
            return carry

        lax.fori_loop(0, T, third, 0)

    for k in range(1, half):
        if k == max(half - 2, 1):
            pass_frames()
        ring(k)
    if half == 1:
        pass_frames()
    own.wait()
    norm(c)
    for d in range(T):
        tt = me.other_t(-d)
        send(blk, f.at[1 - c, tt], x_s.at[d], x_r.at[d], sib, t).wait_recv()
    norm(1 - c)
    ring(half)

    def weight(i):
        return g[:, :, i * R : (i + 1) * R, :].reshape(n_seq * R, 128)

    def project(src, i, dst, first, lanes):
        def go_rows(rb, carry):
            rows = pl.ds(pl.multiple_of(first + rb * Q, Q), Q)
            dst[rows, lanes] = nn(src[half_rows(rb), :], weight(i)).astype(BF)
            return carry

        lax.fori_loop(0, 2, go_rows, 0)

    lo, hi = slice(0, 128), slice(128, 256)
    keys = Chain(
        me, 1, lambda k, e: kx.at[pl.ds((3 - k) * B + e * Q, Q)], k_relay, k_s, k_r, k_rs, k_rx
    )
    queries = Chain(me, -1, lambda k, e: qx.at[pl.ds(k * B + e * Q, Q)], q_relay, q_s, q_r, q_rs, q_rx)
    kv = kx.at[pl.ds(3 * B, B)]
    qd = qx.at[pl.ds(0, B)]
    project(normed, 1, kx, 3 * B, lo)
    project(normed, 2, kx, 3 * B, hi)
    keys.push(1)
    project(normed, 0, qx, 0, lo)
    mycot.wait()
    send(cot, cots.at[half_rows(c)], one_s.at[2], one_r.at[2], sib, t).wait_recv()
    project(cots, 3, qx, 0, hi)
    queries.push(1)

    lane = lax.broadcasted_iota(jnp.int32, (Q, 128), 1)
    row = lax.broadcasted_iota(jnp.int32, (Q, Q), 0)
    col = lax.broadcasted_iota(jnp.int32, (Q, Q), 1)
    heads = [lane < HD, lane >= HD]
    chunks = (WINDOW + Q - 2) // Q + 1
    lead = (chunks - 1) * Q

    def forward_chunk(qb, hd, q, j):
        base = pl.multiple_of((qb + j) * Q, Q)
        w = jnp.exp(nt(q, kx[pl.ds(base, Q), lo]))
        ok = p * B - 3 * B + (qb + j) * Q >= 0
        if lead - j * Q + Q - 1 >= WINDOW:
            ok = ok & (lead + row - j * Q - col < WINDOW)
        if j == chunks - 1:
            ok = ok & (col <= row)
        w = jnp.where(ok, w, 0.0)
        wbuf[qb, hd, j] = w
        return w[:, 0:128] + w[:, 128:256], nn(w.astype(BF), kx[pl.ds(base, Q), hi])

    def forward(k):
        for qb in range(2):
            q_both = qd[qb * Q : (qb + 1) * Q, lo]
            for hd in range(2):
                q = jnp.where(heads[hd], q_both, zero) * jnp.asarray(scale, BF)
                if k == 0:
                    total, mix = jnp.zeros((Q, 128), F32), jnp.zeros((Q, 128), F32)
                else:
                    total, mix = totbuf[qb, hd], mixbuf[qb, hd]
                if k == 4:
                    wt = jnp.where(live, jnp.exp(nt(q, tkv[:, lo])), 0.0)
                    wtbuf[qb, hd] = wt
                    total, mix = total + wt, mix + nn(wt.astype(BF), tkv[:, hi])
                for j in range(chunks):
                    if (qb + j) // 2 == 3 - k:
                        a, b = forward_chunk(qb, hd, q, j)
                        total, mix = total + a, mix + b
                totbuf[qb, hd], mixbuf[qb, hd] = total, mix

    states32[...] = g[:, :, 4 * R : 4 * R + 32, :].reshape(n_seq, 32, 128).astype(F32)
    lanes_of = 8 // (per // 2)
    for e in range(8):
        at = 12 + e if e < 4 else 24 + e
        first = pl.multiple_of((c * (per // 2) + e // lanes_of) * n_seq, n_seq)
        x = (e % lanes_of) * 128
        states[pl.ds(first, n_seq), x : x + 128] = states32[:, at, :].astype(BF)
    my_states = states.at[pl.ds(pl.multiple_of(c * (text // 2), text // 2), text // 2)]
    go(send(my_states, my_states, one_s.at[5], one_r.at[5], sib, t))
    forward(0)
    send(my_states, my_states, one_s.at[5], one_r.at[5], sib, t).wait_recv()
    for i in range(2):
        w = g[:, :, 4 * R + 16 * i : 4 * R + 16 * (i + 1), :].reshape(n_seq * 16, 128)
        tkv[:, i * 128 : (i + 1) * 128] = nn(states[...], w).astype(BF)
    token = lax.broadcasted_iota(jnp.int32, (1, text), 1)
    live = lax.rem(token, n_seq) * per + lax.div(token, n_seq) < text_len[0]

    forward(4)
    for k in (1, 2, 3):
        keys.take(k)
        queries.take(k)
        forward(k)
    for qb in range(2):
        rows = slice(qb * Q, (qb + 1) * Q)
        d_both = qd[rows, hi].astype(F32)
        parts, stats = [], []
        for hd in range(2):
            total = jnp.sum(totbuf[qb, hd], 1, keepdims=True)
            a_head = (mixbuf[qb, hd] / total).astype(BF)
            parts.append(a_head)
            inner = jnp.sum(jnp.where(heads[hd], d_both * a_head.astype(F32), 0.0), 1, keepdims=True)
            stats.append((1.0 / total, inner))
        att[rows, :] = jnp.where(heads[0], parts[0], parts[1])
        (r0, i0), (r1, i1) = stats
        packed = jnp.where(lane == 0, r0, jnp.where(lane == 1, r1, jnp.where(lane == 2, i0, i1)))
        cstat[rows, :] = packed
        st[0, :, rows] = packed.T[0:8, :]
    for k in (1, 2, 3):
        go(send(st.at[0], st.at[k], t_s.at[k], t_r.at[k], me.chip(-k), t))

    def w_block(i, tt):
        n = width // (2 * R)
        return g[pl.ds(tt * n, n), :, i * R : (i + 1) * R, :].reshape(width, 128)

    for d in range(T):
        tt = me.other_t(d)
        opt[d] = nt(att[half_rows(1 - c), :], w_block(3, tt)).astype(BF)
        go(send(opt.at[d], opx.at[d], ox_s.at[d], ox_r.at[d], sib, t))
    for e in range(full // B):
        piece = tn(att[...], cots[:, e * B : (e + 1) * B])
        n = B // R
        for a in range(B // 128):
            rows = piece[:, a * 128 : (a + 1) * 128].T.astype(BF).reshape(128 // R, R, 128)
            for b in range(128 // R):
                who = e * n + a * (128 // R) + b
                hh, zz, cc = who // (2 * Z), (who // 2) % Z, who % 2
                sga[zz, hh, cc] = rows[b]
    for d in range(1, Z):
        zz = me.other_z(d)
        go(send(sga.at[zz], sgza.at[d], za_s.at[d], za_r.at[d], me.seq(h, zz, c), t))

    tkg[...] = jnp.zeros_like(tkg)
    tvg[...] = jnp.zeros_like(tvg)

    def query_grads(qb, carry):
        rows = half_rows(qb)
        q_both = qd[rows, lo]
        d_both = qd[rows, hi]
        parts = []
        for hd in range(2):
            q = jnp.where(heads[hd], q_both, zero)
            d = jnp.where(heads[hd], d_both, zero)
            r = cstat[rows, hd : hd + 1]
            inner = cstat[rows, 2 + hd : 3 + hd]
            sh = wtbuf[qb, hd] * r
            ds = (sh * (nt(d, tkv[:, hi]) - inner)).astype(BF)
            grad = nn(ds, tkv[:, lo])
            tkg[...] += tn(ds, q) * scale
            tvg[...] += tn(sh.astype(BF), d)
            for j in range(chunks):
                base = pl.multiple_of((qb + j) * Q, Q)
                around = kx[pl.ds(base, Q), :]
                ds = (wbuf[qb, hd, j] * r * (nt(d, around[:, hi]) - inner)).astype(BF)
                grad = grad + nn(ds, around[:, lo])
            parts.append(grad)
        dq[rows, :] = (jnp.where(heads[0], parts[0], parts[1]) * scale).astype(BF)
        return carry

    lax.fori_loop(0, 2, query_grads, 0)
    for i, grad in enumerate((tkg, tvg)):
        piece = tn(states[...], grad[...].astype(BF)).astype(BF).reshape(H, Z, 2, 16, 128)
        for zz in range(Z):
            sgb[zz, :, :, 16 * i : 16 * (i + 1), :] = piece[:, zz]
    for d in range(1, Z):
        zz = me.other_z(d)
        go(send(sgb.at[zz], sgzb.at[d], zb_s.at[d], zb_r.at[d], me.seq(h, zz, c), t))
    for d in [*range(1, T), 0]:
        tt = me.other_t(d)
        send(opt.at[d], opx.at[d], ox_s.at[d], ox_r.at[d], sib, t).wait_recv()
        ops[d] = (nt(att[half_rows(c), :], w_block(3, tt)) + opx[d].astype(F32)).astype(BF)
        if d:
            go(send(ops.at[d], opr.at[d], o_s.at[d], o_r.at[d], s, tt))
    for k in (1, 2, 3):
        send(st.at[0], st.at[k], t_s.at[k], t_r.at[k], me.chip(-k), t).wait_recv()

    def key_grads(kb, carry):
        rows = half_rows(kb)
        k_both = kv[rows, lo]
        v_both = kv[rows, hi]
        kparts, vparts = [], []
        for hd in range(2):
            kh = jnp.where(heads[hd], k_both, zero) * jnp.asarray(scale, BF)
            vh = jnp.where(heads[hd], v_both, zero)
            gk = jnp.zeros((Q, 128), F32)
            gv = jnp.zeros((Q, 128), F32)
            for i in range(chunks):
                base = pl.multiple_of((kb + i) * Q, Q)
                qs = qx[pl.ds(base, Q), :]
                at = lax.div(kb + i, 2)
                part = pl.ds(pl.multiple_of(lax.rem(kb + i, 2) * Q, Q), Q)
                r = st[at, hd : hd + 1, part]
                inner = st[at, 2 + hd : 3 + hd, part]
                ok = p * B + (kb + i) * Q < n_seq * Q
                if i == 0:
                    ok = ok & (col >= row)
                if i * Q + Q - 1 >= WINDOW:
                    ok = ok & (i * Q + col - row < WINDOW)
                sh = jnp.where(ok, jnp.exp(nt(kh, qs[:, lo])) * r, 0.0)
                ds = (sh * (nt(vh, qs[:, hi]) - inner)).astype(BF)
                gv = gv + nn(sh.astype(BF), qs[:, hi])
                gk = gk + nn(ds, qs[:, lo])
            kparts.append(gk)
            vparts.append(gv)
        dk[rows, :] = (jnp.where(heads[0], kparts[0], kparts[1]) * scale).astype(BF)
        dv[rows, :] = jnp.where(heads[0], vparts[0], vparts[1]).astype(BF)
        return carry

    key_grads(1 - c, 0)

    def input_block(cc, tt):
        rows = half_rows(cc)
        grad = nt(dq[rows, :], w_block(0, tt)) + nt(dk[rows, :], w_block(1, tt)) + nt(dv[rows, :], w_block(2, tt))
        lanes = pl.ds(pl.multiple_of(tt * width, width), width)
        scaled = grad * gain[0:1, lanes]
        unit = (f[cc, tt].astype(F32) - nst[cc, :, 0:1]) * nst[cc, :, 1:2]
        both = scaled * unit
        return grad, scaled[:, 0:128] + scaled[:, 128:256], both[:, 0:128] + both[:, 128:256]

    def pack_sums(plain, unit):
        plain = jnp.sum(plain, 1, keepdims=True)
        unit = jnp.sum(unit, 1, keepdims=True)
        return jnp.where(lane == 0, plain, unit).T[0:8, :]

    plain = jnp.zeros((Q, 128), F32)
    unit = jnp.zeros((Q, 128), F32)
    for d in [*range(1, T), 0]:
        tt = me.other_t(d)
        grad, a, b = input_block(1 - c, tt)
        plain, unit = plain + a, unit + b
        ipt[d] = grad.astype(BF)
        go(send(ipt.at[d], ipx.at[d], ix_s.at[d], ix_r.at[d], sib, t))
    nst_out[...] = pack_sums(plain, unit)
    go(send(nst_out, nsx, n_s.at[0], n_r.at[0], sib, t))
    key_grads(c, 0)
    plain = jnp.zeros((Q, 128), F32)
    unit = jnp.zeros((Q, 128), F32)
    for d in [*range(1, T), 0]:
        tt = me.other_t(d)
        grad, a, b = input_block(c, tt)
        plain, unit = plain + a, unit + b
        send(ipt.at[d], ipx.at[d], ix_s.at[d], ix_r.at[d], sib, t).wait_recv()
        ips[d] = (grad + ipx[d].astype(F32)).astype(BF)
        if d:
            go(send(ips.at[d], ipr.at[d], i_s.at[d], i_r.at[d], s, tt))
    send(nst_out, nsx, n_s.at[0], n_r.at[0], sib, t).wait_recv()
    nss[...] = pack_sums(plain, unit) + nsx[...]
    for d in range(1, T):
        go(send(nss, nsr.at[d], n_s.at[d], n_r.at[d], s, me.other_t(d)))

    total = ips[0].astype(F32)
    sums = nss[...]
    for d in range(1, T):
        send(nss, nsr.at[d], n_s.at[d], n_r.at[d], sib, t).wait_recv()
        sums = sums + nsr[d]
        send(ips.at[d], ipr.at[d], i_s.at[d], i_r.at[d], sib, t).wait_recv()
        total = total + ipr[d].astype(F32)
    tall = jnp.concatenate([sums] * 16, 0).T
    here = pl.ds(pl.multiple_of(t * width, width), width)
    inv = nst[c, :, 1:2]
    unit = (f[c, t].astype(F32) - nst[c, :, 0:1]) * inv
    grad = inv * (total * gain[0:1, here] - tall[:, 0:1] / full - unit * (tall[:, 1:2] / full))
    fg[...] = grad.astype(BF)
    go(send(fg.at[pl.ds(0, 16)], rim, one_s.at[3], one_r.at[3], me.next(-1), t))

    acc_a = sga[z].astype(F32)
    acc_b = sgb[z].astype(F32)
    for d in range(1, Z):
        send(sga.at[0], sgza.at[d], za_s.at[d], za_r.at[d], sib, t).wait_recv()
        send(sgb.at[0], sgzb.at[d], zb_s.at[d], zb_r.at[d], sib, t).wait_recv()
        acc_a = acc_a + sgza[d].astype(F32)
        acc_b = acc_b + sgzb[d].astype(F32)
    sgh[:, :, 0:R, :] = acc_a
    sgh[:, :, R : R + 32, :] = acc_b
    for d in range(1, H):
        hh = me.other_h(d)
        go(send(sgh.at[hh], sghr.at[d], hh_s.at[d], hh_r.at[d], me.seq(hh, z, c), t))
    acc = sgh[h]
    for d in range(1, H):
        send(sgh.at[0], sghr.at[d], hh_s.at[d], hh_r.at[d], sib, t).wait_recv()
        acc = acc + sghr[d]
    sgs[...] = acc
    go(send(sgs.at[1 - c], sgx, one_s.at[4], one_r.at[4], sib, t))
    longer[0:Q, :] = fg[...].astype(F32)
    total = ops[0].astype(F32)
    for d in range(1, T):
        send(ops.at[d], opr.at[d], o_s.at[d], o_r.at[d], sib, t).wait_recv()
        total = total + opr[d].astype(F32)
    out[...] = total.astype(BF)
    send(fg.at[pl.ds(0, 16)], rim, one_s.at[3], one_r.at[3], sib, t).wait_recv()
    send(sgs.at[0], sgx, one_s.at[4], one_r.at[4], sib, t).wait_recv()
    sgo[:, lo] = jnp.where(c == 0, sgs[c], sgx[...])
    sgo[:, hi] = jnp.where(c == 0, sgx[...], sgs[c])
    for copy in outgoing:
        copy.wait_send()
    for chain in (keys, queries):
        chain.finish()
    longer[Q : Q + 16, :] = jnp.where(s < n_seq - 1, rim[...].astype(F32), 0.0)
    later = [longer[d : d + Q, :] for d in range(4)]
    for k in range(4):
        book = later[0]
        for d in range(1, 4):
            book = jnp.where(delays[k] == d, later[d], book)
        de[k] = book.astype(BF)


def fused(n_seq, n_ten, delays, text_len, weights, text_weights, states, emb, gain, cot, text):
    H, Z = dims_of(n_seq)
    T = n_ten
    _, Q, W = emb.shape
    B = 2 * Q
    full = W * T
    R = weights[0].shape[0]
    pay_shape = (2, 4 * R + 32, 128)
    chunks = (WINDOW + Q - 2) // Q + 1
    dma = pltpu.SemaphoreType.DMA
    vm = pl.BlockSpec(memory_space=pltpu.VMEM)
    sm = pl.BlockSpec(memory_space=pltpu.SMEM)
    V = pltpu.VMEM
    block = V((T, Q, W), BF)
    rows = V((B, 128), BF)
    small = V((text, 128), F32)
    sums = V((8, Q), F32)

    def pair(*shape):
        return [dma(shape), dma(shape)]

    return pl.pallas_call(
        lambda a, b, *refs: fused_kernel(n_seq, n_ten, a, b, refs[0:4], refs[4:6], *refs[6:]),
        out_shape=(
            jax.ShapeDtypeStruct((Q, W), BF),
            jax.ShapeDtypeStruct((4, Q, W), BF),
            jax.ShapeDtypeStruct((R + 32, 256), F32),
        ),
        in_specs=[sm, sm] + [vm] * 9 + [pl.BlockSpec(memory_space=pl.ANY)],
        out_specs=(vm,) * 3,
        scratch_shapes=[
            V(pay_shape, BF), V((2, 16, 256), F32), V((H * Z,) + pay_shape, BF), V((2, T, Q, W), BF), V((B, full), BF), V((16, W), F32), V((Q, W), BF),
            V((Q + 16, W), F32), V((2, Q, 128), F32), V((B, full), BF), V((n_seq, 32, 128), F32),
            V((text, n_seq * 16), BF),
            V((text, 256), BF), V((4 * B, 256), BF), V((4 * B, 256), BF), V((3, Q, 256), BF), V((3, Q, 256), BF),
            V((2, 2, chunks, Q, Q), F32), V((2, 2, Q, text), F32), V((2, 2, Q, 128), F32), V((2, 2, Q, 128), F32),
            V((4, 8, B), F32), V((B, 128), F32),
            rows, rows, rows, rows, small, small,
            block, block, block, block, block, block, block, block, sums, sums, sums, V((T, 8, Q), F32),
            V((Z, H, 2, R, 128), BF), V((Z, H, 2, R, 128), BF), V((Z, H, 2, 32, 128), BF), V((Z, H, 2, 32, 128), BF),
            V((H, 2, R + 32, 128), F32), V((H, 2, R + 32, 128), F32), V((2, R + 32, 128), F32), V((R + 32, 128), F32),
            V((Q, W), BF), V((16, W), BF),
            dma((3,)), *pair(6), *pair(H), *pair(2, Z // 2 + 1, H), *pair(T), *pair(T),
            *pair(2, 3), *pair(3), *pair(2, 3), *pair(3), *pair(4), *pair(T), *pair(T), *pair(T), *pair(T), *pair(T),
            *pair(Z), *pair(Z), *pair(H),
        ],
        compiler_params=pltpu.CompilerParams(collective_id=0, has_side_effects=True, vmem_limit_bytes=56 << 20),
    )(delays, text_len, *weights, *text_weights, states, emb, gain, cot)


def shards(
    n_seq, n_ten, embedded, delays, norm_gain, w_query, w_key, w_value, w_out,
    text_states, w_text_key, w_text_value, text_len, cotangent,
):
    R = w_query.shape[0]
    tr = w_text_key.shape[0]
    per = text_states.shape[0]
    states = jnp.pad(text_states.reshape(per, n_seq, tr), ((0, 0), (0, 0), (0, 16 - tr))).reshape(16, 128)
    out, de, sgo = fused(
        n_seq, n_ten, delays, text_len, (w_query, w_key, w_value, w_out.T), (w_text_key, w_text_value),
        states.astype(F32), embedded.transpose(1, 0, 2), norm_gain.reshape(1, -1), cotangent, per * n_seq,
    )
    return (out, de.transpose(1, 0, 2), sgo[:R].T, sgo[R : R + tr], sgo[R + 16 : R + 16 + tr])


def solution(mesh):
    placed = (
        P("seq", None, "tensor"), P(), P(),
        P("seq", "tensor"), P("seq", "tensor"), P("seq", "tensor"), P("tensor", "seq"),
        P("seq", None), P("seq", "tensor"), P("seq", "tensor"), P(), P("seq", None),
    )
    return jax.shard_map(
        functools.partial(shards, mesh.shape["seq"], mesh.shape["tensor"]),
        mesh=mesh,
        in_specs=placed,
        out_specs=(
            P("seq", "tensor"), P("seq", None, "tensor"), P("tensor", "seq"),
            P("seq", "tensor"), P("seq", "tensor"),
        ),
        check_vma=False,
    )
```
